512 devices in a mesh: gx: 32 (over z, core), gy: 16 (over x, y).
Axes of the slice: x: 4, y: 4, z: 16, core: 2. Of those that a mesh axis runs over, the one named last changes fastest.
Arguments:
- adjoint: float32 [3, 8, 512, 2048], P(None, None, 'gx', 'gy'), may hold values from -12 to 12
- checkpoints: bfloat16 [1, 3, 8, 512, 2048], P(None, None, None, 'gx', 'gy'), may hold values from -3 to 3
- wall_faces: int32 [2, 64, 256], P(None, 'gx', 'gy'), may hold values 0 or 1
Outputs:
- velocity: float32 [3, 8, 512, 2048], P(None, None, 'gx', 'gy')
- pressure: float32 [8, 512, 2048], P(None, 'gx', 'gy')
The draws below stay inside these ranges and needn't reach their ends.
Inputs may be any that keep to these rules, and one draw needn't show every extreme that they name: `wall_faces`: 1 marks a no-slip face, 0 an open one.
All inputs are finite; a program needn't handle non-finite values. No bound on the sum of `wall_faces` on one device may be relied on, other than what follows from the above.
Results may differ from the reference program's by a relative error of at most 0.0003.
Values sent between devices are 32-bit elements; how exact they have to be, the bound alone decides.
No kernel may reach another device: no remote copies, remote signals or barrier semaphores. Data moves between devices by JAX's collectives and lax.ppermute only.
A program may use at most 64 MiB of HBM per device.

```python
import math
import jax
import jax.numpy as jnp
import numpy as np
from jax import lax

NODES = 8
EXD = 2
EYD = 16
ITERS = 4
STEPS = 1
EX = 64
EY = 256
NXN = 512
NYN = 2048


def draw_adjoint(key, part):
    key = jax.random.fold_in(key, 11)
    noise_key, level_key, blend_key, phase_key = jax.random.split(key, 4)
    extent = (3, NODES, NXN, NYN)
    sample = jnp.clip(jax.random.normal(noise_key, extent, jnp.float32), -4.0, 4.0)
    block_rows = NODES * EXD
    block_cols = NODES * EYD
    count_x = NXN // block_rows
    count_y = NYN // block_cols
    levels = jnp.exp(jax.random.uniform(level_key, (count_x, count_y), jnp.float32, -1.0, 1.0))
    blend = jax.random.uniform(blend_key, (count_x, count_y), jnp.float32, 0.15, 1.0)
    level_field = jnp.repeat(jnp.repeat(levels, block_rows, axis=0), block_cols, axis=1)
    blend_field = jnp.repeat(jnp.repeat(blend, block_rows, axis=0), block_cols, axis=1)
    phases = jax.random.uniform(phase_key, (3, 3), jnp.float32, -math.pi, math.pi)
    position_x = jnp.arange(NXN, dtype=jnp.float32) * (math.pi / block_rows)
    position_y = jnp.arange(NYN, dtype=jnp.float32) * (math.pi / block_cols)
    depth_pos = (jnp.arange(NODES, dtype=jnp.float32) * (2.0 / (NODES - 1)) - 1.0) * (math.pi / 2.0)
    wave_x = jnp.sin(position_x[None, :] + phases[:, 0:1])
    wave_y = jnp.cos(position_y[None, :] + phases[:, 1:2])
    wave_z = jnp.cos(depth_pos[None, :] + phases[:, 2:3])
    smooth = wave_z[:, :, None, None] * wave_x[:, None, :, None] * wave_y[:, None, None, :]
    mixed = blend_field * sample + 1.5 * (1.0 - blend_field) * smooth
    ramp_x = 1.0 + 2.0 * jnp.arange(NXN, dtype=jnp.float32) / (NXN - 1)
    ramp_y = 1.0 + 2.0 * jnp.arange(NYN, dtype=jnp.float32) / (NYN - 1)
    field = mixed * level_field * ramp_x[:, None] * ramp_y[None, :] / 3.0
    return jnp.clip(field, -12.0, 12.0)


def plant(values, key, least, largest):
    dims = values.shape
    index_at = [jax.random.randint(jax.random.fold_in(key, axis), (), 0, dims[axis]) for axis in range(len(dims))]
    values = values.at[tuple(index_at)].set(least)
    longest = dims.index(max(dims))
    index_at[longest] = (index_at[longest] + 1) % dims[longest]
    return values.at[tuple(index_at)].set(largest)


def block_levels(own_key, shape, cuts, least, high):
    level = 1.0
    for dim, parts in cuts:
        draws = jax.random.uniform(jax.random.fold_in(jax.random.fold_in(own_key, 6), dim), (parts,), jnp.float32, least / len(cuts), high / len(cuts))
        level = level * jnp.repeat(jnp.exp(draws), shape[dim] // parts).reshape((-1,) + (1,) * (len(shape) - 1 - dim))
    return level


def noise(own_key, dims, width, limit, cuts=(), held_as=jnp.bfloat16):
    loudness = block_levels(own_key, dims, cuts, -0.22, 0.18) if cuts else 1.0
    values = jax.random.normal(own_key, dims, jnp.float32) * width * loudness
    return jnp.minimum(jnp.maximum(values, -limit), limit).astype(held_as)


def setup_inputs(seed: int = 0) -> dict:
    keys = jax.random.split(jax.random.key(seed), 4)
    return {
        "adjoint": draw_adjoint(jax.random.fold_in(keys[3], 71), 0),
        "checkpoints": noise(keys[1], (STEPS, 3, NODES, NXN, NYN), 0.5, 3.0, ((3, 32), (4, 16))),
        "wall_faces": plant((jax.random.randint(keys[2], (2, EX, EY), 0, 2) < 1).astype(jnp.int32), jax.random.fold_in(keys[2], 1), 0, 1),
    }


node_points = np.array([-1.0, -0.8717401485096066, -0.5917001814331423, -0.2092992179024789, 0.2092992179024789, 0.5917001814331423, 0.8717401485096066, 1.0])
node_weights = np.array([0.03571428571428571, 0.2107042271435061, 0.3411226924835044, 0.4124587946587038, 0.4124587946587038, 0.3411226924835044, 0.2107042271435061, 0.03571428571428571])
time_step = 0.05
viscosity = 0.02
highest = lax.Precision.HIGHEST


def derivative_table(points):
    identity = np.eye(points.shape[0])
    spacing = points[:, None] - points[None, :] + identity
    barycentric = 1.0 / np.prod(spacing, axis=1)
    matrix = (barycentric[None, :] / barycentric[:, None]) / spacing
    matrix = matrix * (1.0 - identity)
    return matrix - identity * np.sum(matrix, axis=1)[:, None]


def along_rows(nodal, matrix):
    components, layers, size_x, size_y = nodal.shape
    blocks = nodal.reshape(components, layers, size_x // 8, 8, size_y)
    result = jnp.einsum('ak,czeky->czeay', jnp.asarray(matrix, jnp.float32), blocks, precision=highest)
    return result.reshape(nodal.shape)


def along_columns(nodal, matrix):
    components, layers, size_x, size_y = nodal.shape
    blocks = nodal.reshape(components, layers, size_x, size_y // 8, 8)
    result = jnp.einsum('bk,czxfk->czxfb', jnp.asarray(matrix, jnp.float32), blocks, precision=highest)
    return result.reshape(nodal.shape)


def along_depth(nodal, matrix):
    return jnp.einsum('ck,akxy->acxy', jnp.asarray(matrix, jnp.float32), nodal, precision=highest)


def mass_weights(size_x, size_y):
    weights = jnp.asarray(node_weights, jnp.float32)
    across_x = jnp.tile(weights, size_x // 8)
    across_y = jnp.tile(weights, size_y // 8)
    return weights[:, None, None] * across_x[None, :, None] * across_y[None, None, :]


def edge_flags(length):
    place = jnp.arange(length) % 8
    return ((place == 0) | (place == 7)).astype(jnp.float32)


def share_counts(size_x, size_y):
    return (1.0 + edge_flags(size_x))[:, None] * (1.0 + edge_flags(size_y))[None, :]


def boundary_masks(wall_faces, size_x, size_y):
    walls = jnp.repeat(jnp.repeat(wall_faces.astype(jnp.float32), 8, axis=1), 8, axis=2)
    interior = (1.0 - edge_flags(size_x))[:, None] * (1.0 - edge_flags(size_y))[None, :]
    middle = jnp.ones((6, size_x, size_y), jnp.float32)
    velocity_mask = jnp.concatenate([(interior * (1.0 - walls[0]))[None], middle, (interior * (1.0 - walls[1]))[None]], axis=0)
    pressure_mask = jnp.concatenate([(interior * walls[0])[None], middle, (interior * walls[1])[None]], axis=0)
    return velocity_mask, pressure_mask


def assemble(nodal):
    place_x = jnp.arange(nodal.shape[2]) % 8
    upper_x = (place_x == 7).astype(jnp.float32)[:, None]
    lower_x = (place_x == 0).astype(jnp.float32)[:, None]
    summed = nodal + upper_x * jnp.roll(nodal, -1, axis=2) + lower_x * jnp.roll(nodal, 1, axis=2)
    place_y = jnp.arange(nodal.shape[3]) % 8
    upper_y = (place_y == 7).astype(jnp.float32)
    lower_y = (place_y == 0).astype(jnp.float32)
    return summed + upper_y * jnp.roll(summed, -1, axis=3) + lower_y * jnp.roll(summed, 1, axis=3)


def stiffness(nodal, wmass):
    derivative = derivative_table(node_points)
    transposed = derivative.T
    return (along_rows(wmass * along_rows(nodal, derivative), transposed)
            + along_columns(wmass * along_columns(nodal, derivative), transposed)
            + along_depth(wmass * along_depth(nodal, derivative), transposed))


def inner(former, latter, inverse_share):
    return jnp.sum(former * latter * inverse_share)


def adjoint_step(velocity, forward, velocity_mask, pressure_mask, wmass, amass, inverse_share):
    derivative = derivative_table(node_points)
    flow = forward.astype(jnp.float32)
    flow_dx = along_rows(flow, derivative)
    flow_dy = along_columns(flow, derivative)
    flow_dz = along_depth(flow, derivative)
    velocity_dx = along_rows(velocity, derivative)
    velocity_dy = along_columns(velocity, derivative)
    velocity_dz = along_depth(velocity, derivative)
    transport = flow[0:1] * velocity_dx + flow[1:2] * velocity_dy + flow[2:3] * velocity_dz
    stretch = jnp.concatenate([jnp.sum(velocity * flow_dx, axis=0, keepdims=True),
                               jnp.sum(velocity * flow_dy, axis=0, keepdims=True),
                               jnp.sum(velocity * flow_dz, axis=0, keepdims=True)], axis=0)
    advect = transport - stretch
    forcing = wmass * (velocity + time_step * advect) - time_step * viscosity * stiffness(velocity, wmass)
    moved = velocity_mask * assemble(forcing) / amass
    diverge = along_rows(moved[0:1], derivative) + along_columns(moved[1:2], derivative) + along_depth(moved[2:3], derivative)
    source = -pressure_mask * assemble(wmass * diverge)
    pressure = jnp.zeros_like(source)
    resid = source
    direction = source
    norm_now = inner(resid, resid, inverse_share)
    for round_index in range(ITERS):
        image = pressure_mask * assemble(stiffness(direction, wmass))
        step_length = norm_now / inner(direction, image, inverse_share)
        pressure = pressure + step_length * direction
        resid = resid - step_length * image
        if round_index + 1 < ITERS:
            norm_next = inner(resid, resid, inverse_share)
            direction = resid + (norm_next / norm_now) * direction
            norm_now = norm_next
    slopes = jnp.concatenate([along_rows(pressure, derivative), along_columns(pressure, derivative), along_depth(pressure, derivative)], axis=0)
    correction = assemble(wmass * slopes) / amass
    return velocity_mask * (moved - correction), pressure


def reference(adjoint, checkpoints, wall_faces):
    size_x = adjoint.shape[2]
    size_y = adjoint.shape[3]
    wmass = mass_weights(size_x, size_y)
    counts = share_counts(size_x, size_y)
    inverse_share = 1.0 / counts
    amass = wmass * counts
    velocity_mask, pressure_mask = boundary_masks(wall_faces, size_x, size_y)
    velocity = adjoint
    pressure = jnp.zeros((1,) + adjoint.shape[1:], jnp.float32)
    for section_index in range(STEPS):
        velocity, pressure = adjoint_step(velocity, checkpoints[section_index], velocity_mask, pressure_mask, wmass, amass, inverse_share)
    return velocity, pressure[0]
```

```python
import jax
import jax.numpy as jnp
import numpy as np
from jax import lax
from jax.experimental import pallas as pl
from jax.experimental.pallas import tpu as pltpu
from jax.sharding import PartitionSpec as P

f32 = jnp.float32
bf16 = jnp.bfloat16

node_points = np.array(
    [
        -1.0,
        -0.8717401485096066,
        -0.5917001814331423,
        -0.2092992179024789,
        0.2092992179024789,
        0.5917001814331423,
        0.8717401485096066,
        1.0,
    ]
)
node_weights = np.array(
    [
        0.03571428571428571,
        0.2107042271435061,
        0.3411226924835044,
        0.4124587946587038,
        0.4124587946587038,
        0.3411226924835044,
        0.2107042271435061,
        0.03571428571428571,
    ]
)
time_step = 0.05
viscosity = 0.02
span = 8.0
ROUNDS = 4


def derivative_table(points):
    identity = np.eye(points.shape[0])
    spacing = points[:, None] - points[None, :] + identity
    barycentric = 1.0 / np.prod(spacing, axis=1)
    matrix = barycentric[None, :] / barycentric[:, None] / spacing
    matrix = matrix * (1.0 - identity)
    return matrix - identity * np.sum(matrix, axis=1)[:, None]


deriv = derivative_table(node_points)
stiff = deriv.T @ np.diag(node_weights) @ deriv
copies = np.array([2.0, 1, 1, 1, 1, 1, 1, 2.0])
inverse_mass = 1.0 / (copies * node_weights)


def lane_matrix(matrix):
    full = np.kron(np.eye(16), matrix).T.astype(np.float32)
    high = full.astype(jnp.bfloat16)
    low = (full - high.astype(np.float32)).astype(jnp.bfloat16)
    pair = np.concatenate([high, low], axis=1)
    return np.concatenate([pair, pair], axis=0)


lane_deriv = lane_matrix(deriv)
lane_stiff = lane_matrix(stiff)


def iota(lanes, dim):
    return lax.broadcasted_iota(jnp.int32, (8, lanes), dim)


def pick(place, values):
    out = jnp.full(place.shape, float(values[0]), f32)
    for k in range(1, 8):
        out = jnp.where(place == k, float(values[k]), out)
    return out


def node_x(lanes, values):
    return pick(iota(lanes, 0), values)


def node_y(lanes, values):
    return pick(iota(lanes, 1) & 7, values)


def rim_mask(lanes):
    a = iota(lanes, 0)
    b = iota(lanes, 1) & 7
    return (a == 0) | (a == 7) | (b == 0) | (b == 7)


def row_coefs(lanes, matrix):
    return [node_x(lanes, [matrix[a, (a - r) % 8] for a in range(8)]) for r in range(8)]


def row_turns(value):
    return [value] + [pltpu.roll(value, r, axis=1) for r in range(1, 8)]


def weigh(turns, coefs):
    out = turns[0] * coefs[0]
    for r in range(1, 8):
        out = out + turns[r] * coefs[r]
    return out


def depth(planes, matrix):
    out = []
    for c in range(8):
        total = planes[0] * float(matrix[c, 0])
        for k in range(1, 8):
            total = total + planes[k] * float(matrix[c, k])
        out.append(total)
    return out


def lanes_times(value, table):
    n, _, lanes = value.shape
    blocks = [value[:, :, k * 128 : (k + 1) * 128].reshape(n * 8, 128) for k in range(lanes // 128)]
    rows = blocks[0] if len(blocks) == 1 else jnp.concatenate(blocks, axis=0)
    high = rows.astype(bf16)
    low = (rows - high.astype(f32)).astype(bf16)
    both = jnp.concatenate([high, low], axis=1)
    got = jnp.dot(both, table, preferred_element_type=f32)
    got = got[:, :128] + got[:, 128:]
    parts = [got[k * n * 8 : (k + 1) * n * 8].reshape(n, 8, 128) for k in range(lanes // 128)]
    return parts[0] if len(parts) == 1 else jnp.concatenate(parts, axis=2)


def sum_lanes(value, first, last):
    lanes = value.shape[2]
    return (
        value
        + last * pltpu.roll(value, lanes - 1, axis=2)
        + first * pltpu.roll(value, 1, axis=2)
    )


def sum_rows(before, here, after, first, last):
    return here + last * pltpu.roll(after, 7, axis=1) + first * pltpu.roll(before, 1, axis=1)


def own_lanes(value):
    n = value.shape[0]
    lane = lax.broadcasted_iota(jnp.int32, (n, 8, 128), 2)
    mixed = jnp.where(lane >= 64, value[:, :, :128], value[:, :, 128:])
    return pltpu.roll(mixed, 64, axis=2)


def expand_walls(faces_ref):
    spread = (
        lax.broadcasted_iota(jnp.int32, (16, 128), 1) // 8
        == lax.broadcasted_iota(jnp.int32, (16, 128), 0)
    ).astype(f32)
    out = []
    for face in range(2):
        rows = faces_ref[face].astype(f32)
        wide = jnp.dot(rows, spread, preferred_element_type=f32)
        out.append(wide)
    return out


def rhs_kernel(adj_ref, flow_ref, faces_ref, dy_ref, ky_ref, r_ref, up_ref, down_ref, wall_ref):
    lanes = 128
    for face, wide in enumerate(expand_walls(faces_ref)):
        for e in range(2):
            wall_ref[face, e] = jnp.broadcast_to(wide[e : e + 1], (8, lanes))
    dcoef = row_coefs(lanes, deriv)
    kcoef = row_coefs(lanes, stiff)
    wx = node_x(lanes, node_weights)
    wy = node_y(lanes, node_weights)
    wxy = wx * wy
    rim = rim_mask(lanes)
    half = iota(lanes, 1) < 64

    def body(e, carry):
        v = [adj_ref[c, :, e] for c in range(3)]
        u = [flow_ref[c, :, e].astype(f32) for c in range(3)]
        vall = jnp.concatenate(v, axis=0)
        uall = jnp.concatenate(u, axis=0)
        vdy = lanes_times(vall, dy_ref[...])
        vky = lanes_times(vall, ky_ref[...])
        udy = lanes_times(uall, dy_ref[...])
        stretch_x = jnp.zeros((8, 8, lanes), f32)
        stretch_y = jnp.zeros((8, 8, lanes), f32)
        stretch_z = jnp.zeros((8, 8, lanes), f32)
        for j in range(3):
            stretch_x = stretch_x + v[j] * weigh(row_turns(u[j]), dcoef)
            stretch_y = stretch_y + v[j] * udy[8 * j : 8 * j + 8]
            stretch_z = stretch_z + v[j] * jnp.stack(depth([u[j][z] for z in range(8)], deriv))
        stretch = [stretch_x, stretch_y, stretch_z]
        for i in range(3):
            turns = row_turns(v[i])
            planes = [v[i][z] for z in range(8)]
            zd = depth(planes, deriv)
            zk = depth(planes, stiff)
            xd = weigh(turns, dcoef)
            xk = weigh(turns, kcoef)
            made = []
            for z in range(8):
                wz = float(node_weights[z])
                adv = (
                    u[0][z] * xd[z]
                    + u[1][z] * vdy[8 * i + z]
                    + u[2][z] * zd[z]
                    - stretch[i][z]
                )
                bend = wy * (wz * xk[z]) + wx * (wz * vky[8 * i + z]) + wxy * zk[z]
                out = (wxy * wz) * (v[i][z] + time_step * adv) - (time_step * viscosity) * bend
                if i == 0 and z in (0, 7):
                    out = jnp.where(rim, wall_ref[z // 7, e], out)
                r_ref[i, z, e] = out
                made.append(out)
            for z in range(4):
                up_ref[i, z, e] = jnp.where(half, pltpu.roll(made[z], 64, axis=1), made[z + 4])
                down_ref[i, z, e] = jnp.where(half, made[z], pltpu.roll(made[z + 4], 64, axis=1))
        return carry

    lax.fori_loop(0, 2, body, 0)


def join_kernel(r_ref, left_ref, right_ref, e_ref):
    half = iota(128, 1) < 64

    def body(e, carry):
        for c in range(3):
            for z in range(8):
                turned = pltpu.roll(r_ref[c, z, e], 64, axis=1)
                left = left_ref[c, z % 4, e]
                right = right_ref[c, z % 4, e]
                if z >= 4:
                    left = pltpu.roll(left, 64, axis=1)
                else:
                    right = pltpu.roll(right, 64, axis=1)
                e_ref[c, z, e, :, 0:128] = jnp.where(half, left, turned)
                e_ref[c, z, e, :, 128:256] = jnp.where(half, turned, right)
        return carry

    lax.fori_loop(0, 2, body, 0)


def source_kernel(left_ref, mid_ref, right_ref, dy_ref, b_ref, w_ref, all_ref, s_ref):
    lanes = 256
    for part, ref in enumerate((left_ref, mid_ref, right_ref)):
        for k in range(2):
            all_ref[:, :, 2 * part + k] = ref[:, :, k]
    dcoef = row_coefs(lanes, deriv)
    wxy = node_x(lanes, node_weights) * node_y(lanes, node_weights)
    inv = node_x(lanes, inverse_mass) * node_y(lanes, inverse_mass)
    first_x = (iota(lanes, 0) == 0).astype(f32)
    last_x = (iota(lanes, 0) == 7).astype(f32)
    first_y = ((iota(lanes, 1) & 7) == 0).astype(f32)
    last_y = ((iota(lanes, 1) & 7) == 7).astype(f32)
    inside = 1.0 - rim_mask(lanes).astype(f32)

    def wall(z, e):
        return jnp.broadcast_to(all_ref[0, z, e, 0:1, :], (8, lanes))

    def body(e, carry):
        w = []
        for c in range(3):
            rows = sum_rows(all_ref[c, :, e], all_ref[c, :, e + 1], all_ref[c, :, e + 2], first_x, last_x)
            total = sum_lanes(rows, first_y, last_y)
            planes = []
            for z in range(8):
                got = total[z] * (inv / float(node_weights[z]))
                if z in (0, 7):
                    got = got * (inside * (1.0 - wall(z, e + 1)))
                planes.append(got)
            w.append(jnp.stack(planes))
        div = (
            weigh(row_turns(w[0]), dcoef)
            + lanes_times(w[1], dy_ref[...])
            + jnp.stack(depth([w[2][z] for z in range(8)], deriv))
        )
        for z in range(8):
            s_ref[z, e] = (wxy * float(node_weights[z])) * div[z]

        @pl.when((e == 1) | (e == 2))
        def _():
            for c in range(3):
                w_ref[c, :, e - 1] = own_lanes(w[c])

        return carry

    lax.fori_loop(0, 4, body, 0)

    def body2(e, carry):
        rows = sum_rows(s_ref[:, e], s_ref[:, e + 1], s_ref[:, e + 2], first_x, last_x)
        total = sum_lanes(rows, first_y, last_y)
        for z in range(8):
            if z in (0, 7):
                face = wall(z, e + 2)
                b_ref[z, e] = jnp.where(inside > 0.5, -total[z] * face, face)
            else:
                b_ref[z, e] = -total[z]
        return carry

    lax.fori_loop(0, 2, body2, 0)


def krylov_kernel(mine_ref, other_ref, ky_ref, v_out, m_out, v_ref, k_ref, p_ref, acc_ref):
    lanes = 256
    core = lax.axis_index("gx") % 2
    rim = rim_mask(lanes)
    for k in range(3):
        for ref, shift in ((mine_ref, core), (other_ref, 1 - core)):
            for e in range(2):
                at = 4 * k + 2 * shift + e
                for z in range(8):
                    got = ref[k, z, e]
                    if z in (0, 7):
                        face = jnp.broadcast_to(got[0:1, :], (8, lanes))
                        p_ref[z // 7, at] = jnp.where(rim, 0.0, face)
                        got = jnp.where(rim, 0.0, got)
                    v_ref[0, z, at] = got
    kcoef = row_coefs(lanes, stiff)
    wx = node_x(lanes, node_weights)
    wy = node_y(lanes, node_weights)
    wxy = wx * wy
    first_x = (iota(lanes, 0) == 0).astype(f32)
    last_x = (iota(lanes, 0) == 7).astype(f32)
    first_y = ((iota(lanes, 1) & 7) == 0).astype(f32)
    last_y = ((iota(lanes, 1) & 7) == 7).astype(f32)
    lane = iota(lanes, 1)
    own = ((lane >= 64) & (lane < 192)).astype(f32)
    share = own * node_x(lanes, 1.0 / copies) * node_y(lanes, 1.0 / copies)
    acc_ref[...] = jnp.zeros(acc_ref.shape, f32)

    def fold(value):
        total = value[0]
        for z in range(1, 8):
            total = total + value[z]
        return total[:, :128] + total[:, 128:]

    def apply(j, e):
        v = v_ref[j, :, e]
        xk = weigh(row_turns(v), kcoef)
        yk = lanes_times(v, ky_ref[...])
        zk = depth([v[z] for z in range(8)], stiff)
        for z in range(8):
            wz = float(node_weights[z])
            k_ref[z, e] = wy * (wz * xk[z]) + wx * (wz * yk[z]) + wxy * zk[z]

    slot = 0
    for j in range(ROUNDS):
        low, high = (j, 12 - j) if j < 3 else (4, 8)
        lax.fori_loop(low, high, lambda e, c, j=j: (apply(j, e), c)[1], 0)

        def gram(e, carry, j=j, slot=slot):
            image = k_ref[:, e] * own
            for i in range(j + 1):
                acc_ref[slot + i] += fold(v_ref[i, :, e] * image)
            acc_ref[10 + j] += fold(v_ref[j, :, e] * (v_ref[0, :, e] * share))
            return carry

        lax.fori_loop(4, 8, gram, 0)
        slot += j + 1
        if j < 3:

            def step(e, carry, j=j):
                rows = sum_rows(k_ref[:, e - 1], k_ref[:, e], k_ref[:, e + 1], first_x, last_x)
                total = sum_lanes(rows, first_y, last_y)
                for z in range(8):
                    image = total[z] * (1.0 / span)
                    if z in (0, 7):
                        image = image * p_ref[z // 7, e]
                    v_ref[j + 1, z, e] = image - 0.5 * v_ref[j, z, e]
                return carry

            lax.fori_loop(low + 1, high - 1, step, 0)
    at = 3 + 2 * core
    for j in range(ROUNDS):
        for e in range(4):
            v_out[j, :, e] = v_ref[j, :, at + e]
    lane = iota(128, 1)
    packed = jnp.zeros((8, 128), f32)
    for k in range(14):
        total = jnp.sum(jnp.sum(acc_ref[k], axis=0, keepdims=True), axis=1, keepdims=True)
        packed = jnp.where(lane == k, total, packed)
    for k in range(m_out.shape[0]):
        m_out[k] = packed


def final_kernel(m_ref, v_ref, w_ref, faces_ref, dy_ref, out_ref, q_ref, f_ref):
    lanes = 256
    sums = m_ref[0]
    for k in range(1, m_ref.shape[0]):
        sums = sums + m_ref[k]
    lane = iota(128, 1)

    def moment(k):
        return jnp.sum(jnp.where(lane == k, sums, 0.0), axis=1, keepdims=True)

    e = {}
    slot = 0
    for j in range(ROUNDS):
        for i in range(j + 1):
            e[j, i] = moment(slot)
            slot += 1
    g = [moment(10 + j) for j in range(ROUNDS)]
    low, diag, scaled = {}, [], {}
    for j in range(ROUNDS):
        d = e[j, j]
        for k in range(j):
            d = d - low[j, k] * scaled[j, k]
        diag.append(d)
        for i in range(j + 1, ROUNDS):
            t = e[i, j]
            for k in range(j):
                t = t - scaled[i, k] * low[j, k]
            scaled[i, j] = t
            low[i, j] = t / d
    y = []
    for j in range(ROUNDS):
        t = g[j]
        for k in range(j):
            t = t - low[j, k] * y[k]
        y.append(t)
    c = [None] * ROUNDS
    for j in reversed(range(ROUNDS)):
        t = y[j] / diag[j]
        for k in range(j + 1, ROUNDS):
            t = t - low[k, j] * c[k]
        c[j] = t
    coef = [jnp.broadcast_to(t, (8, lanes)) for t in c]

    dcoef = row_coefs(lanes, deriv)
    wxy = node_x(lanes, node_weights) * node_y(lanes, node_weights)
    inv = node_x(lanes, inverse_mass) * node_y(lanes, inverse_mass)
    first_x = (iota(lanes, 0) == 0).astype(f32)
    last_x = (iota(lanes, 0) == 7).astype(f32)
    first_y = ((iota(lanes, 1) & 7) == 0).astype(f32)
    last_y = ((iota(lanes, 1) & 7) == 7).astype(f32)

    def body(e, carry):
        q = v_ref[0, :, e] * coef[0]
        for j in range(1, ROUNDS):
            q = q + v_ref[j, :, e] * coef[j]

        @pl.when((e == 1) | (e == 2))
        def _():
            q_ref[:, e - 1] = own_lanes(q)

        slopes = [
            weigh(row_turns(q), dcoef),
            lanes_times(q, dy_ref[...]),
            jnp.stack(depth([q[z] for z in range(8)], deriv)),
        ]
        for i in range(3):
            for z in range(8):
                f_ref[i, z, e] = (wxy * float(node_weights[z])) * slopes[i][z]
        return carry

    lax.fori_loop(0, 4, body, 0)
    inside = 1.0 - rim_mask(128).astype(f32)
    walls = expand_walls(faces_ref)
    for e in range(2):
        for i in range(3):
            rows = sum_rows(f_ref[i, :, e], f_ref[i, :, e + 1], f_ref[i, :, e + 2], first_x, last_x)
            total = own_lanes(sum_lanes(rows, first_y, last_y) * inv)
            for z in range(8):
                got = w_ref[i, z, e] - total[z] * float(1.0 / node_weights[z])
                if z in (0, 7):
                    face = jnp.broadcast_to(walls[z // 7][e : e + 1], (8, 128))
                    got = got * (inside * (1.0 - face))
                out_ref[i, z, e] = got


def shape(*dims):
    return jax.ShapeDtypeStruct(dims, f32)


def call(kernel, out_shape, scratch, *args):
    return pl.pallas_call(
        kernel,
        out_shape=out_shape,
        in_specs=[pl.BlockSpec(memory_space=pltpu.VMEM)] * len(args),
        out_specs=jax.tree.map(lambda s: pl.BlockSpec(memory_space=pltpu.VMEM), out_shape),
        scratch_shapes=scratch,
        compiler_params=pltpu.CompilerParams(vmem_limit_bytes=48 * 2**20),
    )(*args)


def shift(value, axis, by):
    size = lax.axis_size(axis)
    return lax.ppermute(value, axis, [(i, (i + by) % size) for i in range(size)])


def spread_sum(value, axis, groups):
    return lax.all_to_all(value, axis, 0, 0, axis_index_groups=groups, tiled=True)


def local(adjoint, checkpoints, wall_faces):
    nx, ny = lax.axis_size("gx"), lax.axis_size("gy")
    dy = jnp.asarray(lane_deriv)
    ky = jnp.asarray(lane_stiff)
    adj = adjoint.reshape(3, 8, 2, 8, 128)
    flow = checkpoints.reshape(3, 8, 2, 8, 128)
    vm = pltpu.VMEM
    rhs, up, down = call(
        rhs_kernel,
        (shape(3, 8, 2, 8, 128), shape(3, 4, 2, 8, 128), shape(3, 4, 2, 8, 128)),
        [vm((2, 2, 8, 128), f32)],
        adj, flow, wall_faces, dy, ky,
    )
    left = shift(up, "gy", 1)
    right = shift(down, "gy", -1)
    wide = call(join_kernel, shape(3, 8, 2, 8, 256), [], rhs, left, right)
    before = shift(wide, "gx", 1)
    after = shift(wide, "gx", -1)
    source, moved = call(
        source_kernel,
        (shape(8, 2, 8, 256), shape(3, 8, 2, 8, 128)),
        [vm((3, 8, 6, 8, 256), f32), vm((8, 4, 8, 256), f32)],
        before, wide, after, dy,
    )
    lower = shift(source, "gx", 2)
    upper = shift(source, "gx", -2)
    mine = jnp.stack([lower, source, upper])
    other = lax.ppermute(mine, "gx", [(i, i ^ 1) for i in range(nx)])
    basis, sums = call(
        krylov_kernel,
        (shape(4, 8, 4, 8, 256), shape(nx // 2, 8, 128)),
        [
            vm((4, 8, 12, 8, 256), f32),
            vm((8, 12, 8, 256), f32),
            vm((2, 12, 8, 256), f32),
            vm((14, 8, 128), f32),
        ],
        mine, other, ky,
    )
    along = [[2 * z + c for z in range(nx // 2)] for c in range(2)]
    sums = jnp.sum(spread_sum(sums, "gx", along), axis=0, keepdims=True)
    sums = spread_sum(jnp.broadcast_to(sums, (ny, 8, 128)), "gy", None)
    velocity, pressure = call(
        final_kernel,
        (shape(3, 8, 2, 8, 128), shape(8, 2, 8, 128)),
        [vm((3, 8, 4, 8, 256), f32)],
        sums, basis, moved, wall_faces, dy,
    )
    return velocity.reshape(3, 8, 16, 128), pressure.reshape(8, 16, 128)


def solution(mesh):
    return jax.shard_map(
        local,
        mesh=mesh,
        in_specs=(P(None, None, "gx", "gy"), P(None, None, None, "gx", "gy"), P(None, "gx", "gy")),
        out_specs=(P(None, None, "gx", "gy"), P(None, "gx", "gy")),
        check_vma=False,
    )
```

```python
import jax
import jax.numpy as jnp
import numpy as np
from jax import lax
from jax.experimental import pallas as pl
from jax.experimental.pallas import tpu as pltpu
from jax.sharding import PartitionSpec as P

f32 = jnp.float32
bf16 = jnp.bfloat16

node_points = np.array(
    [
        -1.0,
        -0.8717401485096066,
        -0.5917001814331423,
        -0.2092992179024789,
        0.2092992179024789,
        0.5917001814331423,
        0.8717401485096066,
        1.0,
    ]
)
node_weights = np.array(
    [
        0.03571428571428571,
        0.2107042271435061,
        0.3411226924835044,
        0.4124587946587038,
        0.4124587946587038,
        0.3411226924835044,
        0.2107042271435061,
        0.03571428571428571,
    ]
)
time_step = 0.05
viscosity = 0.02
span = 8.0
ROUNDS = 4


def derivative_table(points):
    identity = np.eye(points.shape[0])
    spacing = points[:, None] - points[None, :] + identity
    barycentric = 1.0 / np.prod(spacing, axis=1)
    matrix = barycentric[None, :] / barycentric[:, None] / spacing
    matrix = matrix * (1.0 - identity)
    return matrix - identity * np.sum(matrix, axis=1)[:, None]


deriv = derivative_table(node_points)
stiff = deriv.T @ np.diag(node_weights) @ deriv
copies = np.array([2.0, 1, 1, 1, 1, 1, 1, 2.0])
inverse_mass = 1.0 / (copies * node_weights)


scaled_stiff = stiff / node_weights[:, None]


def iota(lanes, dim):
    return lax.broadcasted_iota(jnp.int32, (8, lanes), dim)


def pick(place, values):
    out = jnp.full(place.shape, float(values[0]), f32)
    for k in range(1, 8):
        out = jnp.where(place == k, float(values[k]), out)
    return out


def node_x(lanes, values):
    return pick(iota(lanes, 0), values)


def node_y(lanes, values):
    return pick(iota(lanes, 1) & 7, values)


def rim_mask(lanes):
    a = iota(lanes, 0)
    b = iota(lanes, 1) & 7
    return (a == 0) | (a == 7) | (b == 0) | (b == 7)


def row_coefs(lanes, matrix):
    return [node_x(lanes, [matrix[a, (a - r) % 8] for a in range(8)]) for r in range(8)]


def row_turns(value):
    return [value] + [pltpu.roll(value, r, axis=1) for r in range(1, 8)]


def weigh(turns, coefs):
    out = turns[0] * coefs[0]
    for r in range(1, 8):
        out = out + turns[r] * coefs[r]
    return out


def depth(planes, matrix, sign):
    plus = [planes[k] + planes[7 - k] for k in range(4)]
    minus = [planes[k] - planes[7 - k] for k in range(4)]
    out = [None] * 8
    for a in range(4):
        even = plus[0] * float(0.5 * (matrix[a, 0] + matrix[a, 7]))
        odd = minus[0] * float(0.5 * (matrix[a, 0] - matrix[a, 7]))
        for k in range(1, 4):
            even = even + plus[k] * float(0.5 * (matrix[a, k] + matrix[a, 7 - k]))
            odd = odd + minus[k] * float(0.5 * (matrix[a, k] - matrix[a, 7 - k]))
        out[a] = even + odd
        out[7 - a] = even - odd if sign > 0 else odd - even
    return out


def z_slope(value):
    return jnp.stack(depth([value[z] for z in range(8)], deriv, -1))


def lane_table(matrix):
    lane = iota(128, 1)
    pattern = jnp.zeros((8, 128), f32)
    for b in range(8):
        pattern = jnp.where((lane & 7) == b, node_x(128, matrix[b]), pattern)
    full = jnp.concatenate([jnp.where(lane // 8 == k, pattern, 0.0) for k in range(16)], axis=0)
    high = full.astype(bf16)
    low = (full - high.astype(f32)).astype(bf16)
    pair = jnp.concatenate([high, low], axis=1)
    return jnp.concatenate([pair, pair], axis=0)


def lanes_times(value, table):
    n, _, lanes = value.shape
    blocks = [value[:, :, k * 128 : (k + 1) * 128].reshape(n * 8, 128) for k in range(lanes // 128)]
    rows = blocks[0] if len(blocks) == 1 else jnp.concatenate(blocks, axis=0)
    high = rows.astype(bf16)
    low = (rows - high.astype(f32)).astype(bf16)
    both = jnp.concatenate([high, low], axis=1)
    got = jnp.dot(both, table, preferred_element_type=f32)
    got = got[:, :128] + got[:, 128:]
    parts = [got[k * n * 8 : (k + 1) * n * 8].reshape(n, 8, 128) for k in range(lanes // 128)]
    return parts[0] if len(parts) == 1 else jnp.concatenate(parts, axis=2)


def sum_lanes(value, first, last):
    lanes = value.shape[2]
    return (
        value
        + last * pltpu.roll(value, lanes - 1, axis=2)
        + first * pltpu.roll(value, 1, axis=2)
    )


def sum_rows(before, here, after, first, last):
    return here + last * pltpu.roll(after, 7, axis=1) + first * pltpu.roll(before, 1, axis=1)


def own_lanes(value):
    n = value.shape[0]
    lane = lax.broadcasted_iota(jnp.int32, (n, 8, 128), 2)
    mixed = jnp.where(lane >= 64, value[:, :, :128], value[:, :, 128:])
    return pltpu.roll(mixed, 64, axis=2)


def expand_walls(faces_ref):
    spread = (
        lax.broadcasted_iota(jnp.int32, (16, 128), 1) // 8
        == lax.broadcasted_iota(jnp.int32, (16, 128), 0)
    ).astype(f32)
    out = []
    for face in range(2):
        rows = faces_ref[face].astype(f32)
        wide = jnp.dot(rows, spread, preferred_element_type=f32)
        out.append(wide)
    return out


def rhs_kernel(
    adj_hbm, flow_hbm, faces_hbm,
    r_ref, up_ref, down_ref, dy_ref, ky_ref,
    adj_ref, flow_ref, faces_ref, u_ref, wall_ref, sems,
):
    moves = [
        pltpu.make_async_copy(src, dst, sems.at[k])
        for k, (src, dst) in enumerate(
            ((adj_hbm, adj_ref), (flow_hbm, flow_ref), (faces_hbm, faces_ref))
        )
    ]
    for move in moves:
        move.start()
    lanes = 128
    dy_ref[...] = lane_table(deriv)
    ky_ref[...] = lane_table(scaled_stiff)
    dcoef = row_coefs(lanes, deriv)
    kcoef = row_coefs(lanes, scaled_stiff)
    wxy = node_x(lanes, node_weights) * node_y(lanes, node_weights)
    rim = rim_mask(lanes)
    half = iota(lanes, 1) < 64
    for move in moves:
        move.wait()
    for face, wide in enumerate(expand_walls(faces_ref)):
        for e in range(2):
            wall_ref[face, e] = jnp.broadcast_to(wide[e : e + 1], (8, lanes))
    for c in range(3):
        for z in range(8):
            rows = flow_ref[c, z].astype(f32)
            u_ref[c, z, 0] = rows[:8]
            u_ref[c, z, 1] = rows[8:]

    def body(e, carry):
        v = [adj_ref[c, :, e] for c in range(3)]
        u = [u_ref[c, :, e] for c in range(3)]
        vall = jnp.concatenate(v, axis=0)
        uall = jnp.concatenate(u, axis=0)
        vdy = lanes_times(vall, dy_ref[...])
        vky = lanes_times(vall, ky_ref[...])
        udy = lanes_times(uall, dy_ref[...])
        stretch = [jnp.zeros((8, 8, lanes), f32)] * 3
        for j in range(3):
            stretch[0] = stretch[0] + v[j] * weigh(row_turns(u[j]), dcoef)
            stretch[1] = stretch[1] + v[j] * udy[8 * j : 8 * j + 8]
            stretch[2] = stretch[2] + v[j] * z_slope(u[j])
        for i in range(3):
            turns = row_turns(v[i])
            planes = [v[i][z] for z in range(8)]
            zd = depth(planes, deriv, -1)
            zk = depth(planes, scaled_stiff, 1)
            xd = weigh(turns, dcoef)
            xk = weigh(turns, kcoef)
            made = []
            for z in range(8):
                wz = float(node_weights[z])
                adv = (
                    u[0][z] * xd[z]
                    + u[1][z] * vdy[8 * i + z]
                    + u[2][z] * zd[z]
                    - stretch[i][z]
                )
                bend = xk[z] + vky[8 * i + z] + zk[z]
                out = (wxy * wz) * (v[i][z] + time_step * adv - (time_step * viscosity) * bend)
                if i == 0 and z in (0, 7):
                    out = jnp.where(rim, wall_ref[z // 7, e], out)
                r_ref[i, z, e] = out
                made.append(out)
            for z in range(4):
                up_ref[i, z, e] = jnp.where(half, pltpu.roll(made[z], 64, axis=1), made[z + 4])
                down_ref[i, z, e] = jnp.where(half, made[z], pltpu.roll(made[z + 4], 64, axis=1))
        return carry

    lax.fori_loop(0, 2, body, 0)


def join_kernel(r_ref, left_ref, right_ref, e_ref, up_ref, down_ref):
    half = iota(128, 1) < 64
    place = iota(256, 0)
    first = place == 0
    last = place == 7
    for c in range(3):
        faces_up = jnp.zeros((8, 256), f32)
        faces_down = jnp.zeros((8, 256), f32)
        for z in range(8):
            tiles = []
            for e in range(2):
                turned = pltpu.roll(r_ref[c, z, e], 64, axis=1)
                left = left_ref[c, z % 4, e]
                right = right_ref[c, z % 4, e]
                if z >= 4:
                    left = pltpu.roll(left, 64, axis=1)
                else:
                    right = pltpu.roll(right, 64, axis=1)
                tile = jnp.concatenate(
                    [jnp.where(half, left, turned), jnp.where(half, turned, right)], axis=1
                )
                e_ref[c, z, e] = tile
                tiles.append(tile)
            if c == 0:
                go_up, go_down = tiles[1], tiles[0]
                if 0 < z < 7:
                    go_up = go_up + jnp.where(first, pltpu.roll(tiles[0], 1, axis=0), 0.0)
                    go_down = go_down + jnp.where(last, pltpu.roll(tiles[1], 7, axis=0), 0.0)
                up_ref[z] = go_up
                down_ref[z] = go_down
            else:
                turned = pltpu.roll(tiles[1], (z + 1) % 8, axis=0) if z < 7 else tiles[1]
                faces_up = jnp.where(place == z, turned, faces_up)
                turned = pltpu.roll(tiles[0], z, axis=0) if z else tiles[0]
                faces_down = jnp.where(place == z, turned, faces_down)
        if c:
            up_ref[7 + c] = faces_up
            down_ref[7 + c] = faces_down


def flags(lanes):
    first_x = (iota(lanes, 0) == 0).astype(f32)
    last_x = (iota(lanes, 0) == 7).astype(f32)
    first_y = ((iota(lanes, 1) & 7) == 0).astype(f32)
    last_y = ((iota(lanes, 1) & 7) == 7).astype(f32)
    return first_x, last_x, first_y, last_y


def source_kernel(left_ref, mid_ref, right_ref, dy_ref, b_ref, w_ref, t_ref):
    lanes = 256
    dcoef = row_coefs(lanes, deriv)
    wx = node_x(lanes, node_weights)
    wy = node_y(lanes, node_weights)
    mx = node_x(lanes, copies)
    my = node_y(lanes, copies)
    inv = node_x(lanes, inverse_mass) * node_y(lanes, inverse_mass)
    first_x, last_x, first_y, last_y = flags(lanes)
    inside = 1.0 - rim_mask(lanes).astype(f32)

    def wall(tile):
        return jnp.broadcast_to(tile[0:1, :], (8, lanes))

    def finish(rows, faces):
        total = sum_lanes(rows, first_y, last_y)
        planes = []
        for z in range(8):
            got = total[z] * (inv * float(1.0 / node_weights[z]))
            if z in (0, 7):
                got = got * (inside * (1.0 - wall(faces[z])))
            planes.append(got)
        return jnp.stack(planes)

    def turn(tile, by):
        by = by % 8
        return pltpu.roll(tile, by, axis=0) if by else tile

    slope = {}
    left = left_ref[0:8]
    right = right_ref[0:8]
    near = finish(left + last_x * pltpu.roll(mid_ref[0, :, 0], 7, axis=1), left)
    slope[-1] = weigh(row_turns(near), dcoef)
    near = finish(right + first_x * pltpu.roll(mid_ref[0, :, 1], 1, axis=1), right)
    slope[2] = weigh(row_turns(near), dcoef)
    for e in range(2):
        faces = mid_ref[0, :, e]
        w = []
        for c in range(3):
            if c == 0:
                before, after = left, right
            else:
                before = jnp.stack([turn(left_ref[7 + c], 7 - z) for z in range(8)])
                after = jnp.stack([turn(right_ref[7 + c], 8 - z) for z in range(8)])
            if e == 0:
                rows = sum_rows(before, mid_ref[c, :, 0], mid_ref[c, :, 1], first_x, last_x)
            else:
                rows = sum_rows(mid_ref[c, :, 0], mid_ref[c, :, 1], after, first_x, last_x)
            got = finish(rows, faces)
            w.append(got)
            w_ref[c, :, e] = own_lanes(got)
        slope[e] = weigh(row_turns(w[0]), dcoef)
        along = sum_lanes(lanes_times(w[1], dy_ref[...]) * wy, first_y, last_y) * (mx * wx)
        t_ref[:, e] = along + z_slope(w[2]) * (mx * wx * my * wy)
    for e in range(2):
        faces = mid_ref[0, :, e]
        rows = sum_rows(slope[e - 1], slope[e], slope[e + 1], first_x, last_x)
        total = rows * (wx * my * wy) + t_ref[:, e]
        for z in range(8):
            got = total[z] * float(-node_weights[z])
            if z in (0, 7):
                face = wall(faces[z])
                got = jnp.where(inside > 0.5, got * face, face)
            b_ref[z, e] = got


def krylov_kernel(*refs):
    blocks = refs[:5]
    ky_ref, v_out, m_out, v_ref, k_ref, p_ref, acc_ref = refs[5:]
    lanes = 256
    rim = rim_mask(lanes)
    for k, ref in enumerate(blocks):
        for e in range(2):
            at = 2 * k + e
            for z in range(8):
                got = ref[z, e]
                if z in (0, 7):
                    face = jnp.broadcast_to(got[0:1, :], (8, lanes))
                    p_ref[z // 7, at] = jnp.where(rim, 0.0, face)
                    got = jnp.where(rim, 0.0, got)
                v_ref[0, z, at] = got
    kcoef = row_coefs(lanes, scaled_stiff)
    wxy = node_x(lanes, node_weights) * node_y(lanes, node_weights)
    first_x, last_x, first_y, last_y = flags(lanes)
    acc_ref[...] = jnp.zeros(acc_ref.shape, f32)

    def fold(value):
        total = value[0]
        for z in range(1, 8):
            total = total + value[z]
        return total

    def apply(j, e):
        v = v_ref[j, :, e]
        yk = lanes_times(v, ky_ref[...])
        xk = weigh(row_turns(v), kcoef)
        zk = depth([v[z] for z in range(8)], scaled_stiff, 1)
        for z in range(8):
            k_ref[z, e] = (xk[z] + zk[z] + yk[z]) * (wxy * float(node_weights[z] / span))

    slot = 0
    for j in range(ROUNDS):
        low, high = (j, 10 - j) if j < 3 else (4, 6)
        lax.fori_loop(low, high, lambda e, c, j=j: (apply(j, e), c)[1], 0, unroll=2)

        def gram(e, carry, j=j, slot=slot):
            image = k_ref[:, e]
            for i in range(j + 1):
                acc_ref[slot + i] += fold(v_ref[i, :, e] * image)
            acc_ref[10 + j] += fold(v_ref[j, :, e] * v_ref[0, :, e])
            return carry

        lax.fori_loop(4, 6, gram, 0, unroll=2)
        slot += j + 1
        if j < 3:

            def step(e, carry, j=j):
                rows = sum_rows(k_ref[:, e - 1], k_ref[:, e], k_ref[:, e + 1], first_x, last_x)
                total = sum_lanes(rows, first_y, last_y)
                for z in range(8):
                    image = total[z]
                    if z in (0, 7):
                        image = image * p_ref[z // 7, e]
                    v_ref[j + 1, z, e] = image - 0.5 * v_ref[j, z, e]
                return carry

            lax.fori_loop(low + 1, high - 1, step, 0, unroll=2)
    for j in range(ROUNDS):
        for e in range(4):
            v_out[j, :, e] = v_ref[j, :, 3 + e]
    lane = iota(lanes, 1)
    own = (lane >= 64) & (lane < 192)
    share = node_x(lanes, 1.0 / copies) * node_y(lanes, 1.0 / copies)
    lane = iota(128, 1)
    packed = jnp.zeros((8, 128), f32)
    for k in range(14):
        part = jnp.where(own, acc_ref[k], 0.0)
        if k >= 10:
            part = part * share
        part = part[:, :128] + part[:, 128:]
        total = jnp.sum(jnp.sum(part, axis=0, keepdims=True), axis=1, keepdims=True)
        packed = jnp.where(lane == k, total, packed)
    m_out[...] = packed


def final_kernel(m_ref, v_ref, w_ref, faces_ref, dy_ref, out_ref, q_ref):
    lanes = 256
    count = m_ref.shape[0] // 8
    parts = [m_ref[8 * k : 8 * k + 8] for k in range(count)]
    while len(parts) > 1:
        odd = parts[len(parts) // 2 * 2 :]
        parts = [parts[k] + parts[k + 1] for k in range(0, len(parts) - 1, 2)] + odd
    sums = jnp.broadcast_to(jnp.sum(parts[0], axis=0, keepdims=True), (8, 128))
    lane = iota(128, 1)

    def moment(k):
        return jnp.sum(jnp.where(lane == k, sums, 0.0), axis=1, keepdims=True)

    e = {}
    slot = 0
    for j in range(ROUNDS):
        for i in range(j + 1):
            e[j, i] = moment(slot)
            slot += 1
    g = [moment(10 + j) for j in range(ROUNDS)]
    low, diag, scaled = {}, [], {}
    for j in range(ROUNDS):
        d = e[j, j]
        for k in range(j):
            d = d - low[j, k] * scaled[j, k]
        diag.append(d)
        for i in range(j + 1, ROUNDS):
            t = e[i, j]
            for k in range(j):
                t = t - scaled[i, k] * low[j, k]
            scaled[i, j] = t
            low[i, j] = t / d
    y = []
    for j in range(ROUNDS):
        t = g[j]
        for k in range(j):
            t = t - low[j, k] * y[k]
        y.append(t)
    c = [None] * ROUNDS
    for j in reversed(range(ROUNDS)):
        t = y[j] / diag[j]
        for k in range(j + 1, ROUNDS):
            t = t - low[k, j] * c[k]
        c[j] = t
    coef = [jnp.broadcast_to(t * (1.0 / span), (8, lanes)) for t in c]

    dcoef = row_coefs(lanes, deriv)
    first_x, last_x, first_y, last_y = flags(lanes)
    mean_x = node_x(lanes, 1.0 / copies)
    mean_y = node_y(lanes, 1.0 / copies)
    inside = 1.0 - rim_mask(128).astype(f32)
    walls = expand_walls(faces_ref)
    q, slope = [], []
    for e in range(4):
        got = v_ref[0, :, e] * coef[0]
        for j in range(1, ROUNDS):
            got = got + v_ref[j, :, e] * coef[j]
        q.append(got)
        slope.append(weigh(row_turns(got), dcoef))
    for e in range(2):
        here = q[e + 1]
        q_own = own_lanes(here)
        q_ref[:, e] = q_own
        along_x = sum_rows(slope[e], slope[e + 1], slope[e + 2], first_x, last_x) * mean_x
        along_y = sum_lanes(lanes_times(here, dy_ref[...]), first_y, last_y) * mean_y
        parts = [own_lanes(along_x), own_lanes(along_y), z_slope(q_own)]
        for i in range(3):
            for z in range(8):
                got = w_ref[i, z, e] - parts[i][z]
                if z in (0, 7):
                    face = jnp.broadcast_to(walls[z // 7][e : e + 1], (8, 128))
                    got = got * (inside * (1.0 - face))
                out_ref[i, z, e] = got


def shape(*dims):
    return jax.ShapeDtypeStruct(dims, f32)


def call(kernel, out_shape, scratch, *args, space=pltpu.VMEM, vmem=48):
    return pl.pallas_call(
        kernel,
        out_shape=out_shape,
        in_specs=[pl.BlockSpec(memory_space=space)] * len(args),
        out_specs=jax.tree.map(lambda s: pl.BlockSpec(memory_space=pltpu.VMEM), out_shape),
        scratch_shapes=scratch,
        compiler_params=pltpu.CompilerParams(vmem_limit_bytes=vmem * 2**20),
    )(*args)


def shift(value, axis, by):
    size = lax.axis_size(axis)
    return lax.ppermute(value, axis, [(i, (i + by) % size) for i in range(size)])


def total_rows(packed):
    nx, ny = lax.axis_size("gx"), lax.axis_size("gy")
    pairs = [[i, i + 1] for i in range(0, nx, 2)]
    both = lax.all_gather(packed, "gx", axis_index_groups=pairs)
    rows = jnp.broadcast_to(both[0, :1] + both[1, :1], (nx // 2 * ny, 128))
    chips = [[(2 * z + c) * ny + y for z in range(nx // 2) for y in range(ny)] for c in range(2)]
    return lax.all_to_all(rows, ("gx", "gy"), 0, 0, axis_index_groups=chips, tiled=True)


def local(adjoint, checkpoints, wall_faces):
    adj = adjoint.reshape(3, 8, 2, 8, 128)
    flow = checkpoints.reshape(3, 8, 16, 128)
    vm = pltpu.VMEM
    table = jax.ShapeDtypeStruct((256, 256), bf16)
    strip = shape(3, 4, 2, 8, 128)
    rhs, up, down, dy, ky = call(
        rhs_kernel,
        (shape(3, 8, 2, 8, 128), strip, strip, table, table),
        [
            vm((3, 8, 2, 8, 128), f32),
            vm((3, 8, 16, 128), bf16),
            vm((2, 2, 16), jnp.int32),
            vm((3, 8, 2, 8, 128), f32),
            vm((2, 2, 8, 128), f32),
            pltpu.SemaphoreType.DMA((3,)),
        ],
        adj, flow, wall_faces,
        space=pl.ANY,
        vmem=62,
    )
    left = shift(up, "gy", 1)
    right = shift(down, "gy", -1)
    packet = shape(10, 8, 256)
    wide, up, down = call(
        join_kernel, (shape(3, 8, 2, 8, 256), packet, packet), [], rhs, left, right
    )
    before = shift(up, "gx", 1)
    after = shift(down, "gx", -1)
    source, moved = call(
        source_kernel,
        (shape(8, 2, 8, 256), shape(3, 8, 2, 8, 128)),
        [vm((8, 2, 8, 256), f32)],
        before, wide, after, dy,
    )
    left = shift(source, "gx", 1)
    right = shift(source, "gx", -1)
    left2 = shift(left, "gx", 1)
    right2 = shift(right, "gx", -1)
    basis, packed = call(
        krylov_kernel,
        (shape(4, 8, 4, 8, 256), shape(8, 128)),
        [
            vm((4, 8, 10, 8, 256), f32),
            vm((8, 10, 8, 256), f32),
            vm((2, 10, 8, 256), f32),
            vm((14, 8, 256), f32),
        ],
        left2, left, source, right, right2, ky,
    )
    velocity, pressure = call(
        final_kernel,
        (shape(3, 8, 2, 8, 128), shape(8, 2, 8, 128)),
        [],
        total_rows(packed), basis, moved, wall_faces, dy,
    )
    return velocity.reshape(3, 8, 16, 128), pressure.reshape(8, 16, 128)


def solution(mesh):
    return jax.shard_map(
        local,
        mesh=mesh,
        in_specs=(P(None, None, "gx", "gy"), P(None, None, None, "gx", "gy"), P(None, "gx", "gy")),
        out_specs=(P(None, None, "gx", "gy"), P(None, "gx", "gy")),
        check_vma=False,
    )
```

```python
import jax
import jax.numpy as jnp
import numpy as np
from jax import lax
from jax.experimental import pallas as pl
from jax.experimental.pallas import tpu as pltpu
from jax.sharding import PartitionSpec as P

f32 = jnp.float32
bf16 = jnp.bfloat16

node_points = np.array(
    [
        -1.0,
        -0.8717401485096066,
        -0.5917001814331423,
        -0.2092992179024789,
        0.2092992179024789,
        0.5917001814331423,
        0.8717401485096066,
        1.0,
    ]
)
node_weights = np.array(
    [
        0.03571428571428571,
        0.2107042271435061,
        0.3411226924835044,
        0.4124587946587038,
        0.4124587946587038,
        0.3411226924835044,
        0.2107042271435061,
        0.03571428571428571,
    ]
)
time_step = 0.05
viscosity = 0.02
span = 8.0
ROUNDS = 4


def derivative_table(points):
    identity = np.eye(points.shape[0])
    spacing = points[:, None] - points[None, :] + identity
    barycentric = 1.0 / np.prod(spacing, axis=1)
    matrix = barycentric[None, :] / barycentric[:, None] / spacing
    matrix = matrix * (1.0 - identity)
    return matrix - identity * np.sum(matrix, axis=1)[:, None]


deriv = derivative_table(node_points)
stiff = deriv.T @ np.diag(node_weights) @ deriv
copies = np.array([2.0, 1, 1, 1, 1, 1, 1, 2.0])
inverse_mass = 1.0 / (copies * node_weights)


scaled_stiff = stiff / node_weights[:, None]


def iota(lanes, dim):
    return lax.broadcasted_iota(jnp.int32, (8, lanes), dim)


def pick(place, values):
    out = jnp.full(place.shape, float(values[0]), f32)
    for k in range(1, 8):
        out = jnp.where(place == k, float(values[k]), out)
    return out


def node_x(lanes, values):
    return pick(iota(lanes, 0), values)


def node_y(lanes, values):
    return pick(iota(lanes, 1) & 7, values)


def rim_mask(lanes):
    a = iota(lanes, 0)
    b = iota(lanes, 1) & 7
    return (a == 0) | (a == 7) | (b == 0) | (b == 7)


def row_coefs(lanes, matrix):
    return [node_x(lanes, [matrix[a, (a - r) % 8] for a in range(8)]) for r in range(8)]


def row_turns(value):
    return [value] + [pltpu.roll(value, r, axis=1) for r in range(1, 8)]


def weigh(turns, coefs):
    out = turns[0] * coefs[0]
    for r in range(1, 8):
        out = out + turns[r] * coefs[r]
    return out


def depth(planes, matrix, sign):
    plus = [planes[k] + planes[7 - k] for k in range(4)]
    minus = [planes[k] - planes[7 - k] for k in range(4)]
    out = [None] * 8
    for a in range(4):
        even = plus[0] * float(0.5 * (matrix[a, 0] + matrix[a, 7]))
        odd = minus[0] * float(0.5 * (matrix[a, 0] - matrix[a, 7]))
        for k in range(1, 4):
            even = even + plus[k] * float(0.5 * (matrix[a, k] + matrix[a, 7 - k]))
            odd = odd + minus[k] * float(0.5 * (matrix[a, k] - matrix[a, 7 - k]))
        out[a] = even + odd
        out[7 - a] = even - odd if sign > 0 else odd - even
    return out


def z_slope(value):
    return jnp.stack(depth([value[z] for z in range(8)], deriv, -1))


def lane_table(matrix):
    lane = iota(128, 1)
    pattern = jnp.zeros((8, 128), f32)
    for b in range(8):
        pattern = jnp.where((lane & 7) == b, node_x(128, matrix[b]), pattern)
    full = jnp.concatenate([jnp.where(lane // 8 == k, pattern, 0.0) for k in range(16)], axis=0)
    high = full.astype(bf16)
    low = (full - high.astype(f32)).astype(bf16)
    pair = jnp.concatenate([high, low], axis=1)
    return jnp.concatenate([pair, pair], axis=0)


def lanes_times(value, table):
    n, _, lanes = value.shape
    blocks = [value[:, :, k * 128 : (k + 1) * 128].reshape(n * 8, 128) for k in range(lanes // 128)]
    rows = blocks[0] if len(blocks) == 1 else jnp.concatenate(blocks, axis=0)
    high = rows.astype(bf16)
    low = (rows - high.astype(f32)).astype(bf16)
    both = jnp.concatenate([high, low], axis=1)
    got = jnp.dot(both, table, preferred_element_type=f32)
    got = got[:, :128] + got[:, 128:]
    parts = [got[k * n * 8 : (k + 1) * n * 8].reshape(n, 8, 128) for k in range(lanes // 128)]
    return parts[0] if len(parts) == 1 else jnp.concatenate(parts, axis=2)


def sum_lanes(value, first, last):
    lanes = value.shape[2]
    return (
        value
        + last * pltpu.roll(value, lanes - 1, axis=2)
        + first * pltpu.roll(value, 1, axis=2)
    )


def sum_rows(before, here, after, first, last):
    return here + last * pltpu.roll(after, 7, axis=1) + first * pltpu.roll(before, 1, axis=1)


def own_lanes(value):
    n = value.shape[0]
    lane = lax.broadcasted_iota(jnp.int32, (n, 8, 128), 2)
    mixed = jnp.where(lane >= 64, value[:, :, :128], value[:, :, 128:])
    return pltpu.roll(mixed, 64, axis=2)


def expand_walls(faces_ref):
    spread = (
        lax.broadcasted_iota(jnp.int32, (16, 128), 1) // 8
        == lax.broadcasted_iota(jnp.int32, (16, 128), 0)
    ).astype(f32)
    out = []
    for face in range(2):
        rows = faces_ref[face].astype(f32)
        wide = jnp.dot(rows, spread, preferred_element_type=f32)
        out.append(wide)
    return out


def rhs_kernel(
    adj_hbm, flow_hbm, faces_hbm,
    r_ref, up_ref, down_ref, dy_ref, ky_ref,
    adj_ref, flow_ref, faces_ref, u_ref, wall_ref, sems,
):
    moves = [
        pltpu.make_async_copy(src, dst, sems.at[k])
        for k, (src, dst) in enumerate(
            ((adj_hbm, adj_ref), (flow_hbm, flow_ref), (faces_hbm, faces_ref))
        )
    ]
    for move in moves:
        move.start()
    lanes = 128
    dy_ref[...] = lane_table(deriv)
    ky_ref[...] = lane_table(scaled_stiff)
    dcoef = row_coefs(lanes, deriv)
    kcoef = row_coefs(lanes, scaled_stiff)
    wxy = node_x(lanes, node_weights) * node_y(lanes, node_weights)
    rim = rim_mask(lanes)
    half = iota(lanes, 1) < 64
    for move in moves:
        move.wait()
    for face, wide in enumerate(expand_walls(faces_ref)):
        for e in range(2):
            wall_ref[face, e] = jnp.broadcast_to(wide[e : e + 1], (8, lanes))
    for c in range(3):
        for z in range(8):
            rows = flow_ref[c, z].astype(f32)
            u_ref[c, z, 0] = rows[:8]
            u_ref[c, z, 1] = rows[8:]

    def body(e, carry):
        v = [adj_ref[c, :, e] for c in range(3)]
        u = [u_ref[c, :, e] for c in range(3)]
        vall = jnp.concatenate(v, axis=0)
        uall = jnp.concatenate(u, axis=0)
        vdy = lanes_times(vall, dy_ref[...])
        vky = lanes_times(vall, ky_ref[...])
        udy = lanes_times(uall, dy_ref[...])
        stretch = [jnp.zeros((8, 8, lanes), f32)] * 3
        for j in range(3):
            stretch[0] = stretch[0] + v[j] * weigh(row_turns(u[j]), dcoef)
            stretch[1] = stretch[1] + v[j] * udy[8 * j : 8 * j + 8]
            stretch[2] = stretch[2] + v[j] * z_slope(u[j])
        for i in range(3):
            turns = row_turns(v[i])
            planes = [v[i][z] for z in range(8)]
            zd = depth(planes, deriv, -1)
            zk = depth(planes, scaled_stiff, 1)
            xd = weigh(turns, dcoef)
            xk = weigh(turns, kcoef)
            made = []
            for z in range(8):
                wz = float(node_weights[z])
                adv = (
                    u[0][z] * xd[z]
                    + u[1][z] * vdy[8 * i + z]
                    + u[2][z] * zd[z]
                    - stretch[i][z]
                )
                bend = xk[z] + vky[8 * i + z] + zk[z]
                out = (wxy * wz) * (v[i][z] + time_step * adv - (time_step * viscosity) * bend)
                if i == 0 and z in (0, 7):
                    out = jnp.where(rim, wall_ref[z // 7, e], out)
                r_ref[i, z, e] = out
                made.append(out)
            for z in range(4):
                up_ref[i, z, e] = jnp.where(half, pltpu.roll(made[z], 64, axis=1), made[z + 4])
                down_ref[i, z, e] = jnp.where(half, made[z], pltpu.roll(made[z + 4], 64, axis=1))
        return carry

    lax.fori_loop(0, 2, body, 0)


def hold_kernel(r_ref, turned_ref):
    for c in range(3):
        for z in range(8):
            for e in range(2):
                turned_ref[c, z, e] = pltpu.roll(r_ref[c, z, e], 64, axis=1)


def join_kernel(r_ref, left_ref, right_ref, e_ref, up_ref, down_ref):
    half = iota(128, 1) < 64
    place = iota(256, 0)
    first = place == 0
    last = place == 7
    for c in range(3):
        faces_up = jnp.zeros((8, 256), f32)
        faces_down = jnp.zeros((8, 256), f32)
        for z in range(8):
            tiles = []
            for e in range(2):
                turned = r_ref[c, z, e]
                left = left_ref[c, z % 4, e]
                right = right_ref[c, z % 4, e]
                if z >= 4:
                    left = pltpu.roll(left, 64, axis=1)
                else:
                    right = pltpu.roll(right, 64, axis=1)
                tile = jnp.concatenate(
                    [jnp.where(half, left, turned), jnp.where(half, turned, right)], axis=1
                )
                e_ref[c, z, e] = tile
                tiles.append(tile)
            if c == 0:
                go_up, go_down = tiles[1], tiles[0]
                if 0 < z < 7:
                    go_up = go_up + jnp.where(first, pltpu.roll(tiles[0], 1, axis=0), 0.0)
                    go_down = go_down + jnp.where(last, pltpu.roll(tiles[1], 7, axis=0), 0.0)
                up_ref[z] = go_up
                down_ref[z] = go_down
            else:
                turned = pltpu.roll(tiles[1], (z + 1) % 8, axis=0) if z < 7 else tiles[1]
                faces_up = jnp.where(place == z, turned, faces_up)
                turned = pltpu.roll(tiles[0], z, axis=0) if z else tiles[0]
                faces_down = jnp.where(place == z, turned, faces_down)
        if c:
            up_ref[7 + c] = faces_up
            down_ref[7 + c] = faces_down


def flags(lanes):
    first_x = (iota(lanes, 0) == 0).astype(f32)
    last_x = (iota(lanes, 0) == 7).astype(f32)
    first_y = ((iota(lanes, 1) & 7) == 0).astype(f32)
    last_y = ((iota(lanes, 1) & 7) == 7).astype(f32)
    return first_x, last_x, first_y, last_y


def source_kernel(left_ref, mid_ref, right_ref, dy_ref, b_ref, w_ref, open_ref, t_ref):
    lanes = 256
    dcoef = row_coefs(lanes, deriv)
    wx = node_x(lanes, node_weights)
    wy = node_y(lanes, node_weights)
    mx = node_x(lanes, copies)
    my = node_y(lanes, copies)
    inv = node_x(lanes, inverse_mass) * node_y(lanes, inverse_mass)
    first_x, last_x, first_y, last_y = flags(lanes)
    inside = 1.0 - rim_mask(lanes).astype(f32)

    def wall(tile):
        return jnp.broadcast_to(tile[0:1, :], (8, lanes))

    def finish(rows, faces):
        total = sum_lanes(rows, first_y, last_y)
        planes = []
        for z in range(8):
            got = total[z] * (inv * float(1.0 / node_weights[z]))
            if z in (0, 7):
                got = got * (inside * (1.0 - wall(faces[z])))
            planes.append(got)
        return jnp.stack(planes)

    def turn(tile, by):
        by = by % 8
        return pltpu.roll(tile, by, axis=0) if by else tile

    slope = {}
    left = left_ref[0:8]
    right = right_ref[0:8]
    near = finish(left + last_x * pltpu.roll(mid_ref[0, :, 0], 7, axis=1), left)
    slope[-1] = weigh(row_turns(near), dcoef)
    near = finish(right + first_x * pltpu.roll(mid_ref[0, :, 1], 1, axis=1), right)
    slope[2] = weigh(row_turns(near), dcoef)
    for e in range(2):
        faces = mid_ref[0, :, e]
        for face in range(2):
            open_face = inside * (1.0 - wall(faces[7 * face]))
            open_ref[face, e] = own_lanes(open_face[None])[0]
        w = []
        for c in range(3):
            if c == 0:
                before, after = left, right
            else:
                before = jnp.stack([turn(left_ref[7 + c], 7 - z) for z in range(8)])
                after = jnp.stack([turn(right_ref[7 + c], 8 - z) for z in range(8)])
            if e == 0:
                rows = sum_rows(before, mid_ref[c, :, 0], mid_ref[c, :, 1], first_x, last_x)
            else:
                rows = sum_rows(mid_ref[c, :, 0], mid_ref[c, :, 1], after, first_x, last_x)
            got = finish(rows, faces)
            w.append(got)
            w_ref[c, :, e] = own_lanes(got)
        slope[e] = weigh(row_turns(w[0]), dcoef)
        along = sum_lanes(lanes_times(w[1], dy_ref[...]) * wy, first_y, last_y) * (mx * wx)
        t_ref[:, e] = along + z_slope(w[2]) * (mx * wx * my * wy)
    for e in range(2):
        faces = mid_ref[0, :, e]
        rows = sum_rows(slope[e - 1], slope[e], slope[e + 1], first_x, last_x)
        total = rows * (wx * my * wy) + t_ref[:, e]
        for z in range(8):
            got = total[z] * float(-node_weights[z])
            if z in (0, 7):
                face = wall(faces[z])
                got = jnp.where(inside > 0.5, got * face, face)
            b_ref[z, e] = got


def krylov_kernel(*refs):
    blocks = refs[:5]
    ky_ref, v_out, m_out, v_ref, k_ref, p_ref, acc_ref = refs[5:]
    lanes = 256
    rim = rim_mask(lanes)
    for k, ref in enumerate(blocks):
        for e in range(2):
            at = 2 * k + e
            for z in range(8):
                got = ref[z, e]
                if z in (0, 7):
                    face = jnp.broadcast_to(got[0:1, :], (8, lanes))
                    p_ref[z // 7, at] = jnp.where(rim, 0.0, face)
                    got = jnp.where(rim, 0.0, got)
                v_ref[0, z, at] = got
    kcoef = row_coefs(lanes, scaled_stiff)
    wxy = node_x(lanes, node_weights) * node_y(lanes, node_weights)
    first_x, last_x, first_y, last_y = flags(lanes)
    acc_ref[...] = jnp.zeros(acc_ref.shape, f32)

    def fold(value):
        total = value[0]
        for z in range(1, 8):
            total = total + value[z]
        return total

    def apply(j, e):
        v = v_ref[j, :, e]
        yk = lanes_times(v, ky_ref[...])
        xk = weigh(row_turns(v), kcoef)
        zk = depth([v[z] for z in range(8)], scaled_stiff, 1)
        for z in range(8):
            k_ref[z, e] = (xk[z] + zk[z] + yk[z]) * (wxy * float(node_weights[z] / span))

    slot = 0
    for j in range(ROUNDS):
        low, high = (j, 10 - j) if j < 3 else (4, 6)
        lax.fori_loop(low, high, lambda e, c, j=j: (apply(j, e), c)[1], 0, unroll=2)

        def gram(e, carry, j=j, slot=slot):
            image = k_ref[:, e]
            for i in range(j + 1):
                acc_ref[slot + i] += fold(v_ref[i, :, e] * image)
            acc_ref[10 + j] += fold(v_ref[j, :, e] * v_ref[0, :, e])
            return carry

        lax.fori_loop(4, 6, gram, 0, unroll=2)
        slot += j + 1
        if j < 3:

            def step(e, carry, j=j):
                rows = sum_rows(k_ref[:, e - 1], k_ref[:, e], k_ref[:, e + 1], first_x, last_x)
                total = sum_lanes(rows, first_y, last_y)
                for z in range(8):
                    image = total[z]
                    if z in (0, 7):
                        image = image * p_ref[z // 7, e]
                    v_ref[j + 1, z, e] = image - 0.5 * v_ref[j, z, e]
                return carry

            lax.fori_loop(low + 1, high - 1, step, 0, unroll=2)
    for j in range(ROUNDS):
        for e in range(4):
            v_out[j, :, e] = v_ref[j, :, 3 + e]
    lane = iota(lanes, 1)
    own = (lane >= 64) & (lane < 192)
    share = node_x(lanes, 1.0 / copies) * node_y(lanes, 1.0 / copies)
    lane = iota(128, 1)
    packed = jnp.zeros((8, 128), f32)
    for k in range(14):
        part = jnp.where(own, acc_ref[k], 0.0)
        if k >= 10:
            part = part * share
        part = part[:, :128] + part[:, 128:]
        total = jnp.sum(jnp.sum(part, axis=0, keepdims=True), axis=1, keepdims=True)
        packed = jnp.where(lane == k, total, packed)
    for k in range(m_out.shape[0]):
        m_out[k] = packed


def final_kernel(m_ref, v_ref, w_ref, open_ref, dy_ref, out_ref, q_ref):
    lanes = 256
    parts = [m_ref[k] for k in range(m_ref.shape[0])]
    while len(parts) > 1:
        odd = parts[len(parts) // 2 * 2 :]
        parts = [parts[k] + parts[k + 1] for k in range(0, len(parts) - 1, 2)] + odd
    sums = parts[0]
    lane = iota(128, 1)

    def moment(k):
        return jnp.sum(jnp.where(lane == k, sums, 0.0), axis=1, keepdims=True)

    e = {}
    slot = 0
    for j in range(ROUNDS):
        for i in range(j + 1):
            e[j, i] = moment(slot)
            slot += 1
    g = [moment(10 + j) for j in range(ROUNDS)]
    low, diag, scaled = {}, [], {}
    for j in range(ROUNDS):
        d = e[j, j]
        for k in range(j):
            d = d - low[j, k] * scaled[j, k]
        diag.append(d)
        for i in range(j + 1, ROUNDS):
            t = e[i, j]
            for k in range(j):
                t = t - scaled[i, k] * low[j, k]
            scaled[i, j] = t
            low[i, j] = t / d
    y = []
    for j in range(ROUNDS):
        t = g[j]
        for k in range(j):
            t = t - low[j, k] * y[k]
        y.append(t)
    c = [None] * ROUNDS
    for j in reversed(range(ROUNDS)):
        t = y[j] / diag[j]
        for k in range(j + 1, ROUNDS):
            t = t - low[k, j] * c[k]
        c[j] = t
    coef = [jnp.broadcast_to(t * (1.0 / span), (8, lanes)) for t in c]

    dcoef = row_coefs(lanes, deriv)
    first_x, last_x, first_y, last_y = flags(lanes)
    mean_x = node_x(lanes, 1.0 / copies)
    mean_y = node_y(lanes, 1.0 / copies)
    q, slope = [], []
    for e in range(4):
        got = v_ref[0, :, e] * coef[0]
        for j in range(1, ROUNDS):
            got = got + v_ref[j, :, e] * coef[j]
        q.append(got)
        slope.append(weigh(row_turns(got), dcoef))
    for e in range(2):
        here = q[e + 1]
        q_own = own_lanes(here)
        q_ref[:, e] = q_own
        along_x = sum_rows(slope[e], slope[e + 1], slope[e + 2], first_x, last_x) * mean_x
        along_y = sum_lanes(lanes_times(here, dy_ref[...]), first_y, last_y) * mean_y
        parts = [own_lanes(along_x), own_lanes(along_y), z_slope(q_own)]
        for i in range(3):
            for z in range(8):
                got = w_ref[i, z, e] - parts[i][z]
                if z in (0, 7):
                    got = got * open_ref[z // 7, e]
                out_ref[i, z, e] = got


def shape(*dims):
    return jax.ShapeDtypeStruct(dims, f32)


def call(kernel, out_shape, scratch, *args, space=pltpu.VMEM, vmem=48, cost=None):
    return pl.pallas_call(
        kernel,
        out_shape=out_shape,
        in_specs=[pl.BlockSpec(memory_space=space)] * len(args),
        out_specs=jax.tree.map(lambda s: pl.BlockSpec(memory_space=pltpu.VMEM), out_shape),
        scratch_shapes=scratch,
        cost_estimate=cost,
        compiler_params=pltpu.CompilerParams(vmem_limit_bytes=vmem * 2**20),
    )(*args)


def shift(value, axis, by):
    size = lax.axis_size(axis)
    return lax.ppermute(value, axis, [(i, (i + by) % size) for i in range(size)])


def total_rows(packed):
    nx, ny = lax.axis_size("gx"), lax.axis_size("gy")
    along = [[2 * z + c for z in range(nx // 2)] for c in range(2)]
    part = lax.all_to_all(packed, "gx", 0, 0, axis_index_groups=along, tiled=True)
    part = jnp.broadcast_to(jnp.sum(part, axis=0, keepdims=True), (2 * ny, 8, 128))
    planes = [[(2 * z + c) * ny + y for y in range(ny) for c in range(2)] for z in range(nx // 2)]
    return lax.all_to_all(part, ("gx", "gy"), 0, 0, axis_index_groups=planes, tiled=True)


def local(adjoint, checkpoints, wall_faces):
    adj = adjoint.reshape(3, 8, 2, 8, 128)
    flow = checkpoints.reshape(3, 8, 16, 128)
    vm = pltpu.VMEM
    table = jax.ShapeDtypeStruct((256, 256), bf16)
    strip = shape(3, 4, 2, 8, 128)
    rhs, up, down, dy, ky = call(
        rhs_kernel,
        (shape(3, 8, 2, 8, 128), strip, strip, table, table),
        [
            vm((3, 8, 2, 8, 128), f32),
            vm((3, 8, 16, 128), bf16),
            vm((2, 2, 16), jnp.int32),
            vm((3, 8, 2, 8, 128), f32),
            vm((2, 2, 8, 128), f32),
            pltpu.SemaphoreType.DMA((3,)),
        ],
        adj, flow, wall_faces,
        space=pl.ANY,
        vmem=62,
    )
    left = shift(up, "gy", 1)
    right = shift(down, "gy", -1)
    packet = shape(10, 8, 256)
    cost = pl.CostEstimate(flops=10**6, bytes_accessed=4 * 10**5, transcendentals=0)
    turned = call(hold_kernel, shape(3, 8, 2, 8, 128), [], rhs, cost=cost)
    wide, up, down = call(
        join_kernel, (shape(3, 8, 2, 8, 256), packet, packet), [], turned, left, right
    )
    before = shift(up, "gx", 1)
    after = shift(down, "gx", -1)
    source, moved, opened = call(
        source_kernel,
        (shape(8, 2, 8, 256), shape(3, 8, 2, 8, 128), shape(2, 2, 8, 128)),
        [vm((8, 2, 8, 256), f32)],
        before, wide, after, dy,
    )
    left = shift(source, "gx", 1)
    right = shift(source, "gx", -1)
    left2 = shift(left, "gx", 1)
    right2 = shift(right, "gx", -1)
    basis, packed = call(
        krylov_kernel,
        (shape(4, 8, 4, 8, 256), shape(lax.axis_size("gx") // 2, 8, 128)),
        [
            vm((4, 8, 10, 8, 256), f32),
            vm((8, 10, 8, 256), f32),
            vm((2, 10, 8, 256), f32),
            vm((14, 8, 256), f32),
        ],
        left2, left, source, right, right2, ky,
    )
    velocity, pressure = call(
        final_kernel,
        (shape(3, 8, 2, 8, 128), shape(8, 2, 8, 128)),
        [],
        total_rows(packed), basis, moved, opened, dy,
    )
    return velocity.reshape(3, 8, 16, 128), pressure.reshape(8, 16, 128)


def solution(mesh):
    return jax.shard_map(
        local,
        mesh=mesh,
        in_specs=(P(None, None, "gx", "gy"), P(None, None, None, "gx", "gy"), P(None, "gx", "gy")),
        out_specs=(P(None, None, "gx", "gy"), P(None, "gx", "gy")),
        check_vma=False,
    )
```

```python
import jax
import jax.numpy as jnp
import numpy as np
from jax import lax
from jax.experimental import pallas as pl
from jax.experimental.pallas import tpu as pltpu
from jax.sharding import PartitionSpec as P

f32 = jnp.float32
bf16 = jnp.bfloat16

node_points = np.array(
    [
        -1.0,
        -0.8717401485096066,
        -0.5917001814331423,
        -0.2092992179024789,
        0.2092992179024789,
        0.5917001814331423,
        0.8717401485096066,
        1.0,
    ]
)
node_weights = np.array(
    [
        0.03571428571428571,
        0.2107042271435061,
        0.3411226924835044,
        0.4124587946587038,
        0.4124587946587038,
        0.3411226924835044,
        0.2107042271435061,
        0.03571428571428571,
    ]
)
time_step = 0.05
viscosity = 0.02
span = 8.0
ROUNDS = 4


def derivative_table(points):
    identity = np.eye(points.shape[0])
    spacing = points[:, None] - points[None, :] + identity
    barycentric = 1.0 / np.prod(spacing, axis=1)
    matrix = barycentric[None, :] / barycentric[:, None] / spacing
    matrix = matrix * (1.0 - identity)
    return matrix - identity * np.sum(matrix, axis=1)[:, None]


deriv = derivative_table(node_points)
stiff = deriv.T @ np.diag(node_weights) @ deriv
copies = np.array([2.0, 1, 1, 1, 1, 1, 1, 2.0])
inverse_mass = 1.0 / (copies * node_weights)


scaled_stiff = stiff / node_weights[:, None]


def iota(lanes, dim):
    return lax.broadcasted_iota(jnp.int32, (8, lanes), dim)


def pick(place, values):
    out = jnp.full(place.shape, float(values[0]), f32)
    for k in range(1, 8):
        out = jnp.where(place == k, float(values[k]), out)
    return out


def node_x(lanes, values):
    return pick(iota(lanes, 0), values)


def node_y(lanes, values):
    return pick(iota(lanes, 1) & 7, values)


def rim_mask(lanes):
    a = iota(lanes, 0)
    b = iota(lanes, 1) & 7
    return (a == 0) | (a == 7) | (b == 0) | (b == 7)


def row_coefs(lanes, matrix):
    return [node_x(lanes, [matrix[a, (a - r) % 8] for a in range(8)]) for r in range(8)]


def row_turns(value):
    return [value] + [pltpu.roll(value, r, axis=1) for r in range(1, 8)]


def weigh(turns, coefs):
    out = turns[0] * coefs[0]
    for r in range(1, 8):
        out = out + turns[r] * coefs[r]
    return out


def depth(planes, matrix, sign):
    plus = [planes[k] + planes[7 - k] for k in range(4)]
    minus = [planes[k] - planes[7 - k] for k in range(4)]
    out = [None] * 8
    for a in range(4):
        even = plus[0] * float(0.5 * (matrix[a, 0] + matrix[a, 7]))
        odd = minus[0] * float(0.5 * (matrix[a, 0] - matrix[a, 7]))
        for k in range(1, 4):
            even = even + plus[k] * float(0.5 * (matrix[a, k] + matrix[a, 7 - k]))
            odd = odd + minus[k] * float(0.5 * (matrix[a, k] - matrix[a, 7 - k]))
        out[a] = even + odd
        out[7 - a] = even - odd if sign > 0 else odd - even
    return out


def z_slope(value):
    return jnp.stack(depth([value[z] for z in range(8)], deriv, -1))


def lane_table(matrix):
    lane = iota(128, 1)
    pattern = jnp.zeros((8, 128), f32)
    for b in range(8):
        pattern = jnp.where((lane & 7) == b, node_x(128, matrix[b]), pattern)
    full = jnp.concatenate([jnp.where(lane // 8 == k, pattern, 0.0) for k in range(16)], axis=0)
    high = full.astype(bf16)
    low = (full - high.astype(f32)).astype(bf16)
    pair = jnp.concatenate([high, low], axis=1)
    return jnp.concatenate([pair, pair], axis=0)


def lanes_times(value, table):
    n, _, lanes = value.shape
    blocks = [value[:, :, k * 128 : (k + 1) * 128].reshape(n * 8, 128) for k in range(lanes // 128)]
    rows = blocks[0] if len(blocks) == 1 else jnp.concatenate(blocks, axis=0)
    high = rows.astype(bf16)
    low = (rows - high.astype(f32)).astype(bf16)
    both = jnp.concatenate([high, low], axis=1)
    got = jnp.dot(both, table, preferred_element_type=f32)
    got = got[:, :128] + got[:, 128:]
    parts = [got[k * n * 8 : (k + 1) * n * 8].reshape(n, 8, 128) for k in range(lanes // 128)]
    return parts[0] if len(parts) == 1 else jnp.concatenate(parts, axis=2)


def sum_lanes(value, first, last):
    lanes = value.shape[2]
    return (
        value
        + last * pltpu.roll(value, lanes - 1, axis=2)
        + first * pltpu.roll(value, 1, axis=2)
    )


def sum_rows(before, here, after, first, last):
    return here + last * pltpu.roll(after, 7, axis=1) + first * pltpu.roll(before, 1, axis=1)


def own_lanes(value):
    n = value.shape[0]
    lane = lax.broadcasted_iota(jnp.int32, (n, 8, 128), 2)
    mixed = jnp.where(lane >= 64, value[:, :, :128], value[:, :, 128:])
    return pltpu.roll(mixed, 64, axis=2)


def expand_walls(faces_ref):
    spread = (
        lax.broadcasted_iota(jnp.int32, (16, 128), 1) // 8
        == lax.broadcasted_iota(jnp.int32, (16, 128), 0)
    ).astype(f32)
    out = []
    for face in range(2):
        rows = faces_ref[face].astype(f32)
        wide = jnp.dot(rows, spread, preferred_element_type=f32)
        out.append(wide)
    return out


def rhs_kernel(
    adj_hbm, flow_hbm, faces_hbm,
    r_ref, up_ref, down_ref,
    adj_ref, flow_ref, faces_ref, u_ref, wall_ref, dy_ref, ky_ref, sems,
):
    moves = [
        pltpu.make_async_copy(src, dst, sems.at[k])
        for k, (src, dst) in enumerate(
            ((adj_hbm, adj_ref), (flow_hbm, flow_ref), (faces_hbm, faces_ref))
        )
    ]
    for move in moves:
        move.start()
    lanes = 128
    dy_ref[...] = lane_table(deriv)
    ky_ref[...] = lane_table(scaled_stiff)
    dcoef = row_coefs(lanes, deriv)
    kcoef = row_coefs(lanes, scaled_stiff)
    wxy = node_x(lanes, node_weights) * node_y(lanes, node_weights)
    rim = rim_mask(lanes)
    half = iota(lanes, 1) < 64
    for move in moves:
        move.wait()
    for face, wide in enumerate(expand_walls(faces_ref)):
        for e in range(2):
            wall_ref[face, e] = jnp.broadcast_to(wide[e : e + 1], (8, lanes))
    for c in range(3):
        for z in range(8):
            rows = flow_ref[c, z].astype(f32)
            u_ref[c, z, 0] = rows[:8]
            u_ref[c, z, 1] = rows[8:]

    def body(e, carry):
        v = [adj_ref[c, :, e] for c in range(3)]
        u = [u_ref[c, :, e] for c in range(3)]
        vall = jnp.concatenate(v, axis=0)
        uall = jnp.concatenate(u, axis=0)
        vdy = lanes_times(vall, dy_ref[...])
        vky = lanes_times(vall, ky_ref[...])
        udy = lanes_times(uall, dy_ref[...])
        stretch = [jnp.zeros((8, 8, lanes), f32)] * 3
        for j in range(3):
            stretch[0] = stretch[0] + v[j] * weigh(row_turns(u[j]), dcoef)
            stretch[1] = stretch[1] + v[j] * udy[8 * j : 8 * j + 8]
            stretch[2] = stretch[2] + v[j] * z_slope(u[j])
        for i in range(3):
            turns = row_turns(v[i])
            planes = [v[i][z] for z in range(8)]
            zd = depth(planes, deriv, -1)
            zk = depth(planes, scaled_stiff, 1)
            xd = weigh(turns, dcoef)
            xk = weigh(turns, kcoef)
            made = []
            for z in range(8):
                wz = float(node_weights[z])
                adv = (
                    u[0][z] * xd[z]
                    + u[1][z] * vdy[8 * i + z]
                    + u[2][z] * zd[z]
                    - stretch[i][z]
                )
                bend = xk[z] + vky[8 * i + z] + zk[z]
                out = (wxy * wz) * (v[i][z] + time_step * adv - (time_step * viscosity) * bend)
                if i == 0 and z in (0, 7):
                    out = jnp.where(rim, wall_ref[z // 7, e], out)
                r_ref[i, z, e] = out
                made.append(out)
            for z in range(4):
                up_ref[i, z, e] = jnp.where(half, pltpu.roll(made[z], 64, axis=1), made[z + 4])
                down_ref[i, z, e] = jnp.where(half, made[z], pltpu.roll(made[z + 4], 64, axis=1))
        return carry

    lax.fori_loop(0, 2, body, 0)


def hold_kernel(r_ref, turned_ref, dy_ref, ky_ref):
    dy_ref[...] = lane_table(deriv)
    ky_ref[...] = lane_table(scaled_stiff)
    for c in range(3):
        for z in range(8):
            for e in range(2):
                turned_ref[c, z, e] = pltpu.roll(r_ref[c, z, e], 64, axis=1)


def join_kernel(r_ref, left_ref, right_ref, e_ref, up_ref, down_ref):
    half = iota(128, 1) < 64
    place = iota(256, 0)
    first = place == 0
    last = place == 7
    for c in range(3):
        faces_up = jnp.zeros((8, 256), f32)
        faces_down = jnp.zeros((8, 256), f32)
        for z in range(8):
            tiles = []
            for e in range(2):
                turned = r_ref[c, z, e]
                left = left_ref[c, z % 4, e]
                right = right_ref[c, z % 4, e]
                if z >= 4:
                    left = pltpu.roll(left, 64, axis=1)
                else:
                    right = pltpu.roll(right, 64, axis=1)
                tile = jnp.concatenate(
                    [jnp.where(half, left, turned), jnp.where(half, turned, right)], axis=1
                )
                e_ref[c, z, e] = tile
                tiles.append(tile)
            if c == 0:
                go_up, go_down = tiles[1], tiles[0]
                if 0 < z < 7:
                    go_up = go_up + jnp.where(first, pltpu.roll(tiles[0], 1, axis=0), 0.0)
                    go_down = go_down + jnp.where(last, pltpu.roll(tiles[1], 7, axis=0), 0.0)
                up_ref[z] = go_up
                down_ref[z] = go_down
            else:
                turned = pltpu.roll(tiles[1], (z + 1) % 8, axis=0) if z < 7 else tiles[1]
                faces_up = jnp.where(place == z, turned, faces_up)
                turned = pltpu.roll(tiles[0], z, axis=0) if z else tiles[0]
                faces_down = jnp.where(place == z, turned, faces_down)
        if c:
            up_ref[7 + c] = faces_up
            down_ref[7 + c] = faces_down


def flags(lanes):
    first_x = (iota(lanes, 0) == 0).astype(f32)
    last_x = (iota(lanes, 0) == 7).astype(f32)
    first_y = ((iota(lanes, 1) & 7) == 0).astype(f32)
    last_y = ((iota(lanes, 1) & 7) == 7).astype(f32)
    return first_x, last_x, first_y, last_y


def source_kernel(left_ref, mid_ref, right_ref, dy_ref, b_ref, w_ref, open_ref, t_ref):
    lanes = 256
    dcoef = row_coefs(lanes, deriv)
    wx = node_x(lanes, node_weights)
    wy = node_y(lanes, node_weights)
    mx = node_x(lanes, copies)
    my = node_y(lanes, copies)
    inv = node_x(lanes, inverse_mass) * node_y(lanes, inverse_mass)
    first_x, last_x, first_y, last_y = flags(lanes)
    inside = 1.0 - rim_mask(lanes).astype(f32)

    def wall(tile):
        return jnp.broadcast_to(tile[0:1, :], (8, lanes))

    def finish(rows, faces):
        total = sum_lanes(rows, first_y, last_y)
        planes = []
        for z in range(8):
            got = total[z] * (inv * float(1.0 / node_weights[z]))
            if z in (0, 7):
                got = got * (inside * (1.0 - wall(faces[z])))
            planes.append(got)
        return jnp.stack(planes)

    def turn(tile, by):
        by = by % 8
        return pltpu.roll(tile, by, axis=0) if by else tile

    slope = {}
    left = left_ref[0:8]
    right = right_ref[0:8]
    near = finish(left + last_x * pltpu.roll(mid_ref[0, :, 0], 7, axis=1), left)
    slope[-1] = weigh(row_turns(near), dcoef)
    near = finish(right + first_x * pltpu.roll(mid_ref[0, :, 1], 1, axis=1), right)
    slope[2] = weigh(row_turns(near), dcoef)
    for e in range(2):
        faces = mid_ref[0, :, e]
        for face in range(2):
            open_face = inside * (1.0 - wall(faces[7 * face]))
            open_ref[face, e] = own_lanes(open_face[None])[0]
        w = []
        for c in range(3):
            if c == 0:
                before, after = left, right
            else:
                before = jnp.stack([turn(left_ref[7 + c], 7 - z) for z in range(8)])
                after = jnp.stack([turn(right_ref[7 + c], 8 - z) for z in range(8)])
            if e == 0:
                rows = sum_rows(before, mid_ref[c, :, 0], mid_ref[c, :, 1], first_x, last_x)
            else:
                rows = sum_rows(mid_ref[c, :, 0], mid_ref[c, :, 1], after, first_x, last_x)
            got = finish(rows, faces)
            w.append(got)
            w_ref[c, :, e] = own_lanes(got)
        slope[e] = weigh(row_turns(w[0]), dcoef)
        along = sum_lanes(lanes_times(w[1], dy_ref[...]) * wy, first_y, last_y) * (mx * wx)
        t_ref[:, e] = along + z_slope(w[2]) * (mx * wx * my * wy)
    for e in range(2):
        faces = mid_ref[0, :, e]
        rows = sum_rows(slope[e - 1], slope[e], slope[e + 1], first_x, last_x)
        total = rows * (wx * my * wy) + t_ref[:, e]
        for z in range(8):
            got = total[z] * float(-node_weights[z])
            if z in (0, 7):
                face = wall(faces[z])
                got = jnp.where(inside > 0.5, got * face, face)
            b_ref[z, e] = got


def fold(value):
    total = value[0]
    for z in range(1, 8):
        total = total + value[z]
    return total


def load_block(ref, at, v_ref, p_ref, rim, fill):
    for e in range(2):
        for z in range(8):
            got = ref[z, e]
            if z in (0, 7):
                face = jnp.broadcast_to(got[0:1, :], got.shape)
                p_ref[z // 7, at + e] = jnp.where(rim, 0.0, face)
                got = jnp.where(rim, 0.0, got)
            if fill:
                v_ref[0, z, at + e] = got


def krylov_tools(ky_ref, v_ref, k_ref, p_ref):
    lanes = 256
    kcoef = row_coefs(lanes, scaled_stiff)
    wxy = node_x(lanes, node_weights) * node_y(lanes, node_weights)
    first_x, last_x, first_y, last_y = flags(lanes)

    def apply(j, e):
        v = v_ref[j, :, e]
        yk = lanes_times(v, ky_ref[...])
        xk = weigh(row_turns(v), kcoef)
        zk = depth([v[z] for z in range(8)], scaled_stiff, 1)
        for z in range(8):
            k_ref[j, z, e] = (xk[z] + zk[z] + yk[z]) * (wxy * float(node_weights[z] / span))

    def step(j, e):
        rows = sum_rows(
            k_ref[j, :, e - 1], k_ref[j, :, e], k_ref[j, :, e + 1], first_x, last_x
        )
        total = sum_lanes(rows, first_y, last_y)
        for z in range(8):
            image = total[z]
            if z in (0, 7):
                image = image * p_ref[z // 7, e]
            v_ref[j + 1, z, e] = image - 0.5 * v_ref[j, z, e]

    return apply, step


def over(low, high, body):
    lax.fori_loop(low, high, lambda e, c: (body(e), c)[1], 0, unroll=2)


def sides(low, body):
    over(0, 4, lambda t: body(low + t + (t // 2) * (6 - 2 * low)))


def inner_kernel(left_ref, mid_ref, right_ref, ky_ref, v_ref, k_ref, acc_ref, p_ref):
    rim = rim_mask(256)
    for at, ref in ((2, left_ref), (4, mid_ref), (6, right_ref)):
        load_block(ref, at, v_ref, p_ref, rim, True)
    apply, step = krylov_tools(ky_ref, v_ref, k_ref, p_ref)
    slot = 0
    for j in range(3):
        over(2 + j, 8 - j, lambda e, j=j: apply(j, e))
        for i in range(j + 1):
            acc_ref[slot + i] = fold(v_ref[i, :, 4] * k_ref[j, :, 4]) + fold(
                v_ref[i, :, 5] * k_ref[j, :, 5]
            )
        acc_ref[6 + j] = fold(v_ref[j, :, 4] * v_ref[0, :, 4]) + fold(
            v_ref[j, :, 5] * v_ref[0, :, 5]
        )
        slot += j + 1
        if j < 2:
            over(3 + j, 7 - j, lambda e, j=j: step(j, e))


def outer_kernel(*refs):
    blocks = refs[:5]
    v_in, k_in, acc_ref, ky_ref, v_out, m_out, v_ref, k_ref, p_ref = refs[5:]
    lanes = 256
    rim = rim_mask(lanes)
    for k, ref in enumerate(blocks):
        load_block(ref, 2 * k, v_ref, p_ref, rim, k in (0, 4))
    for j, els in ((0, (2, 3, 4, 5, 6, 7)), (1, (3, 4, 5, 6)), (2, (4, 5))):
        for e in els:
            v_ref[j, :, e] = v_in[j, :, e]
            if j or e not in (4, 5):
                k_ref[j, :, e] = k_in[j, :, e]
    apply, step = krylov_tools(ky_ref, v_ref, k_ref, p_ref)
    for j in range(3):
        sides(j, lambda e, j=j: apply(j, e))
        if j < 2:
            sides(j + 1, lambda e, j=j: step(j, e))
        else:
            over(3, 7, lambda e: step(2, e))
    over(4, 6, lambda e: apply(3, e))
    for e in range(4):
        v_out[0, :, e] = v_ref[2, :, 3 + e]
        v_out[1, :, e] = v_ref[3, :, 3 + e]
    energy = [acc_ref[k] for k in range(6)]
    for i in range(ROUNDS):
        energy.append(
            fold(v_ref[i, :, 4] * k_ref[3, :, 4]) + fold(v_ref[i, :, 5] * k_ref[3, :, 5])
        )
    load = [acc_ref[6 + k] for k in range(3)]
    load.append(
        fold(v_ref[3, :, 4] * v_ref[0, :, 4]) + fold(v_ref[3, :, 5] * v_ref[0, :, 5])
    )
    lane = iota(lanes, 1)
    own = (lane >= 64) & (lane < 192)
    share = node_x(lanes, 1.0 / copies) * node_y(lanes, 1.0 / copies)
    lane = iota(128, 1)
    packed = jnp.zeros((8, 128), f32)
    for k, part in enumerate(energy + load):
        part = jnp.where(own, part, 0.0)
        if k >= 10:
            part = part * share
        part = part[:, :128] + part[:, 128:]
        total = jnp.sum(jnp.sum(part, axis=0, keepdims=True), axis=1, keepdims=True)
        packed = jnp.where(lane == k, total, packed)
    for k in range(m_out.shape[0]):
        m_out[k] = packed


def final_kernel(m_ref, low_ref, high_ref, w_ref, open_ref, dy_ref, out_ref, q_ref):
    lanes = 256
    parts = [m_ref[k] for k in range(m_ref.shape[0])]
    while len(parts) > 1:
        odd = parts[len(parts) // 2 * 2 :]
        parts = [parts[k] + parts[k + 1] for k in range(0, len(parts) - 1, 2)] + odd
    sums = parts[0]
    lane = iota(128, 1)

    def moment(k):
        return jnp.sum(jnp.where(lane == k, sums, 0.0), axis=1, keepdims=True)

    e = {}
    slot = 0
    for j in range(ROUNDS):
        for i in range(j + 1):
            e[j, i] = moment(slot)
            slot += 1
    g = [moment(10 + j) for j in range(ROUNDS)]
    low, diag, scaled = {}, [], {}
    for j in range(ROUNDS):
        d = e[j, j]
        for k in range(j):
            d = d - low[j, k] * scaled[j, k]
        diag.append(d)
        for i in range(j + 1, ROUNDS):
            t = e[i, j]
            for k in range(j):
                t = t - scaled[i, k] * low[j, k]
            scaled[i, j] = t
            low[i, j] = t / d
    y = []
    for j in range(ROUNDS):
        t = g[j]
        for k in range(j):
            t = t - low[j, k] * y[k]
        y.append(t)
    c = [None] * ROUNDS
    for j in reversed(range(ROUNDS)):
        t = y[j] / diag[j]
        for k in range(j + 1, ROUNDS):
            t = t - low[k, j] * c[k]
        c[j] = t
    coef = [jnp.broadcast_to(t * (1.0 / span), (8, lanes)) for t in c]

    dcoef = row_coefs(lanes, deriv)
    first_x, last_x, first_y, last_y = flags(lanes)
    mean_x = node_x(lanes, 1.0 / copies)
    mean_y = node_y(lanes, 1.0 / copies)
    q, slope = [], []
    for e in range(4):
        got = low_ref[0, :, 3 + e] * coef[0] + low_ref[1, :, 3 + e] * coef[1]
        got = got + high_ref[0, :, e] * coef[2] + high_ref[1, :, e] * coef[3]
        q.append(got)
        slope.append(weigh(row_turns(got), dcoef))
    for e in range(2):
        here = q[e + 1]
        q_own = own_lanes(here)
        q_ref[:, e] = q_own
        along_x = sum_rows(slope[e], slope[e + 1], slope[e + 2], first_x, last_x) * mean_x
        along_y = sum_lanes(lanes_times(here, dy_ref[...]), first_y, last_y) * mean_y
        parts = [own_lanes(along_x), own_lanes(along_y), z_slope(q_own)]
        for i in range(3):
            for z in range(8):
                got = w_ref[i, z, e] - parts[i][z]
                if z in (0, 7):
                    got = got * open_ref[z // 7, e]
                out_ref[i, z, e] = got


def shape(*dims):
    return jax.ShapeDtypeStruct(dims, f32)


def call(kernel, out_shape, scratch, *args, space=pltpu.VMEM, vmem=48, cost=None):
    return pl.pallas_call(
        kernel,
        out_shape=out_shape,
        in_specs=[pl.BlockSpec(memory_space=space)] * len(args),
        out_specs=jax.tree.map(lambda s: pl.BlockSpec(memory_space=pltpu.VMEM), out_shape),
        scratch_shapes=scratch,
        cost_estimate=cost,
        compiler_params=pltpu.CompilerParams(vmem_limit_bytes=vmem * 2**20),
    )(*args)


def shift(value, axis, by):
    size = lax.axis_size(axis)
    return lax.ppermute(value, axis, [(i, (i + by) % size) for i in range(size)])


def total_rows(packed):
    nx, ny = lax.axis_size("gx"), lax.axis_size("gy")
    along = [[2 * z + c for z in range(nx // 2)] for c in range(2)]
    part = lax.all_to_all(packed, "gx", 0, 0, axis_index_groups=along, tiled=True)
    part = jnp.broadcast_to(jnp.sum(part, axis=0, keepdims=True), (ny, 8, 128))
    part = lax.all_to_all(part, "gy", 0, 0, tiled=True)
    pairs = [[i, i + 1] for i in range(0, nx, 2)]
    return lax.all_gather(part, "gx", axis_index_groups=pairs, tiled=True)


def local(adjoint, checkpoints, wall_faces):
    adj = adjoint.reshape(3, 8, 2, 8, 128)
    flow = checkpoints.reshape(3, 8, 16, 128)
    vm = pltpu.VMEM
    table = jax.ShapeDtypeStruct((256, 256), bf16)
    strip = shape(3, 4, 2, 8, 128)
    rhs, up, down = call(
        rhs_kernel,
        (shape(3, 8, 2, 8, 128), strip, strip),
        [
            vm((3, 8, 2, 8, 128), f32),
            vm((3, 8, 16, 128), bf16),
            vm((2, 2, 16), jnp.int32),
            vm((3, 8, 2, 8, 128), f32),
            vm((2, 2, 8, 128), f32),
            vm((256, 256), bf16),
            vm((256, 256), bf16),
            pltpu.SemaphoreType.DMA((3,)),
        ],
        adj, flow, wall_faces,
        space=pl.ANY,
        vmem=62,
    )
    left = shift(up, "gy", 1)
    right = shift(down, "gy", -1)
    packet = shape(10, 8, 256)
    cost = pl.CostEstimate(flops=10**6, bytes_accessed=4 * 10**5, transcendentals=0)
    turned, dy, ky = call(
        hold_kernel, (shape(3, 8, 2, 8, 128), table, table), [], rhs, cost=cost
    )
    wide, up, down = call(
        join_kernel, (shape(3, 8, 2, 8, 256), packet, packet), [], turned, left, right
    )
    before = shift(up, "gx", 1)
    after = shift(down, "gx", -1)
    source, moved, opened = call(
        source_kernel,
        (shape(8, 2, 8, 256), shape(3, 8, 2, 8, 128), shape(2, 2, 8, 128)),
        [vm((8, 2, 8, 256), f32)],
        before, wide, after, dy,
    )
    left = shift(source, "gx", 1)
    right = shift(source, "gx", -1)
    left2 = shift(left, "gx", 1)
    right2 = shift(right, "gx", -1)
    cost = pl.CostEstimate(flops=5 * 10**6, bytes_accessed=4 * 10**6, transcendentals=0)
    low, images, acc = call(
        inner_kernel,
        (shape(3, 8, 10, 8, 256), shape(3, 8, 10, 8, 256), shape(9, 8, 256)),
        [vm((2, 10, 8, 256), f32)],
        left, source, right, ky,
        cost=cost,
    )
    high, packed = call(
        outer_kernel,
        (shape(2, 8, 4, 8, 256), shape(lax.axis_size("gx") // 2, 8, 128)),
        [
            vm((4, 8, 10, 8, 256), f32),
            vm((4, 8, 10, 8, 256), f32),
            vm((2, 10, 8, 256), f32),
        ],
        left2, left, source, right, right2, low, images, acc, ky,
    )
    velocity, pressure = call(
        final_kernel,
        (shape(3, 8, 2, 8, 128), shape(8, 2, 8, 128)),
        [],
        total_rows(packed), low, high, moved, opened, dy,
    )
    return velocity.reshape(3, 8, 16, 128), pressure.reshape(8, 16, 128)


def solution(mesh):
    return jax.shard_map(
        local,
        mesh=mesh,
        in_specs=(P(None, None, "gx", "gy"), P(None, None, None, "gx", "gy"), P(None, "gx", "gy")),
        out_specs=(P(None, None, "gx", "gy"), P(None, "gx", "gy")),
        check_vma=False,
    )
```

```python
import jax
import jax.numpy as jnp
import numpy as np
from jax import lax
from jax.experimental import pallas as pl
from jax.experimental.pallas import tpu as pltpu
from jax.sharding import PartitionSpec as P

f32 = jnp.float32
bf16 = jnp.bfloat16

node_points = np.array(
    [
        -1.0,
        -0.8717401485096066,
        -0.5917001814331423,
        -0.2092992179024789,
        0.2092992179024789,
        0.5917001814331423,
        0.8717401485096066,
        1.0,
    ]
)
node_weights = np.array(
    [
        0.03571428571428571,
        0.2107042271435061,
        0.3411226924835044,
        0.4124587946587038,
        0.4124587946587038,
        0.3411226924835044,
        0.2107042271435061,
        0.03571428571428571,
    ]
)
time_step = 0.05
viscosity = 0.02
span = 8.0
ROUNDS = 4


def derivative_table(points):
    identity = np.eye(points.shape[0])
    spacing = points[:, None] - points[None, :] + identity
    barycentric = 1.0 / np.prod(spacing, axis=1)
    matrix = barycentric[None, :] / barycentric[:, None] / spacing
    matrix = matrix * (1.0 - identity)
    return matrix - identity * np.sum(matrix, axis=1)[:, None]


deriv = derivative_table(node_points)
stiff = deriv.T @ np.diag(node_weights) @ deriv
copies = np.array([2.0, 1, 1, 1, 1, 1, 1, 2.0])
inverse_mass = 1.0 / (copies * node_weights)


scaled_stiff = stiff / node_weights[:, None]


def iota(lanes, dim):
    return lax.broadcasted_iota(jnp.int32, (8, lanes), dim)


def pick(place, values):
    out = jnp.full(place.shape, float(values[0]), f32)
    for k in range(1, 8):
        out = jnp.where(place == k, float(values[k]), out)
    return out


def node_x(lanes, values):
    return pick(iota(lanes, 0), values)


def node_y(lanes, values):
    return pick(iota(lanes, 1) & 7, values)


def rim_mask(lanes):
    a = iota(lanes, 0)
    b = iota(lanes, 1) & 7
    return (a == 0) | (a == 7) | (b == 0) | (b == 7)


def row_coefs(lanes, matrix):
    return [node_x(lanes, [matrix[a, (a - r) % 8] for a in range(8)]) for r in range(8)]


def row_turns(value):
    return [value] + [pltpu.roll(value, r, axis=1) for r in range(1, 8)]


def weigh(turns, coefs):
    out = turns[0] * coefs[0]
    for r in range(1, 8):
        out = out + turns[r] * coefs[r]
    return out


def depth(planes, matrix, sign):
    plus = [planes[k] + planes[7 - k] for k in range(4)]
    minus = [planes[k] - planes[7 - k] for k in range(4)]
    out = [None] * 8
    for a in range(4):
        even = plus[0] * float(0.5 * (matrix[a, 0] + matrix[a, 7]))
        odd = minus[0] * float(0.5 * (matrix[a, 0] - matrix[a, 7]))
        for k in range(1, 4):
            even = even + plus[k] * float(0.5 * (matrix[a, k] + matrix[a, 7 - k]))
            odd = odd + minus[k] * float(0.5 * (matrix[a, k] - matrix[a, 7 - k]))
        out[a] = even + odd
        out[7 - a] = even - odd if sign > 0 else odd - even
    return out


def z_slope(value):
    return jnp.stack(depth([value[z] for z in range(8)], deriv, -1))


def lane_table(matrix):
    lane = iota(128, 1)
    pattern = jnp.zeros((8, 128), f32)
    for b in range(8):
        pattern = jnp.where((lane & 7) == b, node_x(128, matrix[b]), pattern)
    full = jnp.concatenate([jnp.where(lane // 8 == k, pattern, 0.0) for k in range(16)], axis=0)
    high = full.astype(bf16)
    low = (full - high.astype(f32)).astype(bf16)
    pair = jnp.concatenate([high, low], axis=1)
    return jnp.concatenate([pair, pair], axis=0)


def lanes_times(value, table):
    n, _, lanes = value.shape
    blocks = [value[:, :, k * 128 : (k + 1) * 128].reshape(n * 8, 128) for k in range(lanes // 128)]
    rows = blocks[0] if len(blocks) == 1 else jnp.concatenate(blocks, axis=0)
    high = rows.astype(bf16)
    low = (rows - high.astype(f32)).astype(bf16)
    both = jnp.concatenate([high, low], axis=1)
    got = jnp.dot(both, table, preferred_element_type=f32)
    got = got[:, :128] + got[:, 128:]
    parts = [got[k * n * 8 : (k + 1) * n * 8].reshape(n, 8, 128) for k in range(lanes // 128)]
    return parts[0] if len(parts) == 1 else jnp.concatenate(parts, axis=2)


def sum_lanes(value, first, last):
    lanes = value.shape[2]
    return (
        value
        + last * pltpu.roll(value, lanes - 1, axis=2)
        + first * pltpu.roll(value, 1, axis=2)
    )


def sum_rows(before, here, after, first, last):
    return here + last * pltpu.roll(after, 7, axis=1) + first * pltpu.roll(before, 1, axis=1)


def own_lanes(value):
    n = value.shape[0]
    lane = lax.broadcasted_iota(jnp.int32, (n, 8, 128), 2)
    mixed = jnp.where(lane >= 64, value[:, :, :128], value[:, :, 128:])
    return pltpu.roll(mixed, 64, axis=2)


def expand_walls(faces_ref):
    spread = (
        lax.broadcasted_iota(jnp.int32, (16, 128), 1) // 8
        == lax.broadcasted_iota(jnp.int32, (16, 128), 0)
    ).astype(f32)
    out = []
    for face in range(2):
        rows = faces_ref[face].astype(f32)
        wide = jnp.dot(rows, spread, preferred_element_type=f32)
        out.append(wide)
    return out


def rhs_kernel(
    adj_hbm, flow_hbm, faces_hbm,
    r_ref, up_ref, down_ref,
    adj_ref, flow_ref, faces_ref, u_ref, wall_ref, dy_ref, ky_ref, sems,
):
    moves = [
        pltpu.make_async_copy(src, dst, sems.at[k])
        for k, (src, dst) in enumerate(
            ((adj_hbm, adj_ref), (flow_hbm, flow_ref), (faces_hbm, faces_ref))
        )
    ]
    for move in moves:
        move.start()
    lanes = 128
    dy_ref[...] = lane_table(deriv)
    ky_ref[...] = lane_table(scaled_stiff)
    dcoef = row_coefs(lanes, deriv)
    kcoef = row_coefs(lanes, scaled_stiff)
    wxy = node_x(lanes, node_weights) * node_y(lanes, node_weights)
    rim = rim_mask(lanes)
    half = iota(lanes, 1) < 64
    for move in moves:
        move.wait()
    for face, wide in enumerate(expand_walls(faces_ref)):
        for e in range(2):
            wall_ref[face, e] = jnp.broadcast_to(wide[e : e + 1], (8, lanes))
    for c in range(3):
        for z in range(8):
            rows = flow_ref[c, z].astype(f32)
            u_ref[c, z, 0] = rows[:8]
            u_ref[c, z, 1] = rows[8:]

    def body(e, carry):
        v = [adj_ref[c, :, e] for c in range(3)]
        u = [u_ref[c, :, e] for c in range(3)]
        vall = jnp.concatenate(v, axis=0)
        uall = jnp.concatenate(u, axis=0)
        vdy = lanes_times(vall, dy_ref[...])
        vky = lanes_times(vall, ky_ref[...])
        udy = lanes_times(uall, dy_ref[...])
        stretch = [jnp.zeros((8, 8, lanes), f32)] * 3
        for j in range(3):
            stretch[0] = stretch[0] + v[j] * weigh(row_turns(u[j]), dcoef)
            stretch[1] = stretch[1] + v[j] * udy[8 * j : 8 * j + 8]
            stretch[2] = stretch[2] + v[j] * z_slope(u[j])
        for i in range(3):
            turns = row_turns(v[i])
            planes = [v[i][z] for z in range(8)]
            zd = depth(planes, deriv, -1)
            zk = depth(planes, scaled_stiff, 1)
            xd = weigh(turns, dcoef)
            xk = weigh(turns, kcoef)
            made = []
            for z in range(8):
                wz = float(node_weights[z])
                adv = (
                    u[0][z] * xd[z]
                    + u[1][z] * vdy[8 * i + z]
                    + u[2][z] * zd[z]
                    - stretch[i][z]
                )
                bend = xk[z] + vky[8 * i + z] + zk[z]
                out = (wxy * wz) * (v[i][z] + time_step * adv - (time_step * viscosity) * bend)
                if i == 0 and z in (0, 7):
                    out = jnp.where(rim, wall_ref[z // 7, e], out)
                r_ref[i, z, e] = out
                made.append(out)
            for z in range(4):
                up_ref[i, z, e] = jnp.where(half, pltpu.roll(made[z], 64, axis=1), made[z + 4])
                down_ref[i, z, e] = jnp.where(half, made[z], pltpu.roll(made[z + 4], 64, axis=1))
        return carry

    lax.fori_loop(0, 2, body, 0)


def hold_kernel(r_ref, turned_ref, dy_ref, ky_ref):
    dy_ref[...] = lane_table(deriv)
    ky_ref[...] = lane_table(scaled_stiff)
    for c in range(3):
        for z in range(8):
            for e in range(2):
                turned_ref[c, z, e] = pltpu.roll(r_ref[c, z, e], 64, axis=1)


def join_kernel(r_ref, left_ref, right_ref, e_ref, up_ref, down_ref):
    half = iota(128, 1) < 64
    place = iota(256, 0)
    first = place == 0
    last = place == 7
    for c in range(3):
        faces_up = jnp.zeros((8, 256), f32)
        faces_down = jnp.zeros((8, 256), f32)
        for z in range(8):
            tiles = []
            for e in range(2):
                turned = r_ref[c, z, e]
                left = left_ref[c, z % 4, e]
                right = right_ref[c, z % 4, e]
                if z >= 4:
                    left = pltpu.roll(left, 64, axis=1)
                else:
                    right = pltpu.roll(right, 64, axis=1)
                tile = jnp.concatenate(
                    [jnp.where(half, left, turned), jnp.where(half, turned, right)], axis=1
                )
                e_ref[c, z, e] = tile
                tiles.append(tile)
            if c == 0:
                go_up, go_down = tiles[1], tiles[0]
                if 0 < z < 7:
                    go_up = go_up + jnp.where(first, pltpu.roll(tiles[0], 1, axis=0), 0.0)
                    go_down = go_down + jnp.where(last, pltpu.roll(tiles[1], 7, axis=0), 0.0)
                up_ref[z] = go_up
                down_ref[z] = go_down
            else:
                turned = pltpu.roll(tiles[1], (z + 1) % 8, axis=0) if z < 7 else tiles[1]
                faces_up = jnp.where(place == z, turned, faces_up)
                turned = pltpu.roll(tiles[0], z, axis=0) if z else tiles[0]
                faces_down = jnp.where(place == z, turned, faces_down)
        if c:
            up_ref[7 + c] = faces_up
            down_ref[7 + c] = faces_down


def flags(lanes):
    first_x = (iota(lanes, 0) == 0).astype(f32)
    last_x = (iota(lanes, 0) == 7).astype(f32)
    first_y = ((iota(lanes, 1) & 7) == 0).astype(f32)
    last_y = ((iota(lanes, 1) & 7) == 7).astype(f32)
    return first_x, last_x, first_y, last_y


def source_kernel(left_ref, mid_ref, right_ref, dy_ref, b_ref, w_ref, open_ref, t_ref):
    lanes = 256
    dcoef = row_coefs(lanes, deriv)
    wx = node_x(lanes, node_weights)
    wy = node_y(lanes, node_weights)
    mx = node_x(lanes, copies)
    my = node_y(lanes, copies)
    inv = node_x(lanes, inverse_mass) * node_y(lanes, inverse_mass)
    first_x, last_x, first_y, last_y = flags(lanes)
    inside = 1.0 - rim_mask(lanes).astype(f32)

    def wall(tile):
        return jnp.broadcast_to(tile[0:1, :], (8, lanes))

    def finish(rows, faces):
        total = sum_lanes(rows, first_y, last_y)
        planes = []
        for z in range(8):
            got = total[z] * (inv * float(1.0 / node_weights[z]))
            if z in (0, 7):
                got = got * (inside * (1.0 - wall(faces[z])))
            planes.append(got)
        return jnp.stack(planes)

    def turn(tile, by):
        by = by % 8
        return pltpu.roll(tile, by, axis=0) if by else tile

    slope = {}
    left = left_ref[0:8]
    right = right_ref[0:8]
    near = finish(left + last_x * pltpu.roll(mid_ref[0, :, 0], 7, axis=1), left)
    slope[-1] = weigh(row_turns(near), dcoef)
    near = finish(right + first_x * pltpu.roll(mid_ref[0, :, 1], 1, axis=1), right)
    slope[2] = weigh(row_turns(near), dcoef)
    for e in range(2):
        faces = mid_ref[0, :, e]
        for face in range(2):
            open_face = inside * (1.0 - wall(faces[7 * face]))
            open_ref[face, e] = own_lanes(open_face[None])[0]
        w = []
        for c in range(3):
            if c == 0:
                before, after = left, right
            else:
                before = jnp.stack([turn(left_ref[7 + c], 7 - z) for z in range(8)])
                after = jnp.stack([turn(right_ref[7 + c], 8 - z) for z in range(8)])
            if e == 0:
                rows = sum_rows(before, mid_ref[c, :, 0], mid_ref[c, :, 1], first_x, last_x)
            else:
                rows = sum_rows(mid_ref[c, :, 0], mid_ref[c, :, 1], after, first_x, last_x)
            got = finish(rows, faces)
            w.append(got)
            w_ref[c, :, e] = own_lanes(got)
        slope[e] = weigh(row_turns(w[0]), dcoef)
        along = sum_lanes(lanes_times(w[1], dy_ref[...]) * wy, first_y, last_y) * (mx * wx)
        t_ref[:, e] = along + z_slope(w[2]) * (mx * wx * my * wy)
    for e in range(2):
        faces = mid_ref[0, :, e]
        rows = sum_rows(slope[e - 1], slope[e], slope[e + 1], first_x, last_x)
        total = rows * (wx * my * wy) + t_ref[:, e]
        for z in range(8):
            got = total[z] * float(-node_weights[z])
            if z in (0, 7):
                face = wall(faces[z])
                got = jnp.where(inside > 0.5, got * face, face)
            b_ref[z, e] = got


def fold(value):
    total = value[0]
    for z in range(1, 8):
        total = total + value[z]
    return total


def load_block(ref, at, v_ref, p_ref, rim, fill):
    for e in range(2):
        for z in range(8):
            got = ref[z, e]
            if z in (0, 7):
                face = jnp.broadcast_to(got[0:1, :], got.shape)
                p_ref[z // 7, at + e] = jnp.where(rim, 0.0, face)
                got = jnp.where(rim, 0.0, got)
            if fill:
                v_ref[0, z, at + e] = got


def krylov_tools(ky_ref, v_ref, k_ref, p_ref):
    lanes = 256
    kcoef = row_coefs(lanes, scaled_stiff)
    wxy = node_x(lanes, node_weights) * node_y(lanes, node_weights)
    first_x, last_x, first_y, last_y = flags(lanes)

    def apply(j, e):
        v = v_ref[j, :, e]
        yk = lanes_times(v, ky_ref[...])
        xk = weigh(row_turns(v), kcoef)
        zk = depth([v[z] for z in range(8)], scaled_stiff, 1)
        for z in range(8):
            k_ref[j, z, e] = (xk[z] + zk[z] + yk[z]) * (wxy * float(node_weights[z] / span))

    def step(j, e):
        rows = sum_rows(
            k_ref[j, :, e - 1], k_ref[j, :, e], k_ref[j, :, e + 1], first_x, last_x
        )
        total = sum_lanes(rows, first_y, last_y)
        for z in range(8):
            image = total[z]
            if z in (0, 7):
                image = image * p_ref[z // 7, e]
            v_ref[j + 1, z, e] = image - 0.5 * v_ref[j, z, e]

    return apply, step


def over(low, high, body):
    lax.fori_loop(low, high, lambda e, c: (body(e), c)[1], 0, unroll=2)


def sides(low, body):
    over(0, 4, lambda t: body(low + t + (t // 2) * (6 - 2 * low)))


def inner_kernel(left_ref, mid_ref, right_ref, ky_ref, v_ref, k_ref, acc_ref, p_ref):
    rim = rim_mask(256)
    for at, ref in ((2, left_ref), (4, mid_ref), (6, right_ref)):
        load_block(ref, at, v_ref, p_ref, rim, True)
    apply, step = krylov_tools(ky_ref, v_ref, k_ref, p_ref)
    slot = 0
    for j in range(3):
        over(2 + j, 8 - j, lambda e, j=j: apply(j, e))
        for i in range(j + 1):
            acc_ref[slot + i] = fold(v_ref[i, :, 4] * k_ref[j, :, 4]) + fold(
                v_ref[i, :, 5] * k_ref[j, :, 5]
            )
        acc_ref[6 + j] = fold(v_ref[j, :, 4] * v_ref[0, :, 4]) + fold(
            v_ref[j, :, 5] * v_ref[0, :, 5]
        )
        slot += j + 1
        if j < 2:
            over(3 + j, 7 - j, lambda e, j=j: step(j, e))


def outer_kernel(*refs):
    blocks = refs[:5]
    v_in, k_in, acc_ref, ky_ref, v_out, m_out, v_ref, k_ref, p_ref = refs[5:]
    lanes = 256
    rim = rim_mask(lanes)
    for k, ref in enumerate(blocks):
        load_block(ref, 2 * k, v_ref, p_ref, rim, k in (0, 4))
    for j, els in ((0, (2, 3, 4, 5, 6, 7)), (1, (3, 4, 5, 6)), (2, (4, 5))):
        for e in els:
            v_ref[j, :, e] = v_in[j, :, e]
            if j or e not in (4, 5):
                k_ref[j, :, e] = k_in[j, :, e]
    apply, step = krylov_tools(ky_ref, v_ref, k_ref, p_ref)
    for j in range(3):
        sides(j, lambda e, j=j: apply(j, e))
        if j < 2:
            sides(j + 1, lambda e, j=j: step(j, e))
        else:
            over(3, 7, lambda e: step(2, e))
    over(4, 6, lambda e: apply(3, e))
    for e in range(4):
        v_out[0, :, e] = v_ref[2, :, 3 + e]
        v_out[1, :, e] = v_ref[3, :, 3 + e]
    energy = [acc_ref[k] for k in range(6)]
    for i in range(ROUNDS):
        energy.append(
            fold(v_ref[i, :, 4] * k_ref[3, :, 4]) + fold(v_ref[i, :, 5] * k_ref[3, :, 5])
        )
    load = [acc_ref[6 + k] for k in range(3)]
    load.append(
        fold(v_ref[3, :, 4] * v_ref[0, :, 4]) + fold(v_ref[3, :, 5] * v_ref[0, :, 5])
    )
    lane = iota(lanes, 1)
    own = (lane >= 64) & (lane < 192)
    share = node_x(lanes, 1.0 / copies) * node_y(lanes, 1.0 / copies)
    lane = iota(128, 1)
    packed = jnp.zeros((8, 128), f32)
    for k, part in enumerate(energy + load):
        part = jnp.where(own, part, 0.0)
        if k >= 10:
            part = part * share
        part = part[:, :128] + part[:, 128:]
        total = jnp.sum(jnp.sum(part, axis=0, keepdims=True), axis=1, keepdims=True)
        packed = jnp.where(lane == k, total, packed)
    for k in range(m_out.shape[0]):
        m_out[k] = packed


def final_kernel(m_ref, low_ref, high_ref, w_ref, open_ref, dy_ref, out_ref, q_ref):
    lanes = 256
    parts = [m_ref[k] for k in range(m_ref.shape[0])]
    while len(parts) > 1:
        odd = parts[len(parts) // 2 * 2 :]
        parts = [parts[k] + parts[k + 1] for k in range(0, len(parts) - 1, 2)] + odd
    sums = parts[0]
    lane = iota(128, 1)

    def moment(k):
        return jnp.sum(jnp.where(lane == k, sums, 0.0), axis=1, keepdims=True)

    e = {}
    slot = 0
    for j in range(ROUNDS):
        for i in range(j + 1):
            e[j, i] = moment(slot)
            slot += 1
    g = [moment(10 + j) for j in range(ROUNDS)]
    low, diag, scaled = {}, [], {}
    for j in range(ROUNDS):
        d = e[j, j]
        for k in range(j):
            d = d - low[j, k] * scaled[j, k]
        diag.append(d)
        for i in range(j + 1, ROUNDS):
            t = e[i, j]
            for k in range(j):
                t = t - scaled[i, k] * low[j, k]
            scaled[i, j] = t
            low[i, j] = t / d
    y = []
    for j in range(ROUNDS):
        t = g[j]
        for k in range(j):
            t = t - low[j, k] * y[k]
        y.append(t)
    c = [None] * ROUNDS
    for j in reversed(range(ROUNDS)):
        t = y[j] / diag[j]
        for k in range(j + 1, ROUNDS):
            t = t - low[k, j] * c[k]
        c[j] = t
    coef = [jnp.broadcast_to(t * (1.0 / span), (8, lanes)) for t in c]

    dcoef = row_coefs(lanes, deriv)
    first_x, last_x, first_y, last_y = flags(lanes)
    mean_x = node_x(lanes, 1.0 / copies)
    mean_y = node_y(lanes, 1.0 / copies)
    q, slope = [], []
    for e in range(4):
        got = low_ref[0, :, 3 + e] * coef[0] + low_ref[1, :, 3 + e] * coef[1]
        got = got + high_ref[0, :, e] * coef[2] + high_ref[1, :, e] * coef[3]
        q.append(got)
        slope.append(weigh(row_turns(got), dcoef))
    for e in range(2):
        here = q[e + 1]
        q_own = own_lanes(here)
        q_ref[:, e] = q_own
        along_x = sum_rows(slope[e], slope[e + 1], slope[e + 2], first_x, last_x) * mean_x
        along_y = sum_lanes(lanes_times(here, dy_ref[...]), first_y, last_y) * mean_y
        parts = [own_lanes(along_x), own_lanes(along_y), z_slope(q_own)]
        for i in range(3):
            for z in range(8):
                got = w_ref[i, z, e] - parts[i][z]
                if z in (0, 7):
                    got = got * open_ref[z // 7, e]
                out_ref[i, z, e] = got


def shape(*dims):
    return jax.ShapeDtypeStruct(dims, f32)


def call(kernel, out_shape, scratch, *args, space=pltpu.VMEM, vmem=48, cost=None):
    return pl.pallas_call(
        kernel,
        out_shape=out_shape,
        in_specs=[pl.BlockSpec(memory_space=space)] * len(args),
        out_specs=jax.tree.map(lambda s: pl.BlockSpec(memory_space=pltpu.VMEM), out_shape),
        scratch_shapes=scratch,
        cost_estimate=cost,
        compiler_params=pltpu.CompilerParams(vmem_limit_bytes=int(vmem * 2**20)),
    )(*args)


def shift(value, axis, by):
    size = lax.axis_size(axis)
    return lax.ppermute(value, axis, [(i, (i + by) % size) for i in range(size)])


def total_rows(packed):
    nx, ny = lax.axis_size("gx"), lax.axis_size("gy")
    planes = [[(2 * z + c) * ny + y for y in range(ny) for c in range(2)] for z in range(nx // 2)]
    part = lax.all_to_all(packed, ("gx", "gy"), 0, 0, axis_index_groups=planes, tiled=True)
    part = jnp.broadcast_to(jnp.sum(part, axis=0, keepdims=True), (nx // 2, 8, 128))
    along = [[2 * z + c for z in range(nx // 2)] for c in range(2)]
    return lax.all_to_all(part, "gx", 0, 0, axis_index_groups=along, tiled=True)


def local(adjoint, checkpoints, wall_faces):
    adj = adjoint.reshape(3, 8, 2, 8, 128)
    flow = checkpoints.reshape(3, 8, 16, 128)
    vm = pltpu.VMEM
    table = jax.ShapeDtypeStruct((256, 256), bf16)
    strip = shape(3, 4, 2, 8, 128)
    rhs, up, down = call(
        rhs_kernel,
        (shape(3, 8, 2, 8, 128), strip, strip),
        [
            vm((3, 8, 2, 8, 128), f32),
            vm((3, 8, 16, 128), bf16),
            vm((2, 2, 16), jnp.int32),
            vm((3, 8, 2, 8, 128), f32),
            vm((2, 2, 8, 128), f32),
            vm((256, 256), bf16),
            vm((256, 256), bf16),
            pltpu.SemaphoreType.DMA((3,)),
        ],
        adj, flow, wall_faces,
        space=pl.ANY,
        vmem=62,
    )
    left = shift(up, "gy", 1)
    right = shift(down, "gy", -1)
    packet = shape(10, 8, 256)
    cost = pl.CostEstimate(flops=10**6, bytes_accessed=4 * 10**5, transcendentals=0)
    turned, dy, ky = call(
        hold_kernel, (shape(3, 8, 2, 8, 128), table, table), [], rhs, cost=cost
    )
    wide, up, down = call(
        join_kernel, (shape(3, 8, 2, 8, 256), packet, packet), [], turned, left, right
    )
    before = shift(up, "gx", 1)
    after = shift(down, "gx", -1)
    source, moved, opened = call(
        source_kernel,
        (shape(8, 2, 8, 256), shape(3, 8, 2, 8, 128), shape(2, 2, 8, 128)),
        [vm((8, 2, 8, 256), f32)],
        before, wide, after, dy,
    )
    left = shift(source, "gx", 1)
    right = shift(source, "gx", -1)
    left2 = shift(left, "gx", 1)
    right2 = shift(right, "gx", -1)
    cost = pl.CostEstimate(flops=5 * 10**6, bytes_accessed=4 * 10**6, transcendentals=0)
    low, images, acc = call(
        inner_kernel,
        (shape(3, 8, 10, 8, 256), shape(3, 8, 10, 8, 256), shape(9, 8, 256)),
        [vm((2, 10, 8, 256), f32)],
        left, source, right, ky,
        cost=cost,
    )
    high, packed = call(
        outer_kernel,
        (shape(2, 8, 4, 8, 256), shape(2 * lax.axis_size("gy"), 8, 128)),
        [
            vm((4, 8, 10, 8, 256), f32),
            vm((4, 8, 10, 8, 256), f32),
            vm((2, 10, 8, 256), f32),
        ],
        left2, left, source, right, right2, low, images, acc, ky,
    )
    velocity, pressure = call(
        final_kernel,
        (shape(3, 8, 2, 8, 128), shape(8, 2, 8, 128)),
        [],
        total_rows(packed), low, high, moved, opened, dy,
    )
    return velocity.reshape(3, 8, 16, 128), pressure.reshape(8, 16, 128)


def solution(mesh):
    return jax.shard_map(
        local,
        mesh=mesh,
        in_specs=(P(None, None, "gx", "gy"), P(None, None, None, "gx", "gy"), P(None, "gx", "gy")),
        out_specs=(P(None, None, "gx", "gy"), P(None, "gx", "gy")),
        check_vma=False,
    )
```

```python
import jax
import jax.numpy as jnp
import numpy as np
from jax import lax
from jax.experimental import pallas as pl
from jax.experimental.pallas import tpu as pltpu
from jax.sharding import PartitionSpec as P

f32 = jnp.float32
bf16 = jnp.bfloat16

node_points = np.array(
    [
        -1.0,
        -0.8717401485096066,
        -0.5917001814331423,
        -0.2092992179024789,
        0.2092992179024789,
        0.5917001814331423,
        0.8717401485096066,
        1.0,
    ]
)
node_weights = np.array(
    [
        0.03571428571428571,
        0.2107042271435061,
        0.3411226924835044,
        0.4124587946587038,
        0.4124587946587038,
        0.3411226924835044,
        0.2107042271435061,
        0.03571428571428571,
    ]
)
time_step = 0.05
viscosity = 0.02
span = 8.0
ROUNDS = 4


def derivative_table(points):
    identity = np.eye(points.shape[0])
    spacing = points[:, None] - points[None, :] + identity
    barycentric = 1.0 / np.prod(spacing, axis=1)
    matrix = barycentric[None, :] / barycentric[:, None] / spacing
    matrix = matrix * (1.0 - identity)
    return matrix - identity * np.sum(matrix, axis=1)[:, None]


deriv = derivative_table(node_points)
stiff = deriv.T @ np.diag(node_weights) @ deriv
copies = np.array([2.0, 1, 1, 1, 1, 1, 1, 2.0])
inverse_mass = 1.0 / (copies * node_weights)


scaled_stiff = stiff / node_weights[:, None]


def iota(lanes, dim):
    return lax.broadcasted_iota(jnp.int32, (8, lanes), dim)


def pick(place, values):
    out = jnp.full(place.shape, float(values[0]), f32)
    for k in range(1, 8):
        out = jnp.where(place == k, float(values[k]), out)
    return out


def node_x(lanes, values):
    return pick(iota(lanes, 0), values)


def node_y(lanes, values):
    return pick(iota(lanes, 1) & 7, values)


def rim_mask(lanes):
    a = iota(lanes, 0)
    b = iota(lanes, 1) & 7
    return (a == 0) | (a == 7) | (b == 0) | (b == 7)


def row_coefs(lanes, matrix):
    return [node_x(lanes, [matrix[a, (a - r) % 8] for a in range(8)]) for r in range(8)]


def row_turns(value):
    return [value] + [pltpu.roll(value, r, axis=1) for r in range(1, 8)]


def weigh(turns, coefs):
    out = turns[0] * coefs[0]
    for r in range(1, 8):
        out = out + turns[r] * coefs[r]
    return out


def depth(planes, matrix, sign):
    plus = [planes[k] + planes[7 - k] for k in range(4)]
    minus = [planes[k] - planes[7 - k] for k in range(4)]
    out = [None] * 8
    for a in range(4):
        even = plus[0] * float(0.5 * (matrix[a, 0] + matrix[a, 7]))
        odd = minus[0] * float(0.5 * (matrix[a, 0] - matrix[a, 7]))
        for k in range(1, 4):
            even = even + plus[k] * float(0.5 * (matrix[a, k] + matrix[a, 7 - k]))
            odd = odd + minus[k] * float(0.5 * (matrix[a, k] - matrix[a, 7 - k]))
        out[a] = even + odd
        out[7 - a] = even - odd if sign > 0 else odd - even
    return out


def z_slope(value):
    return jnp.stack(depth([value[z] for z in range(8)], deriv, -1))


def lane_table(matrix):
    lane = iota(128, 1)
    pattern = jnp.zeros((8, 128), f32)
    for b in range(8):
        pattern = jnp.where((lane & 7) == b, node_x(128, matrix[b]), pattern)
    full = jnp.concatenate([jnp.where(lane // 8 == k, pattern, 0.0) for k in range(16)], axis=0)
    high = full.astype(bf16)
    low = (full - high.astype(f32)).astype(bf16)
    pair = jnp.concatenate([high, low], axis=1)
    return jnp.concatenate([pair, pair], axis=0)


def lanes_times(value, table):
    n, _, lanes = value.shape
    blocks = [value[:, :, k * 128 : (k + 1) * 128].reshape(n * 8, 128) for k in range(lanes // 128)]
    rows = blocks[0] if len(blocks) == 1 else jnp.concatenate(blocks, axis=0)
    high = rows.astype(bf16)
    low = (rows - high.astype(f32)).astype(bf16)
    both = jnp.concatenate([high, low], axis=1)
    got = jnp.dot(both, table, preferred_element_type=f32)
    got = got[:, :128] + got[:, 128:]
    parts = [got[k * n * 8 : (k + 1) * n * 8].reshape(n, 8, 128) for k in range(lanes // 128)]
    return parts[0] if len(parts) == 1 else jnp.concatenate(parts, axis=2)


def sum_lanes(value, first, last):
    lanes = value.shape[2]
    return (
        value
        + last * pltpu.roll(value, lanes - 1, axis=2)
        + first * pltpu.roll(value, 1, axis=2)
    )


def sum_rows(before, here, after, first, last):
    return here + last * pltpu.roll(after, 7, axis=1) + first * pltpu.roll(before, 1, axis=1)


def own_lanes(value):
    n = value.shape[0]
    lane = lax.broadcasted_iota(jnp.int32, (n, 8, 128), 2)
    mixed = jnp.where(lane >= 64, value[:, :, :128], value[:, :, 128:])
    return pltpu.roll(mixed, 64, axis=2)


def expand_walls(faces_ref):
    spread = (
        lax.broadcasted_iota(jnp.int32, (16, 128), 1) // 8
        == lax.broadcasted_iota(jnp.int32, (16, 128), 0)
    ).astype(f32)
    out = []
    for face in range(2):
        rows = faces_ref[face].astype(f32)
        wide = jnp.dot(rows, spread, preferred_element_type=f32)
        out.append(wide)
    return out


def rhs_kernel(
    adj_hbm, flow_hbm, faces_hbm,
    r_ref, up_ref, down_ref,
    adj_ref, flow_ref, faces_ref, u_ref, wall_ref, dy_ref, ky_ref, sems,
):
    moves = [
        pltpu.make_async_copy(src, dst, sems.at[k])
        for k, (src, dst) in enumerate(
            ((adj_hbm, adj_ref), (flow_hbm, flow_ref), (faces_hbm, faces_ref))
        )
    ]
    for move in moves:
        move.start()
    lanes = 128
    dy_ref[...] = lane_table(deriv)
    ky_ref[...] = lane_table(scaled_stiff)
    dcoef = row_coefs(lanes, deriv)
    kcoef = row_coefs(lanes, scaled_stiff)
    wxy = node_x(lanes, node_weights) * node_y(lanes, node_weights)
    rim = rim_mask(lanes)
    lane = iota(lanes, 1)
    for move in moves:
        move.wait()
    for face, wide in enumerate(expand_walls(faces_ref)):
        for e in range(2):
            wall_ref[face, e] = jnp.broadcast_to(wide[e : e + 1], (8, lanes))
    for c in range(3):
        for z in range(8):
            rows = flow_ref[c, z].astype(f32)
            u_ref[c, z, 0] = rows[:8]
            u_ref[c, z, 1] = rows[8:]

    def body(e, carry):
        v = [adj_ref[c, :, e] for c in range(3)]
        u = [u_ref[c, :, e] for c in range(3)]
        vall = jnp.concatenate(v, axis=0)
        uall = jnp.concatenate(u, axis=0)
        vdy = lanes_times(vall, dy_ref[...])
        vky = lanes_times(vall, ky_ref[...])
        udy = lanes_times(uall, dy_ref[...])
        stretch = [jnp.zeros((8, 8, lanes), f32)] * 3
        for j in range(3):
            stretch[0] = stretch[0] + v[j] * weigh(row_turns(u[j]), dcoef)
            stretch[1] = stretch[1] + v[j] * udy[8 * j : 8 * j + 8]
            stretch[2] = stretch[2] + v[j] * z_slope(u[j])
        ups, downs = [None] * 8, [None] * 8
        for i in range(3):
            turns = row_turns(v[i])
            planes = [v[i][z] for z in range(8)]
            zd = depth(planes, deriv, -1)
            zk = depth(planes, scaled_stiff, 1)
            xd = weigh(turns, dcoef)
            xk = weigh(turns, kcoef)
            made = []
            for z in range(8):
                wz = float(node_weights[z])
                adv = (
                    u[0][z] * xd[z]
                    + u[1][z] * vdy[8 * i + z]
                    + u[2][z] * zd[z]
                    - stretch[i][z]
                )
                bend = xk[z] + vky[8 * i + z] + zk[z]
                out = (wxy * wz) * (v[i][z] + time_step * adv - (time_step * viscosity) * bend)
                if i == 0 and z in (0, 7):
                    out = jnp.where(rim, wall_ref[z // 7, e], out)
                r_ref[i, z, e] = out
                made.append(out)
            for z in range(8):
                up, down = made[z], made[z]
                if 0 < z < 7:
                    up = up + jnp.where(lane == 88, pltpu.roll(up, 1, axis=1), 0.0)
                    down = down + jnp.where(lane == 39, pltpu.roll(down, 127, axis=1), 0.0)
                up = pltpu.roll(up, (40 * i - 88) % 128, axis=1)
                down = pltpu.roll(down, 40 * i, axis=1) if i else down
                here = (lane >= 40 * i) & (lane < 40 * i + 40)
                ups[z] = up if i == 0 else jnp.where(here, up, ups[z])
                downs[z] = down if i == 0 else jnp.where(here, down, downs[z])
        for z in range(8):
            up_ref[z, e] = ups[z]
            down_ref[z, e] = downs[z]
        return carry

    lax.fori_loop(0, 2, body, 0)


def hold_kernel(r_ref, turned_ref, dy_ref, ky_ref):
    dy_ref[...] = lane_table(deriv)
    ky_ref[...] = lane_table(scaled_stiff)
    for c in range(3):
        for z in range(8):
            for e in range(2):
                turned_ref[c, z, e] = pltpu.roll(r_ref[c, z, e], 64, axis=1)


def join_kernel(r_ref, left_ref, right_ref, e_ref, up_ref, down_ref):
    lane = iota(128, 1)
    half = lane < 64
    place = iota(256, 0)
    first = place == 0
    last = place == 7
    for c in range(3):
        faces_up = jnp.zeros((8, 256), f32)
        faces_down = jnp.zeros((8, 256), f32)
        for z in range(8):
            tiles = []
            for e in range(2):
                turned = r_ref[c, z, e]
                left = pltpu.roll(left_ref[z, e], (24 - 40 * c) % 128, axis=1)
                right = pltpu.roll(right_ref[z, e], (64 - 40 * c) % 128, axis=1)
                tile = jnp.concatenate(
                    [
                        jnp.where(half, jnp.where(lane >= 24, left, 0.0), turned),
                        jnp.where(half, turned, jnp.where(lane < 104, right, 0.0)),
                    ],
                    axis=1,
                )
                e_ref[c, z, e] = tile
                tiles.append(tile)
            if c == 0:
                go_up, go_down = tiles[1], tiles[0]
                if 0 < z < 7:
                    go_up = go_up + jnp.where(first, pltpu.roll(tiles[0], 1, axis=0), 0.0)
                    go_down = go_down + jnp.where(last, pltpu.roll(tiles[1], 7, axis=0), 0.0)
                up_ref[z] = go_up
                down_ref[z] = go_down
            else:
                turned = pltpu.roll(tiles[1], (z + 1) % 8, axis=0) if z < 7 else tiles[1]
                faces_up = jnp.where(place == z, turned, faces_up)
                turned = pltpu.roll(tiles[0], z, axis=0) if z else tiles[0]
                faces_down = jnp.where(place == z, turned, faces_down)
        if c:
            up_ref[7 + c] = faces_up
            down_ref[7 + c] = faces_down


def flags(lanes):
    first_x = (iota(lanes, 0) == 0).astype(f32)
    last_x = (iota(lanes, 0) == 7).astype(f32)
    first_y = ((iota(lanes, 1) & 7) == 0).astype(f32)
    last_y = ((iota(lanes, 1) & 7) == 7).astype(f32)
    return first_x, last_x, first_y, last_y


def source_kernel(left_ref, mid_ref, right_ref, dy_ref, b_ref, w_ref, open_ref, t_ref):
    lanes = 256
    dcoef = row_coefs(lanes, deriv)
    wx = node_x(lanes, node_weights)
    wy = node_y(lanes, node_weights)
    mx = node_x(lanes, copies)
    my = node_y(lanes, copies)
    inv = node_x(lanes, inverse_mass) * node_y(lanes, inverse_mass)
    first_x, last_x, first_y, last_y = flags(lanes)
    inside = 1.0 - rim_mask(lanes).astype(f32)

    def wall(tile):
        return jnp.broadcast_to(tile[0:1, :], (8, lanes))

    def finish(rows, faces):
        total = sum_lanes(rows, first_y, last_y)
        planes = []
        for z in range(8):
            got = total[z] * (inv * float(1.0 / node_weights[z]))
            if z in (0, 7):
                got = got * (inside * (1.0 - wall(faces[z])))
            planes.append(got)
        return jnp.stack(planes)

    def turn(tile, by):
        by = by % 8
        return pltpu.roll(tile, by, axis=0) if by else tile

    slope = {}
    left = left_ref[0:8]
    right = right_ref[0:8]
    near = finish(left + last_x * pltpu.roll(mid_ref[0, :, 0], 7, axis=1), left)
    slope[-1] = weigh(row_turns(near), dcoef)
    near = finish(right + first_x * pltpu.roll(mid_ref[0, :, 1], 1, axis=1), right)
    slope[2] = weigh(row_turns(near), dcoef)
    for e in range(2):
        faces = mid_ref[0, :, e]
        for face in range(2):
            open_face = inside * (1.0 - wall(faces[7 * face]))
            open_ref[face, e] = own_lanes(open_face[None])[0]
        w = []
        for c in range(3):
            if c == 0:
                before, after = left, right
            else:
                before = jnp.stack([turn(left_ref[7 + c], 7 - z) for z in range(8)])
                after = jnp.stack([turn(right_ref[7 + c], 8 - z) for z in range(8)])
            if e == 0:
                rows = sum_rows(before, mid_ref[c, :, 0], mid_ref[c, :, 1], first_x, last_x)
            else:
                rows = sum_rows(mid_ref[c, :, 0], mid_ref[c, :, 1], after, first_x, last_x)
            got = finish(rows, faces)
            w.append(got)
            w_ref[c, :, e] = own_lanes(got)
        slope[e] = weigh(row_turns(w[0]), dcoef)
        along = sum_lanes(lanes_times(w[1], dy_ref[...]) * wy, first_y, last_y) * (mx * wx)
        t_ref[:, e] = along + z_slope(w[2]) * (mx * wx * my * wy)
    for e in range(2):
        faces = mid_ref[0, :, e]
        rows = sum_rows(slope[e - 1], slope[e], slope[e + 1], first_x, last_x)
        total = rows * (wx * my * wy) + t_ref[:, e]
        for z in range(8):
            got = total[z] * float(-node_weights[z])
            if z in (0, 7):
                face = wall(faces[z])
                got = jnp.where(inside > 0.5, got * face, face)
            b_ref[z, e] = got


def fold(value):
    total = value[0]
    for z in range(1, 8):
        total = total + value[z]
    return total


def load_block(ref, at, v_ref, p_ref, rim, fill):
    for e in range(2):
        for z in range(8):
            got = ref[z, e]
            if z in (0, 7):
                face = jnp.broadcast_to(got[0:1, :], got.shape)
                p_ref[z // 7, at + e] = jnp.where(rim, 0.0, face)
                got = jnp.where(rim, 0.0, got)
            if fill:
                v_ref[0, z, at + e] = got


def krylov_tools(ky_ref, v_ref, k_ref, p_ref):
    lanes = 256
    kcoef = row_coefs(lanes, scaled_stiff)
    wxy = node_x(lanes, node_weights) * node_y(lanes, node_weights)
    first_x, last_x, first_y, last_y = flags(lanes)

    def apply(j, e):
        v = v_ref[j, :, e]
        yk = lanes_times(v, ky_ref[...])
        xk = weigh(row_turns(v), kcoef)
        zk = depth([v[z] for z in range(8)], scaled_stiff, 1)
        for z in range(8):
            k_ref[j, z, e] = (xk[z] + zk[z] + yk[z]) * (wxy * float(node_weights[z] / span))

    def step(j, e):
        rows = sum_rows(
            k_ref[j, :, e - 1], k_ref[j, :, e], k_ref[j, :, e + 1], first_x, last_x
        )
        total = sum_lanes(rows, first_y, last_y)
        for z in range(8):
            image = total[z]
            if z in (0, 7):
                image = image * p_ref[z // 7, e]
            v_ref[j + 1, z, e] = image - 0.5 * v_ref[j, z, e]

    return apply, step


def over(low, high, body):
    count = high - low
    lax.fori_loop(
        low, high, lambda e, c: (body(e), c)[1], 0, unroll=count if count <= 4 else count // 2
    )


def sides(low, body):
    over(0, 4, lambda t: body(low + t + (t // 2) * (6 - 2 * low)))


def inner_kernel(left_ref, mid_ref, right_ref, ky_ref, v_ref, k_ref, acc_ref, p_ref):
    rim = rim_mask(256)
    for at, ref in ((2, left_ref), (4, mid_ref), (6, right_ref)):
        load_block(ref, at, v_ref, p_ref, rim, True)
    apply, step = krylov_tools(ky_ref, v_ref, k_ref, p_ref)
    slot = 0
    for j in range(3):
        over(2 + j, 8 - j, lambda e, j=j: apply(j, e))
        for i in range(j + 1):
            acc_ref[slot + i] = fold(v_ref[i, :, 4] * k_ref[j, :, 4]) + fold(
                v_ref[i, :, 5] * k_ref[j, :, 5]
            )
        acc_ref[6 + j] = fold(v_ref[j, :, 4] * v_ref[0, :, 4]) + fold(
            v_ref[j, :, 5] * v_ref[0, :, 5]
        )
        slot += j + 1
        if j < 2:
            over(3 + j, 7 - j, lambda e, j=j: step(j, e))


def outer_kernel(*refs):
    blocks = refs[:5]
    v_in, k_in, acc_ref, ky_ref, v_out, m_out, v_ref, k_ref, p_ref = refs[5:]
    lanes = 256
    rim = rim_mask(lanes)
    for k, ref in enumerate(blocks):
        load_block(ref, 2 * k, v_ref, p_ref, rim, k in (0, 4))
    for j, els in ((0, (2, 3, 4, 5, 6, 7)), (1, (3, 4, 5, 6)), (2, (4, 5))):
        for e in els:
            v_ref[j, :, e] = v_in[j, :, e]
            if j or e not in (4, 5):
                k_ref[j, :, e] = k_in[j, :, e]
    apply, step = krylov_tools(ky_ref, v_ref, k_ref, p_ref)
    for j in range(3):
        sides(j, lambda e, j=j: apply(j, e))
        if j < 2:
            sides(j + 1, lambda e, j=j: step(j, e))
        else:
            over(3, 7, lambda e: step(2, e))
    over(4, 6, lambda e: apply(3, e))
    for e in range(4):
        v_out[0, :, e] = v_ref[2, :, 3 + e]
        v_out[1, :, e] = v_ref[3, :, 3 + e]
    energy = [acc_ref[k] for k in range(6)]
    for i in range(ROUNDS):
        energy.append(
            fold(v_ref[i, :, 4] * k_ref[3, :, 4]) + fold(v_ref[i, :, 5] * k_ref[3, :, 5])
        )
    load = [acc_ref[6 + k] for k in range(3)]
    load.append(
        fold(v_ref[3, :, 4] * v_ref[0, :, 4]) + fold(v_ref[3, :, 5] * v_ref[0, :, 5])
    )
    lane = iota(lanes, 1)
    own = (lane >= 64) & (lane < 192)
    share = node_x(lanes, 1.0 / copies) * node_y(lanes, 1.0 / copies)
    lane = iota(128, 1)
    packed = jnp.zeros((8, 128), f32)
    for k, part in enumerate(energy + load):
        part = jnp.where(own, part, 0.0)
        if k >= 10:
            part = part * share
        part = part[:, :128] + part[:, 128:]
        total = jnp.sum(jnp.sum(part, axis=0, keepdims=True), axis=1, keepdims=True)
        packed = jnp.where(lane == k, total, packed)
    m_out[...] = packed


def final_kernel(m_ref, low_ref, high_ref, w_ref, open_ref, dy_ref, out_ref, q_ref):
    lanes = 256
    parts = [m_ref[k] for k in range(m_ref.shape[0])]
    while len(parts) > 1:
        odd = parts[len(parts) // 2 * 2 :]
        parts = [parts[k] + parts[k + 1] for k in range(0, len(parts) - 1, 2)] + odd
    sums = parts[0]
    lane = iota(128, 1)

    def moment(k):
        return jnp.sum(jnp.where(lane == k, sums, 0.0), axis=1, keepdims=True)

    e = {}
    slot = 0
    for j in range(ROUNDS):
        for i in range(j + 1):
            e[j, i] = moment(slot)
            slot += 1
    g = [moment(10 + j) for j in range(ROUNDS)]
    low, diag, scaled = {}, [], {}
    for j in range(ROUNDS):
        d = e[j, j]
        for k in range(j):
            d = d - low[j, k] * scaled[j, k]
        diag.append(d)
        for i in range(j + 1, ROUNDS):
            t = e[i, j]
            for k in range(j):
                t = t - scaled[i, k] * low[j, k]
            scaled[i, j] = t
            low[i, j] = t / d
    y = []
    for j in range(ROUNDS):
        t = g[j]
        for k in range(j):
            t = t - low[j, k] * y[k]
        y.append(t)
    c = [None] * ROUNDS
    for j in reversed(range(ROUNDS)):
        t = y[j] / diag[j]
        for k in range(j + 1, ROUNDS):
            t = t - low[k, j] * c[k]
        c[j] = t
    coef = [jnp.broadcast_to(t * (1.0 / span), (8, lanes)) for t in c]

    dcoef = row_coefs(lanes, deriv)
    first_x, last_x, first_y, last_y = flags(lanes)
    mean_x = node_x(lanes, 1.0 / copies)
    mean_y = node_y(lanes, 1.0 / copies)
    q, slope = [], []
    for e in range(4):
        got = low_ref[0, :, 3 + e] * coef[0] + low_ref[1, :, 3 + e] * coef[1]
        got = got + high_ref[0, :, e] * coef[2] + high_ref[1, :, e] * coef[3]
        q.append(got)
        slope.append(weigh(row_turns(got), dcoef))
    for e in range(2):
        here = q[e + 1]
        q_own = own_lanes(here)
        q_ref[:, e] = q_own
        along_x = sum_rows(slope[e], slope[e + 1], slope[e + 2], first_x, last_x) * mean_x
        along_y = sum_lanes(lanes_times(here, dy_ref[...]), first_y, last_y) * mean_y
        parts = [own_lanes(along_x), own_lanes(along_y), z_slope(q_own)]
        for i in range(3):
            for z in range(8):
                got = w_ref[i, z, e] - parts[i][z]
                if z in (0, 7):
                    got = got * open_ref[z // 7, e]
                out_ref[i, z, e] = got


def shape(*dims):
    return jax.ShapeDtypeStruct(dims, f32)


def call(kernel, out_shape, scratch, *args, space=pltpu.VMEM, vmem=48, cost=None):
    return pl.pallas_call(
        kernel,
        out_shape=out_shape,
        in_specs=[pl.BlockSpec(memory_space=space)] * len(args),
        out_specs=jax.tree.map(lambda s: pl.BlockSpec(memory_space=pltpu.VMEM), out_shape),
        scratch_shapes=scratch,
        cost_estimate=cost,
        compiler_params=pltpu.CompilerParams(vmem_limit_bytes=int(vmem * 2**20)),
    )(*args)


def shift(value, axis, by):
    size = lax.axis_size(axis)
    return lax.ppermute(value, axis, [(i, (i + by) % size) for i in range(size)])


def total_rows(packed):
    nx, ny = lax.axis_size("gx"), lax.axis_size("gy")
    pairs = [[i, i + 1] for i in range(0, nx, 2)]
    part = lax.all_gather(packed, "gx", axis_index_groups=pairs)
    part = jnp.broadcast_to(jnp.sum(part, axis=0, keepdims=True), (ny, 8, 128))
    part = lax.all_to_all(part, "gy", 0, 0, tiled=True)
    part = jnp.broadcast_to(jnp.sum(part, axis=0, keepdims=True), (nx // 2, 8, 128))
    along = [[2 * z + c for z in range(nx // 2)] for c in range(2)]
    return lax.all_to_all(part, "gx", 0, 0, axis_index_groups=along, tiled=True)


def local(adjoint, checkpoints, wall_faces):
    adj = adjoint.reshape(3, 8, 2, 8, 128)
    flow = checkpoints.reshape(3, 8, 16, 128)
    vm = pltpu.VMEM
    table = jax.ShapeDtypeStruct((256, 256), bf16)
    strip = shape(8, 2, 8, 128)
    rhs, up, down = call(
        rhs_kernel,
        (shape(3, 8, 2, 8, 128), strip, strip),
        [
            vm((3, 8, 2, 8, 128), f32),
            vm((3, 8, 16, 128), bf16),
            vm((2, 2, 16), jnp.int32),
            vm((3, 8, 2, 8, 128), f32),
            vm((2, 2, 8, 128), f32),
            vm((256, 256), bf16),
            vm((256, 256), bf16),
            pltpu.SemaphoreType.DMA((3,)),
        ],
        adj, flow, wall_faces,
        space=pl.ANY,
        vmem=62,
    )
    left = shift(up, "gy", 1)
    right = shift(down, "gy", -1)
    packet = shape(10, 8, 256)
    cost = pl.CostEstimate(flops=10**6, bytes_accessed=4 * 10**5, transcendentals=0)
    turned, dy, ky = call(
        hold_kernel, (shape(3, 8, 2, 8, 128), table, table), [], rhs, cost=cost
    )
    wide, up, down = call(
        join_kernel, (shape(3, 8, 2, 8, 256), packet, packet), [], turned, left, right
    )
    before = shift(up, "gx", 1)
    after = shift(down, "gx", -1)
    source, moved, opened = call(
        source_kernel,
        (shape(8, 2, 8, 256), shape(3, 8, 2, 8, 128), shape(2, 2, 8, 128)),
        [vm((8, 2, 8, 256), f32)],
        before, wide, after, dy,
    )
    left = shift(source, "gx", 1)
    right = shift(source, "gx", -1)
    left2 = shift(left, "gx", 1)
    right2 = shift(right, "gx", -1)
    cost = pl.CostEstimate(flops=5 * 10**6, bytes_accessed=4 * 10**6, transcendentals=0)
    low, images, acc = call(
        inner_kernel,
        (shape(3, 8, 10, 8, 256), shape(3, 8, 10, 8, 256), shape(9, 8, 256)),
        [vm((2, 10, 8, 256), f32)],
        left, source, right, ky,
        cost=cost,
    )
    high, packed = call(
        outer_kernel,
        (shape(2, 8, 4, 8, 256), shape(8, 128)),
        [
            vm((4, 8, 10, 8, 256), f32),
            vm((4, 8, 10, 8, 256), f32),
            vm((2, 10, 8, 256), f32),
        ],
        left2, left, source, right, right2, low, images, acc, ky,
    )
    velocity, pressure = call(
        final_kernel,
        (shape(3, 8, 2, 8, 128), shape(8, 2, 8, 128)),
        [],
        total_rows(packed), low, high, moved, opened, dy,
    )
    return velocity.reshape(3, 8, 16, 128), pressure.reshape(8, 16, 128)


def solution(mesh):
    return jax.shard_map(
        local,
        mesh=mesh,
        in_specs=(P(None, None, "gx", "gy"), P(None, None, None, "gx", "gy"), P(None, "gx", "gy")),
        out_specs=(P(None, None, "gx", "gy"), P(None, "gx", "gy")),
        check_vma=False,
    )
```

```python
import jax
import jax.numpy as jnp
import numpy as np
from jax import lax
from jax.experimental import pallas as pl
from jax.experimental.pallas import tpu as pltpu
from jax.sharding import PartitionSpec as P

f32 = jnp.float32
bf16 = jnp.bfloat16

node_points = np.array(
    [
        -1.0,
        -0.8717401485096066,
        -0.5917001814331423,
        -0.2092992179024789,
        0.2092992179024789,
        0.5917001814331423,
        0.8717401485096066,
        1.0,
    ]
)
node_weights = np.array(
    [
        0.03571428571428571,
        0.2107042271435061,
        0.3411226924835044,
        0.4124587946587038,
        0.4124587946587038,
        0.3411226924835044,
        0.2107042271435061,
        0.03571428571428571,
    ]
)
time_step = 0.05
viscosity = 0.02
span = 8.0
ROUNDS = 4


def derivative_table(points):
    identity = np.eye(points.shape[0])
    spacing = points[:, None] - points[None, :] + identity
    barycentric = 1.0 / np.prod(spacing, axis=1)
    matrix = barycentric[None, :] / barycentric[:, None] / spacing
    matrix = matrix * (1.0 - identity)
    return matrix - identity * np.sum(matrix, axis=1)[:, None]


deriv = derivative_table(node_points)
stiff = deriv.T @ np.diag(node_weights) @ deriv
copies = np.array([2.0, 1, 1, 1, 1, 1, 1, 2.0])
inverse_mass = 1.0 / (copies * node_weights)


scaled_stiff = stiff / node_weights[:, None]


def iota(lanes, dim):
    return lax.broadcasted_iota(jnp.int32, (8, lanes), dim)


def pick(place, values):
    out = jnp.full(place.shape, float(values[0]), f32)
    for k in range(1, 8):
        out = jnp.where(place == k, float(values[k]), out)
    return out


def node_x(lanes, values):
    return pick(iota(lanes, 0), values)


def node_y(lanes, values):
    return pick(iota(lanes, 1) & 7, values)


def rim_mask(lanes):
    a = iota(lanes, 0)
    b = iota(lanes, 1) & 7
    return (a == 0) | (a == 7) | (b == 0) | (b == 7)


def row_coefs(lanes, matrix):
    return [node_x(lanes, [matrix[a, (a - r) % 8] for a in range(8)]) for r in range(8)]


def row_turns(value):
    return [value] + [pltpu.roll(value, r, axis=1) for r in range(1, 8)]


def weigh(turns, coefs):
    out = turns[0] * coefs[0]
    for r in range(1, 8):
        out = out + turns[r] * coefs[r]
    return out


def depth(planes, matrix, sign):
    plus = [planes[k] + planes[7 - k] for k in range(4)]
    minus = [planes[k] - planes[7 - k] for k in range(4)]
    out = [None] * 8
    for a in range(4):
        even = plus[0] * float(0.5 * (matrix[a, 0] + matrix[a, 7]))
        odd = minus[0] * float(0.5 * (matrix[a, 0] - matrix[a, 7]))
        for k in range(1, 4):
            even = even + plus[k] * float(0.5 * (matrix[a, k] + matrix[a, 7 - k]))
            odd = odd + minus[k] * float(0.5 * (matrix[a, k] - matrix[a, 7 - k]))
        out[a] = even + odd
        out[7 - a] = even - odd if sign > 0 else odd - even
    return out


def z_slope(value):
    return jnp.stack(depth([value[z] for z in range(8)], deriv, -1))


def lane_table(matrix):
    lane = iota(128, 1)
    pattern = jnp.zeros((8, 128), f32)
    for b in range(8):
        pattern = jnp.where((lane & 7) == b, node_x(128, matrix[b]), pattern)
    full = jnp.concatenate([jnp.where(lane // 8 == k, pattern, 0.0) for k in range(16)], axis=0)
    high = full.astype(bf16)
    low = (full - high.astype(f32)).astype(bf16)
    pair = jnp.concatenate([high, low], axis=1)
    return jnp.concatenate([pair, pair], axis=0)


def lanes_times(value, table):
    n, _, lanes = value.shape
    blocks = [value[:, :, k * 128 : (k + 1) * 128].reshape(n * 8, 128) for k in range(lanes // 128)]
    rows = blocks[0] if len(blocks) == 1 else jnp.concatenate(blocks, axis=0)
    high = rows.astype(bf16)
    low = (rows - high.astype(f32)).astype(bf16)
    both = jnp.concatenate([high, low], axis=1)
    got = jnp.dot(both, table, preferred_element_type=f32)
    got = got[:, :128] + got[:, 128:]
    parts = [got[k * n * 8 : (k + 1) * n * 8].reshape(n, 8, 128) for k in range(lanes // 128)]
    return parts[0] if len(parts) == 1 else jnp.concatenate(parts, axis=2)


def sum_lanes(value, first, last):
    lanes = value.shape[2]
    return (
        value
        + last * pltpu.roll(value, lanes - 1, axis=2)
        + first * pltpu.roll(value, 1, axis=2)
    )


def sum_rows(before, here, after, first, last):
    return here + last * pltpu.roll(after, 7, axis=1) + first * pltpu.roll(before, 1, axis=1)


def own_lanes(value):
    n = value.shape[0]
    lane = lax.broadcasted_iota(jnp.int32, (n, 8, 128), 2)
    mixed = jnp.where(lane >= 64, value[:, :, :128], value[:, :, 128:])
    return pltpu.roll(mixed, 64, axis=2)


def expand_walls(faces_ref):
    spread = (
        lax.broadcasted_iota(jnp.int32, (16, 128), 1) // 8
        == lax.broadcasted_iota(jnp.int32, (16, 128), 0)
    ).astype(f32)
    out = []
    for face in range(2):
        rows = faces_ref[face].astype(f32)
        wide = jnp.dot(rows, spread, preferred_element_type=f32)
        out.append(wide)
    return out


def rhs_kernel(
    adj_hbm, flow_hbm, faces_hbm,
    r_ref, up_ref, down_ref,
    adj_ref, flow_ref, faces_ref, u_ref, wall_ref, dy_ref, ky_ref, sems,
):
    moves = [
        pltpu.make_async_copy(src, dst, sems.at[k])
        for k, (src, dst) in enumerate(
            ((adj_hbm, adj_ref), (flow_hbm, flow_ref), (faces_hbm, faces_ref))
        )
    ]
    for move in moves:
        move.start()
    lanes = 128
    dy_ref[...] = lane_table(deriv)
    ky_ref[...] = lane_table(scaled_stiff)
    dcoef = row_coefs(lanes, deriv)
    kcoef = row_coefs(lanes, scaled_stiff)
    wxy = node_x(lanes, node_weights) * node_y(lanes, node_weights)
    rim = rim_mask(lanes)
    lane = iota(lanes, 1)
    for move in moves:
        move.wait()
    for face, wide in enumerate(expand_walls(faces_ref)):
        for e in range(2):
            wall_ref[face, e] = jnp.broadcast_to(wide[e : e + 1], (8, lanes))
    for c in range(3):
        for z in range(8):
            rows = flow_ref[c, z].astype(f32)
            u_ref[c, z, 0] = rows[:8]
            u_ref[c, z, 1] = rows[8:]

    def body(e, carry):
        v = [adj_ref[c, :, e] for c in range(3)]
        u = [u_ref[c, :, e] for c in range(3)]
        vall = jnp.concatenate(v, axis=0)
        uall = jnp.concatenate(u, axis=0)
        vdy = lanes_times(vall, dy_ref[...])
        vky = lanes_times(vall, ky_ref[...])
        udy = lanes_times(uall, dy_ref[...])
        stretch = [jnp.zeros((8, 8, lanes), f32)] * 3
        for j in range(3):
            stretch[0] = stretch[0] + v[j] * weigh(row_turns(u[j]), dcoef)
            stretch[1] = stretch[1] + v[j] * udy[8 * j : 8 * j + 8]
            stretch[2] = stretch[2] + v[j] * z_slope(u[j])
        ups, downs = [None] * 8, [None] * 8
        for i in range(3):
            turns = row_turns(v[i])
            planes = [v[i][z] for z in range(8)]
            zd = depth(planes, deriv, -1)
            zk = depth(planes, scaled_stiff, 1)
            xd = weigh(turns, dcoef)
            xk = weigh(turns, kcoef)
            made = []
            for z in range(8):
                wz = float(node_weights[z])
                adv = (
                    u[0][z] * xd[z]
                    + u[1][z] * vdy[8 * i + z]
                    + u[2][z] * zd[z]
                    - stretch[i][z]
                )
                bend = xk[z] + vky[8 * i + z] + zk[z]
                out = (wxy * wz) * (v[i][z] + time_step * adv - (time_step * viscosity) * bend)
                if i == 0 and z in (0, 7):
                    out = jnp.where(rim, wall_ref[z // 7, e], out)
                r_ref[i, z, e] = out
                made.append(out)
            for z in range(8):
                up, down = made[z], made[z]
                if 0 < z < 7:
                    up = up + jnp.where(lane == 88, pltpu.roll(up, 1, axis=1), 0.0)
                    down = down + jnp.where(lane == 39, pltpu.roll(down, 127, axis=1), 0.0)
                up = pltpu.roll(up, (40 * i - 88) % 128, axis=1)
                down = pltpu.roll(down, 40 * i, axis=1) if i else down
                here = (lane >= 40 * i) & (lane < 40 * i + 40)
                ups[z] = up if i == 0 else jnp.where(here, up, ups[z])
                downs[z] = down if i == 0 else jnp.where(here, down, downs[z])
        for z in range(8):
            up_ref[z, e] = ups[z]
            down_ref[z, e] = downs[z]
        return carry

    lax.fori_loop(0, 2, body, 0)


def hold_kernel(r_ref, turned_ref, dy_ref, ky_ref):
    dy_ref[...] = lane_table(deriv)
    ky_ref[...] = lane_table(scaled_stiff)
    for c in range(3):
        for z in range(8):
            for e in range(2):
                turned_ref[c, z, e] = pltpu.roll(r_ref[c, z, e], 64, axis=1)


def join_kernel(r_ref, left_ref, right_ref, e_ref, up_ref, down_ref):
    lane = iota(128, 1)
    half = lane < 64
    place = iota(256, 0)
    first = place == 0
    last = place == 7
    for c in range(3):
        faces_up = jnp.zeros((8, 256), f32)
        faces_down = jnp.zeros((8, 256), f32)
        for z in range(8):
            tiles = []
            for e in range(2):
                turned = r_ref[c, z, e]
                left = pltpu.roll(left_ref[z, e], (24 - 40 * c) % 128, axis=1)
                right = pltpu.roll(right_ref[z, e], (64 - 40 * c) % 128, axis=1)
                tile = jnp.concatenate(
                    [
                        jnp.where(half, jnp.where(lane >= 24, left, 0.0), turned),
                        jnp.where(half, turned, jnp.where(lane < 104, right, 0.0)),
                    ],
                    axis=1,
                )
                e_ref[c, z, e] = tile
                tiles.append(tile)
            if c == 0:
                go_up, go_down = tiles[1], tiles[0]
                if 0 < z < 7:
                    go_up = go_up + jnp.where(first, pltpu.roll(tiles[0], 1, axis=0), 0.0)
                    go_down = go_down + jnp.where(last, pltpu.roll(tiles[1], 7, axis=0), 0.0)
                up_ref[z] = go_up
                down_ref[z] = go_down
            else:
                turned = pltpu.roll(tiles[1], (z + 1) % 8, axis=0) if z < 7 else tiles[1]
                faces_up = jnp.where(place == z, turned, faces_up)
                turned = pltpu.roll(tiles[0], z, axis=0) if z else tiles[0]
                faces_down = jnp.where(place == z, turned, faces_down)
        if c:
            up_ref[7 + c] = faces_up
            down_ref[7 + c] = faces_down


def flags(lanes):
    first_x = (iota(lanes, 0) == 0).astype(f32)
    last_x = (iota(lanes, 0) == 7).astype(f32)
    first_y = ((iota(lanes, 1) & 7) == 0).astype(f32)
    last_y = ((iota(lanes, 1) & 7) == 7).astype(f32)
    return first_x, last_x, first_y, last_y


def source_kernel(left_ref, mid_ref, right_ref, dy_ref, b_ref, w_ref, open_ref, t_ref):
    lanes = 256
    dcoef = row_coefs(lanes, deriv)
    wx = node_x(lanes, node_weights)
    wy = node_y(lanes, node_weights)
    mx = node_x(lanes, copies)
    my = node_y(lanes, copies)
    inv = node_x(lanes, inverse_mass) * node_y(lanes, inverse_mass)
    first_x, last_x, first_y, last_y = flags(lanes)
    inside = 1.0 - rim_mask(lanes).astype(f32)

    def wall(tile):
        return jnp.broadcast_to(tile[0:1, :], (8, lanes))

    def finish(rows, faces):
        total = sum_lanes(rows, first_y, last_y)
        planes = []
        for z in range(8):
            got = total[z] * (inv * float(1.0 / node_weights[z]))
            if z in (0, 7):
                got = got * (inside * (1.0 - wall(faces[z])))
            planes.append(got)
        return jnp.stack(planes)

    def turn(tile, by):
        by = by % 8
        return pltpu.roll(tile, by, axis=0) if by else tile

    slope = {}
    left = left_ref[0:8]
    right = right_ref[0:8]
    near = finish(left + last_x * pltpu.roll(mid_ref[0, :, 0], 7, axis=1), left)
    slope[-1] = weigh(row_turns(near), dcoef)
    near = finish(right + first_x * pltpu.roll(mid_ref[0, :, 1], 1, axis=1), right)
    slope[2] = weigh(row_turns(near), dcoef)
    for e in range(2):
        faces = mid_ref[0, :, e]
        for face in range(2):
            open_face = inside * (1.0 - wall(faces[7 * face]))
            open_ref[face, e] = own_lanes(open_face[None])[0]
        w = []
        for c in range(3):
            if c == 0:
                before, after = left, right
            else:
                before = jnp.stack([turn(left_ref[7 + c], 7 - z) for z in range(8)])
                after = jnp.stack([turn(right_ref[7 + c], 8 - z) for z in range(8)])
            if e == 0:
                rows = sum_rows(before, mid_ref[c, :, 0], mid_ref[c, :, 1], first_x, last_x)
            else:
                rows = sum_rows(mid_ref[c, :, 0], mid_ref[c, :, 1], after, first_x, last_x)
            got = finish(rows, faces)
            w.append(got)
            w_ref[c, :, e] = own_lanes(got)
        slope[e] = weigh(row_turns(w[0]), dcoef)
        along = sum_lanes(lanes_times(w[1], dy_ref[...]) * wy, first_y, last_y) * (mx * wx)
        t_ref[:, e] = along + z_slope(w[2]) * (mx * wx * my * wy)
    for e in range(2):
        faces = mid_ref[0, :, e]
        rows = sum_rows(slope[e - 1], slope[e], slope[e + 1], first_x, last_x)
        total = rows * (wx * my * wy) + t_ref[:, e]
        for z in range(8):
            got = total[z] * float(-node_weights[z])
            if z in (0, 7):
                face = wall(faces[z])
                got = jnp.where(inside > 0.5, got * face, face)
            b_ref[z, e] = got


def fold(value):
    total = value[0]
    for z in range(1, 8):
        total = total + value[z]
    return total


def load_block(ref, at, v_ref, p_ref, rim, fill):
    for e in range(2):
        for z in range(8):
            got = ref[z, e]
            if z in (0, 7):
                face = jnp.broadcast_to(got[0:1, :], got.shape)
                p_ref[z // 7, at + e] = jnp.where(rim, 0.0, face)
                got = jnp.where(rim, 0.0, got)
            if fill:
                v_ref[0, z, at + e] = got


def krylov_tools(ky_ref, v_ref, k_ref, p_ref):
    lanes = 256
    kcoef = row_coefs(lanes, scaled_stiff)
    wxy = node_x(lanes, node_weights) * node_y(lanes, node_weights)
    first_x, last_x, first_y, last_y = flags(lanes)

    def apply(j, e):
        v = v_ref[j, :, e]
        yk = lanes_times(v, ky_ref[...])
        xk = weigh(row_turns(v), kcoef)
        zk = depth([v[z] for z in range(8)], scaled_stiff, 1)
        for z in range(8):
            k_ref[j, z, e] = (xk[z] + zk[z] + yk[z]) * (wxy * float(node_weights[z] / span))

    def step(j, e):
        rows = sum_rows(
            k_ref[j, :, e - 1], k_ref[j, :, e], k_ref[j, :, e + 1], first_x, last_x
        )
        total = sum_lanes(rows, first_y, last_y)
        for z in range(8):
            image = total[z]
            if z in (0, 7):
                image = image * p_ref[z // 7, e]
            v_ref[j + 1, z, e] = image - 0.5 * v_ref[j, z, e]

    return apply, step


def over(low, high, body):
    count = high - low
    lax.fori_loop(
        low, high, lambda e, c: (body(e), c)[1], 0, unroll=count if count <= 4 else count // 2
    )


def sides(low, body):
    over(0, 4, lambda t: body(low + t + (t // 2) * (6 - 2 * low)))


def inner_kernel(left_ref, mid_ref, right_ref, ky_ref, v_ref, k_ref, acc_ref, p_ref):
    rim = rim_mask(256)
    for at, ref in ((2, left_ref), (4, mid_ref), (6, right_ref)):
        load_block(ref, at, v_ref, p_ref, rim, True)
    apply, step = krylov_tools(ky_ref, v_ref, k_ref, p_ref)
    slot = 0
    for j in range(3):
        over(2 + j, 8 - j, lambda e, j=j: apply(j, e))
        for i in range(j + 1):
            acc_ref[slot + i] = fold(v_ref[i, :, 4] * k_ref[j, :, 4]) + fold(
                v_ref[i, :, 5] * k_ref[j, :, 5]
            )
        acc_ref[6 + j] = fold(v_ref[j, :, 4] * v_ref[0, :, 4]) + fold(
            v_ref[j, :, 5] * v_ref[0, :, 5]
        )
        slot += j + 1
        if j < 2:
            over(3 + j, 7 - j, lambda e, j=j: step(j, e))


def outer_kernel(*refs):
    blocks = refs[:5]
    v_in, k_in, acc_ref, ky_ref, v_out, m_out, v_ref, k_ref, p_ref = refs[5:]
    lanes = 256
    rim = rim_mask(lanes)
    for k, ref in enumerate(blocks):
        load_block(ref, 2 * k, v_ref, p_ref, rim, k in (0, 4))
    for j, els in ((0, (2, 3, 4, 5, 6, 7)), (1, (3, 4, 5, 6)), (2, (4, 5))):
        for e in els:
            v_ref[j, :, e] = v_in[j, :, e]
            if j or e not in (4, 5):
                k_ref[j, :, e] = k_in[j, :, e]
    apply, step = krylov_tools(ky_ref, v_ref, k_ref, p_ref)
    for j in range(3):
        sides(j, lambda e, j=j: apply(j, e))
        if j < 2:
            sides(j + 1, lambda e, j=j: step(j, e))
        else:
            over(3, 7, lambda e: step(2, e))
    over(4, 6, lambda e: apply(3, e))
    for e in range(4):
        v_out[0, :, e] = v_ref[2, :, 3 + e]
        v_out[1, :, e] = v_ref[3, :, 3 + e]
    energy = [acc_ref[k] for k in range(6)]
    for i in range(ROUNDS):
        energy.append(
            fold(v_ref[i, :, 4] * k_ref[3, :, 4]) + fold(v_ref[i, :, 5] * k_ref[3, :, 5])
        )
    load = [acc_ref[6 + k] for k in range(3)]
    load.append(
        fold(v_ref[3, :, 4] * v_ref[0, :, 4]) + fold(v_ref[3, :, 5] * v_ref[0, :, 5])
    )
    lane = iota(lanes, 1)
    own = (lane >= 64) & (lane < 192)
    share = node_x(lanes, 1.0 / copies) * node_y(lanes, 1.0 / copies)
    lane = iota(128, 1)
    packed = jnp.zeros((8, 128), f32)
    for k, part in enumerate(energy + load):
        part = jnp.where(own, part, 0.0)
        if k >= 10:
            part = part * share
        part = part[:, :128] + part[:, 128:]
        total = jnp.sum(jnp.sum(part, axis=0, keepdims=True), axis=1, keepdims=True)
        packed = jnp.where(lane == k, total, packed)
    for k in range(m_out.shape[0]):
        m_out[k] = packed


def final_kernel(m_ref, low_ref, high_ref, w_ref, open_ref, dy_ref, out_ref, q_ref):
    lanes = 256
    parts = [m_ref[k] for k in range(m_ref.shape[0])]
    while len(parts) > 1:
        odd = parts[len(parts) // 2 * 2 :]
        parts = [parts[k] + parts[k + 1] for k in range(0, len(parts) - 1, 2)] + odd
    sums = parts[0]
    lane = iota(128, 1)

    def moment(k):
        return jnp.sum(jnp.where(lane == k, sums, 0.0), axis=1, keepdims=True)

    e = {}
    slot = 0
    for j in range(ROUNDS):
        for i in range(j + 1):
            e[j, i] = moment(slot)
            slot += 1
    g = [moment(10 + j) for j in range(ROUNDS)]
    low, diag, scaled = {}, [], {}
    for j in range(ROUNDS):
        d = e[j, j]
        for k in range(j):
            d = d - low[j, k] * scaled[j, k]
        diag.append(d)
        for i in range(j + 1, ROUNDS):
            t = e[i, j]
            for k in range(j):
                t = t - scaled[i, k] * low[j, k]
            scaled[i, j] = t
            low[i, j] = t / d
    y = []
    for j in range(ROUNDS):
        t = g[j]
        for k in range(j):
            t = t - low[j, k] * y[k]
        y.append(t)
    c = [None] * ROUNDS
    for j in reversed(range(ROUNDS)):
        t = y[j] / diag[j]
        for k in range(j + 1, ROUNDS):
            t = t - low[k, j] * c[k]
        c[j] = t
    coef = [jnp.broadcast_to(t * (1.0 / span), (8, lanes)) for t in c]

    dcoef = row_coefs(lanes, deriv)
    first_x, last_x, first_y, last_y = flags(lanes)
    mean_x = node_x(lanes, 1.0 / copies)
    mean_y = node_y(lanes, 1.0 / copies)
    q, slope = [], []
    for e in range(4):
        got = low_ref[0, :, 3 + e] * coef[0] + low_ref[1, :, 3 + e] * coef[1]
        got = got + high_ref[0, :, e] * coef[2] + high_ref[1, :, e] * coef[3]
        q.append(got)
        slope.append(weigh(row_turns(got), dcoef))
    for e in range(2):
        here = q[e + 1]
        q_own = own_lanes(here)
        q_ref[:, e] = q_own
        along_x = sum_rows(slope[e], slope[e + 1], slope[e + 2], first_x, last_x) * mean_x
        along_y = sum_lanes(lanes_times(here, dy_ref[...]), first_y, last_y) * mean_y
        parts = [own_lanes(along_x), own_lanes(along_y), z_slope(q_own)]
        for i in range(3):
            for z in range(8):
                got = w_ref[i, z, e] - parts[i][z]
                if z in (0, 7):
                    got = got * open_ref[z // 7, e]
                out_ref[i, z, e] = got


def shape(*dims):
    return jax.ShapeDtypeStruct(dims, f32)


def call(kernel, out_shape, scratch, *args, space=pltpu.VMEM, vmem=48, cost=None):
    return pl.pallas_call(
        kernel,
        out_shape=out_shape,
        in_specs=[pl.BlockSpec(memory_space=space)] * len(args),
        out_specs=jax.tree.map(lambda s: pl.BlockSpec(memory_space=pltpu.VMEM), out_shape),
        scratch_shapes=scratch,
        cost_estimate=cost,
        compiler_params=pltpu.CompilerParams(vmem_limit_bytes=int(vmem * 2**20)),
    )(*args)


def shift(value, axis, by):
    size = lax.axis_size(axis)
    return lax.ppermute(value, axis, [(i, (i + by) % size) for i in range(size)])


def total_rows(packed):
    nx, ny = lax.axis_size("gx"), lax.axis_size("gy")
    planes = [[(2 * z + c) * ny + y for y in range(ny) for c in range(2)] for z in range(nx // 2)]
    part = lax.all_to_all(packed, ("gx", "gy"), 0, 0, axis_index_groups=planes, tiled=True)
    part = jnp.broadcast_to(jnp.sum(part, axis=0, keepdims=True), (nx // 2, 8, 128))
    along = [[2 * z + c for z in range(nx // 2)] for c in range(2)]
    return lax.all_to_all(part, "gx", 0, 0, axis_index_groups=along, tiled=True)


def local(adjoint, checkpoints, wall_faces):
    adj = adjoint.reshape(3, 8, 2, 8, 128)
    flow = checkpoints.reshape(3, 8, 16, 128)
    vm = pltpu.VMEM
    table = jax.ShapeDtypeStruct((256, 256), bf16)
    strip = shape(8, 2, 8, 128)
    rhs, up, down = call(
        rhs_kernel,
        (shape(3, 8, 2, 8, 128), strip, strip),
        [
            vm((3, 8, 2, 8, 128), f32),
            vm((3, 8, 16, 128), bf16),
            vm((2, 2, 16), jnp.int32),
            vm((3, 8, 2, 8, 128), f32),
            vm((2, 2, 8, 128), f32),
            vm((256, 256), bf16),
            vm((256, 256), bf16),
            pltpu.SemaphoreType.DMA((3,)),
        ],
        adj, flow, wall_faces,
        space=pl.ANY,
        vmem=62,
    )
    left = shift(up, "gy", 1)
    right = shift(down, "gy", -1)
    packet = shape(10, 8, 256)
    cost = pl.CostEstimate(flops=10**6, bytes_accessed=4 * 10**5, transcendentals=0)
    turned, dy, ky = call(
        hold_kernel, (shape(3, 8, 2, 8, 128), table, table), [], rhs, cost=cost
    )
    wide, up, down = call(
        join_kernel, (shape(3, 8, 2, 8, 256), packet, packet), [], turned, left, right
    )
    before = shift(up, "gx", 1)
    after = shift(down, "gx", -1)
    source, moved, opened = call(
        source_kernel,
        (shape(8, 2, 8, 256), shape(3, 8, 2, 8, 128), shape(2, 2, 8, 128)),
        [vm((8, 2, 8, 256), f32)],
        before, wide, after, dy,
    )
    left = shift(source, "gx", 1)
    right = shift(source, "gx", -1)
    right, left = lax.optimization_barrier((right, left))
    left2 = shift(left, "gx", 1)
    right2 = shift(right, "gx", -1)
    cost = pl.CostEstimate(flops=5 * 10**6, bytes_accessed=4 * 10**6, transcendentals=0)
    low, images, acc = call(
        inner_kernel,
        (shape(3, 8, 10, 8, 256), shape(3, 8, 10, 8, 256), shape(9, 8, 256)),
        [vm((2, 10, 8, 256), f32)],
        left, source, right, ky,
        cost=cost,
    )
    high, packed = call(
        outer_kernel,
        (shape(2, 8, 4, 8, 256), shape(2 * lax.axis_size("gy"), 8, 128)),
        [
            vm((4, 8, 10, 8, 256), f32),
            vm((4, 8, 10, 8, 256), f32),
            vm((2, 10, 8, 256), f32),
        ],
        left2, left, source, right, right2, low, images, acc, ky,
    )
    velocity, pressure = call(
        final_kernel,
        (shape(3, 8, 2, 8, 128), shape(8, 2, 8, 128)),
        [],
        total_rows(packed), low, high, moved, opened, dy,
    )
    return velocity.reshape(3, 8, 16, 128), pressure.reshape(8, 16, 128)


def solution(mesh):
    return jax.shard_map(
        local,
        mesh=mesh,
        in_specs=(P(None, None, "gx", "gy"), P(None, None, None, "gx", "gy"), P(None, "gx", "gy")),
        out_specs=(P(None, None, "gx", "gy"), P(None, "gx", "gy")),
        check_vma=False,
    )
```

```python
import jax
import jax.numpy as jnp
import numpy as np
from jax import lax
from jax.experimental import pallas as pl
from jax.experimental.pallas import tpu as pltpu
from jax.sharding import PartitionSpec as P

f32 = jnp.float32
bf16 = jnp.bfloat16

node_points = np.array(
    [
        -1.0,
        -0.8717401485096066,
        -0.5917001814331423,
        -0.2092992179024789,
        0.2092992179024789,
        0.5917001814331423,
        0.8717401485096066,
        1.0,
    ]
)
node_weights = np.array(
    [
        0.03571428571428571,
        0.2107042271435061,
        0.3411226924835044,
        0.4124587946587038,
        0.4124587946587038,
        0.3411226924835044,
        0.2107042271435061,
        0.03571428571428571,
    ]
)
time_step = 0.05
viscosity = 0.02
span = 8.0
ROUNDS = 4


def derivative_table(points):
    identity = np.eye(points.shape[0])
    spacing = points[:, None] - points[None, :] + identity
    barycentric = 1.0 / np.prod(spacing, axis=1)
    matrix = barycentric[None, :] / barycentric[:, None] / spacing
    matrix = matrix * (1.0 - identity)
    return matrix - identity * np.sum(matrix, axis=1)[:, None]


deriv = derivative_table(node_points)
stiff = deriv.T @ np.diag(node_weights) @ deriv
copies = np.array([2.0, 1, 1, 1, 1, 1, 1, 2.0])
inverse_mass = 1.0 / (copies * node_weights)


scaled_stiff = stiff / node_weights[:, None]


def iota(lanes, dim):
    return lax.broadcasted_iota(jnp.int32, (8, lanes), dim)


def pick(place, values):
    out = jnp.full(place.shape, float(values[0]), f32)
    for k in range(1, 8):
        out = jnp.where(place == k, float(values[k]), out)
    return out


def node_x(lanes, values):
    return pick(iota(lanes, 0), values)


def node_y(lanes, values):
    return pick(iota(lanes, 1) & 7, values)


def rim_mask(lanes):
    a = iota(lanes, 0)
    b = iota(lanes, 1) & 7
    return (a == 0) | (a == 7) | (b == 0) | (b == 7)


def row_coefs(lanes, matrix):
    return [node_x(lanes, [matrix[a, (a - r) % 8] for a in range(8)]) for r in range(8)]


def row_turns(value):
    return [value] + [pltpu.roll(value, r, axis=1) for r in range(1, 8)]


def weigh(turns, coefs):
    out = turns[0] * coefs[0]
    for r in range(1, 8):
        out = out + turns[r] * coefs[r]
    return out


def depth(planes, matrix, sign):
    plus = [planes[k] + planes[7 - k] for k in range(4)]
    minus = [planes[k] - planes[7 - k] for k in range(4)]
    out = [None] * 8
    for a in range(4):
        even = plus[0] * float(0.5 * (matrix[a, 0] + matrix[a, 7]))
        odd = minus[0] * float(0.5 * (matrix[a, 0] - matrix[a, 7]))
        for k in range(1, 4):
            even = even + plus[k] * float(0.5 * (matrix[a, k] + matrix[a, 7 - k]))
            odd = odd + minus[k] * float(0.5 * (matrix[a, k] - matrix[a, 7 - k]))
        out[a] = even + odd
        out[7 - a] = even - odd if sign > 0 else odd - even
    return out


def z_slope(value):
    return jnp.stack(depth([value[z] for z in range(8)], deriv, -1))


def lane_table(matrix):
    lane = iota(128, 1)
    pattern = jnp.zeros((8, 128), f32)
    for b in range(8):
        pattern = jnp.where((lane & 7) == b, node_x(128, matrix[b]), pattern)
    full = jnp.concatenate([jnp.where(lane // 8 == k, pattern, 0.0) for k in range(16)], axis=0)
    high = full.astype(bf16)
    low = (full - high.astype(f32)).astype(bf16)
    pair = jnp.concatenate([high, low], axis=1)
    return jnp.concatenate([pair, pair], axis=0)


def lanes_times(value, table):
    n, _, lanes = value.shape
    blocks = [value[:, :, k * 128 : (k + 1) * 128].reshape(n * 8, 128) for k in range(lanes // 128)]
    rows = blocks[0] if len(blocks) == 1 else jnp.concatenate(blocks, axis=0)
    high = rows.astype(bf16)
    low = (rows - high.astype(f32)).astype(bf16)
    both = jnp.concatenate([high, low], axis=1)
    got = jnp.dot(both, table, preferred_element_type=f32)
    got = got[:, :128] + got[:, 128:]
    parts = [got[k * n * 8 : (k + 1) * n * 8].reshape(n, 8, 128) for k in range(lanes // 128)]
    return parts[0] if len(parts) == 1 else jnp.concatenate(parts, axis=2)


def sum_lanes(value, first, last):
    lanes = value.shape[2]
    return (
        value
        + last * pltpu.roll(value, lanes - 1, axis=2)
        + first * pltpu.roll(value, 1, axis=2)
    )


def sum_rows(before, here, after, first, last):
    return here + last * pltpu.roll(after, 7, axis=1) + first * pltpu.roll(before, 1, axis=1)


def own_lanes(value):
    n = value.shape[0]
    lane = lax.broadcasted_iota(jnp.int32, (n, 8, 128), 2)
    mixed = jnp.where(lane >= 64, value[:, :, :128], value[:, :, 128:])
    return pltpu.roll(mixed, 64, axis=2)


def expand_walls(faces_ref):
    spread = (
        lax.broadcasted_iota(jnp.int32, (16, 128), 1) // 8
        == lax.broadcasted_iota(jnp.int32, (16, 128), 0)
    ).astype(f32)
    out = []
    for face in range(2):
        rows = faces_ref[face].astype(f32)
        wide = jnp.dot(rows, spread, preferred_element_type=f32)
        out.append(wide)
    return out


def rhs_kernel(
    adj_hbm, flow_hbm, faces_hbm,
    r_ref, up_ref, down_ref,
    adj_ref, flow_ref, faces_ref, u_ref, wall_ref, dy_ref, ky_ref, sems,
):
    moves = [
        pltpu.make_async_copy(src, dst, sems.at[k])
        for k, (src, dst) in enumerate(
            ((adj_hbm, adj_ref), (flow_hbm, flow_ref), (faces_hbm, faces_ref))
        )
    ]
    for move in moves:
        move.start()
    lanes = 128
    dy_ref[...] = lane_table(deriv)
    ky_ref[...] = lane_table(scaled_stiff)
    dcoef = row_coefs(lanes, deriv)
    kcoef = row_coefs(lanes, scaled_stiff)
    wxy = node_x(lanes, node_weights) * node_y(lanes, node_weights)
    rim = rim_mask(lanes)
    lane = iota(lanes, 1)
    for move in moves:
        move.wait()
    for face, wide in enumerate(expand_walls(faces_ref)):
        for e in range(2):
            wall_ref[face, e] = jnp.broadcast_to(wide[e : e + 1], (8, lanes))
    for c in range(3):
        for z in range(8):
            rows = flow_ref[c, z].astype(f32)
            u_ref[c, z, 0] = rows[:8]
            u_ref[c, z, 1] = rows[8:]

    def body(e, carry):
        v = [adj_ref[c, :, e] for c in range(3)]
        u = [u_ref[c, :, e] for c in range(3)]
        vall = jnp.concatenate(v, axis=0)
        uall = jnp.concatenate(u, axis=0)
        vdy = lanes_times(vall, dy_ref[...])
        vky = lanes_times(vall, ky_ref[...])
        udy = lanes_times(uall, dy_ref[...])
        stretch = [jnp.zeros((8, 8, lanes), f32)] * 3
        for j in range(3):
            stretch[0] = stretch[0] + v[j] * weigh(row_turns(u[j]), dcoef)
            stretch[1] = stretch[1] + v[j] * udy[8 * j : 8 * j + 8]
            stretch[2] = stretch[2] + v[j] * z_slope(u[j])
        ups, downs = [None] * 8, [None] * 8
        for i in range(3):
            turns = row_turns(v[i])
            planes = [v[i][z] for z in range(8)]
            zd = depth(planes, deriv, -1)
            zk = depth(planes, scaled_stiff, 1)
            xd = weigh(turns, dcoef)
            xk = weigh(turns, kcoef)
            made = []
            for z in range(8):
                wz = float(node_weights[z])
                adv = (
                    u[0][z] * xd[z]
                    + u[1][z] * vdy[8 * i + z]
                    + u[2][z] * zd[z]
                    - stretch[i][z]
                )
                bend = xk[z] + vky[8 * i + z] + zk[z]
                out = (wxy * wz) * (v[i][z] + time_step * adv - (time_step * viscosity) * bend)
                if i == 0 and z in (0, 7):
                    out = jnp.where(rim, wall_ref[z // 7, e], out)
                r_ref[i, z, e] = out
                made.append(out)
            for z in range(8):
                up, down = made[z], made[z]
                if 0 < z < 7:
                    up = up + jnp.where(lane == 88, pltpu.roll(up, 1, axis=1), 0.0)
                    down = down + jnp.where(lane == 39, pltpu.roll(down, 127, axis=1), 0.0)
                up = pltpu.roll(up, (40 * i - 88) % 128, axis=1)
                down = pltpu.roll(down, 40 * i, axis=1) if i else down
                here = (lane >= 40 * i) & (lane < 40 * i + 40)
                ups[z] = up if i == 0 else jnp.where(here, up, ups[z])
                downs[z] = down if i == 0 else jnp.where(here, down, downs[z])
        for z in range(8):
            up_ref[z, e] = ups[z]
            down_ref[z, e] = downs[z]
        return carry

    lax.fori_loop(0, 2, body, 0)


def hold_kernel(r_ref, turned_ref, dy_ref, ky_ref):
    dy_ref[...] = lane_table(deriv)
    ky_ref[...] = lane_table(scaled_stiff)
    for c in range(3):
        for z in range(8):
            for e in range(2):
                turned_ref[c, z, e] = pltpu.roll(r_ref[c, z, e], 64, axis=1)


def join_kernel(r_ref, left_ref, right_ref, e_ref, up_ref, down_ref):
    lane = iota(128, 1)
    half = lane < 64
    place = iota(256, 0)
    first = place == 0
    last = place == 7
    for c in range(3):
        faces_up = jnp.zeros((8, 256), f32)
        faces_down = jnp.zeros((8, 256), f32)
        for z in range(8):
            tiles = []
            for e in range(2):
                turned = r_ref[c, z, e]
                left = pltpu.roll(left_ref[z, e], (24 - 40 * c) % 128, axis=1)
                right = pltpu.roll(right_ref[z, e], (64 - 40 * c) % 128, axis=1)
                tile = jnp.concatenate(
                    [
                        jnp.where(half, jnp.where(lane >= 24, left, 0.0), turned),
                        jnp.where(half, turned, jnp.where(lane < 104, right, 0.0)),
                    ],
                    axis=1,
                )
                e_ref[c, z, e] = tile
                tiles.append(tile)
            if c == 0:
                go_up, go_down = tiles[1], tiles[0]
                if 0 < z < 7:
                    go_up = go_up + jnp.where(first, pltpu.roll(tiles[0], 1, axis=0), 0.0)
                    go_down = go_down + jnp.where(last, pltpu.roll(tiles[1], 7, axis=0), 0.0)
                up_ref[z] = go_up
                down_ref[z] = go_down
            else:
                turned = pltpu.roll(tiles[1], (z + 1) % 8, axis=0) if z < 7 else tiles[1]
                faces_up = jnp.where(place == z, turned, faces_up)
                turned = pltpu.roll(tiles[0], z, axis=0) if z else tiles[0]
                faces_down = jnp.where(place == z, turned, faces_down)
        if c:
            up_ref[7 + c] = faces_up
            down_ref[7 + c] = faces_down


def flags(lanes):
    first_x = (iota(lanes, 0) == 0).astype(f32)
    last_x = (iota(lanes, 0) == 7).astype(f32)
    first_y = ((iota(lanes, 1) & 7) == 0).astype(f32)
    last_y = ((iota(lanes, 1) & 7) == 7).astype(f32)
    return first_x, last_x, first_y, last_y


def source_kernel(left_ref, mid_ref, right_ref, dy_ref, b_ref, w_ref, open_ref, t_ref):
    lanes = 256
    dcoef = row_coefs(lanes, deriv)
    wx = node_x(lanes, node_weights)
    wy = node_y(lanes, node_weights)
    mx = node_x(lanes, copies)
    my = node_y(lanes, copies)
    inv = node_x(lanes, inverse_mass) * node_y(lanes, inverse_mass)
    first_x, last_x, first_y, last_y = flags(lanes)
    inside = 1.0 - rim_mask(lanes).astype(f32)

    def wall(tile):
        return jnp.broadcast_to(tile[0:1, :], (8, lanes))

    def finish(rows, faces):
        total = sum_lanes(rows, first_y, last_y)
        planes = []
        for z in range(8):
            got = total[z] * (inv * float(1.0 / node_weights[z]))
            if z in (0, 7):
                got = got * (inside * (1.0 - wall(faces[z])))
            planes.append(got)
        return jnp.stack(planes)

    def turn(tile, by):
        by = by % 8
        return pltpu.roll(tile, by, axis=0) if by else tile

    slope = {}
    left = left_ref[0:8]
    right = right_ref[0:8]
    near = finish(left + last_x * pltpu.roll(mid_ref[0, :, 0], 7, axis=1), left)
    slope[-1] = weigh(row_turns(near), dcoef)
    near = finish(right + first_x * pltpu.roll(mid_ref[0, :, 1], 1, axis=1), right)
    slope[2] = weigh(row_turns(near), dcoef)
    for e in range(2):
        faces = mid_ref[0, :, e]
        for face in range(2):
            open_face = inside * (1.0 - wall(faces[7 * face]))
            open_ref[face, e] = own_lanes(open_face[None])[0]
        w = []
        for c in range(3):
            if c == 0:
                before, after = left, right
            else:
                before = jnp.stack([turn(left_ref[7 + c], 7 - z) for z in range(8)])
                after = jnp.stack([turn(right_ref[7 + c], 8 - z) for z in range(8)])
            if e == 0:
                rows = sum_rows(before, mid_ref[c, :, 0], mid_ref[c, :, 1], first_x, last_x)
            else:
                rows = sum_rows(mid_ref[c, :, 0], mid_ref[c, :, 1], after, first_x, last_x)
            got = finish(rows, faces)
            w.append(got)
            w_ref[c, :, e] = own_lanes(got)
        slope[e] = weigh(row_turns(w[0]), dcoef)
        along = sum_lanes(lanes_times(w[1], dy_ref[...]) * wy, first_y, last_y) * (mx * wx)
        t_ref[:, e] = along + z_slope(w[2]) * (mx * wx * my * wy)
    for e in range(2):
        faces = mid_ref[0, :, e]
        rows = sum_rows(slope[e - 1], slope[e], slope[e + 1], first_x, last_x)
        total = rows * (wx * my * wy) + t_ref[:, e]
        for z in range(8):
            got = total[z] * float(-node_weights[z])
            if z in (0, 7):
                face = wall(faces[z])
                got = jnp.where(inside > 0.5, got * face, face)
            b_ref[z, e] = got


def fold(value):
    total = value[0]
    for z in range(1, 8):
        total = total + value[z]
    return total


def load_block(ref, at, v_ref, p_ref, rim, fill):
    for e in range(2):
        for z in range(8):
            got = ref[z, e]
            if z in (0, 7):
                face = jnp.broadcast_to(got[0:1, :], got.shape)
                p_ref[z // 7, at + e] = jnp.where(rim, 0.0, face)
                got = jnp.where(rim, 0.0, got)
            if fill:
                v_ref[0, z, at + e] = got


def krylov_tools(ky_ref, v_ref, k_ref, p_ref):
    lanes = 256
    kcoef = row_coefs(lanes, scaled_stiff)
    wxy = node_x(lanes, node_weights) * node_y(lanes, node_weights)
    first_x, last_x, first_y, last_y = flags(lanes)

    def apply(j, e):
        v = v_ref[j, :, e]
        yk = lanes_times(v, ky_ref[...])
        xk = weigh(row_turns(v), kcoef)
        zk = depth([v[z] for z in range(8)], scaled_stiff, 1)
        for z in range(8):
            k_ref[j, z, e] = (xk[z] + zk[z] + yk[z]) * (wxy * float(node_weights[z] / span))

    def step(j, e):
        rows = sum_rows(
            k_ref[j, :, e - 1], k_ref[j, :, e], k_ref[j, :, e + 1], first_x, last_x
        )
        total = sum_lanes(rows, first_y, last_y)
        for z in range(8):
            image = total[z]
            if z in (0, 7):
                image = image * p_ref[z // 7, e]
            v_ref[j + 1, z, e] = image - 0.5 * v_ref[j, z, e]

    return apply, step


def over(low, high, body):
    count = high - low
    lax.fori_loop(
        low, high, lambda e, c: (body(e), c)[1], 0, unroll=count if count <= 4 else count // 2
    )


def sides(low, body):
    over(0, 4, lambda t: body(low + t + (t // 2) * (6 - 2 * low)))


def inner_kernel(left_ref, mid_ref, right_ref, ky_ref, v_ref, k_ref, acc_ref, p_ref):
    rim = rim_mask(256)
    for at, ref in ((2, left_ref), (4, mid_ref), (6, right_ref)):
        load_block(ref, at, v_ref, p_ref, rim, True)
    apply, step = krylov_tools(ky_ref, v_ref, k_ref, p_ref)
    slot = 0
    for j in range(3):
        over(2 + j, 8 - j, lambda e, j=j: apply(j, e))
        for i in range(j + 1):
            acc_ref[slot + i] = fold(v_ref[i, :, 4] * k_ref[j, :, 4]) + fold(
                v_ref[i, :, 5] * k_ref[j, :, 5]
            )
        acc_ref[6 + j] = fold(v_ref[j, :, 4] * v_ref[0, :, 4]) + fold(
            v_ref[j, :, 5] * v_ref[0, :, 5]
        )
        slot += j + 1
        if j < 2:
            over(3 + j, 7 - j, lambda e, j=j: step(j, e))


def outer_kernel(*refs):
    blocks = refs[:5]
    v_in, k_in, acc_ref, ky_ref, v_out, m_out, v_ref, k_ref, p_ref = refs[5:]
    lanes = 256
    rim = rim_mask(lanes)
    for k, ref in enumerate(blocks):
        load_block(ref, 2 * k, v_ref, p_ref, rim, k in (0, 4))
    for j, els in ((0, (2, 3, 4, 5, 6, 7)), (1, (3, 4, 5, 6)), (2, (4, 5))):
        for e in els:
            v_ref[j, :, e] = v_in[j, :, e]
            if j or e not in (4, 5):
                k_ref[j, :, e] = k_in[j, :, e]
    apply, step = krylov_tools(ky_ref, v_ref, k_ref, p_ref)
    for j in range(3):
        sides(j, lambda e, j=j: apply(j, e))
        if j < 2:
            sides(j + 1, lambda e, j=j: step(j, e))
        else:
            over(3, 7, lambda e: step(2, e))
    over(4, 6, lambda e: apply(3, e))
    for e in range(4):
        v_out[0, :, e] = v_ref[2, :, 3 + e]
        v_out[1, :, e] = v_ref[3, :, 3 + e]
    energy = [acc_ref[k] for k in range(6)]
    for i in range(ROUNDS):
        energy.append(
            fold(v_ref[i, :, 4] * k_ref[3, :, 4]) + fold(v_ref[i, :, 5] * k_ref[3, :, 5])
        )
    load = [acc_ref[6 + k] for k in range(3)]
    load.append(
        fold(v_ref[3, :, 4] * v_ref[0, :, 4]) + fold(v_ref[3, :, 5] * v_ref[0, :, 5])
    )
    lane = iota(lanes, 1)
    own = (lane >= 64) & (lane < 192)
    share = node_x(lanes, 1.0 / copies) * node_y(lanes, 1.0 / copies)
    lane = iota(128, 1)
    packed = jnp.zeros((8, 128), f32)
    for k, part in enumerate(energy + load):
        part = jnp.where(own, part, 0.0)
        if k >= 10:
            part = part * share
        part = part[:, :128] + part[:, 128:]
        total = jnp.sum(jnp.sum(part, axis=0, keepdims=True), axis=1, keepdims=True)
        packed = jnp.where(lane == k, total, packed)
    for k in range(m_out.shape[0] // 8):
        m_out[8 * k : 8 * k + 8] = packed


def final_kernel(m_ref, low_ref, high_ref, w_ref, open_ref, dy_ref, out_ref, q_ref):
    lanes = 256
    parts = [m_ref[8 * k : 8 * k + 8] for k in range(m_ref.shape[0] // 8)]
    while len(parts) > 1:
        odd = parts[len(parts) // 2 * 2 :]
        parts = [parts[k] + parts[k + 1] for k in range(0, len(parts) - 1, 2)] + odd
    sums = jnp.broadcast_to(jnp.sum(parts[0], axis=0, keepdims=True), (8, 128))
    lane = iota(128, 1)

    def moment(k):
        return jnp.sum(jnp.where(lane == k, sums, 0.0), axis=1, keepdims=True)

    e = {}
    slot = 0
    for j in range(ROUNDS):
        for i in range(j + 1):
            e[j, i] = moment(slot)
            slot += 1
    g = [moment(10 + j) for j in range(ROUNDS)]
    low, diag, scaled = {}, [], {}
    for j in range(ROUNDS):
        d = e[j, j]
        for k in range(j):
            d = d - low[j, k] * scaled[j, k]
        diag.append(d)
        for i in range(j + 1, ROUNDS):
            t = e[i, j]
            for k in range(j):
                t = t - scaled[i, k] * low[j, k]
            scaled[i, j] = t
            low[i, j] = t / d
    y = []
    for j in range(ROUNDS):
        t = g[j]
        for k in range(j):
            t = t - low[j, k] * y[k]
        y.append(t)
    c = [None] * ROUNDS
    for j in reversed(range(ROUNDS)):
        t = y[j] / diag[j]
        for k in range(j + 1, ROUNDS):
            t = t - low[k, j] * c[k]
        c[j] = t
    coef = [jnp.broadcast_to(t * (1.0 / span), (8, lanes)) for t in c]

    dcoef = row_coefs(lanes, deriv)
    first_x, last_x, first_y, last_y = flags(lanes)
    mean_x = node_x(lanes, 1.0 / copies)
    mean_y = node_y(lanes, 1.0 / copies)
    q, slope = [], []
    for e in range(4):
        got = low_ref[0, :, 3 + e] * coef[0] + low_ref[1, :, 3 + e] * coef[1]
        got = got + high_ref[0, :, e] * coef[2] + high_ref[1, :, e] * coef[3]
        q.append(got)
        slope.append(weigh(row_turns(got), dcoef))
    for e in range(2):
        here = q[e + 1]
        q_own = own_lanes(here)
        q_ref[:, e] = q_own
        along_x = sum_rows(slope[e], slope[e + 1], slope[e + 2], first_x, last_x) * mean_x
        along_y = sum_lanes(lanes_times(here, dy_ref[...]), first_y, last_y) * mean_y
        parts = [own_lanes(along_x), own_lanes(along_y), z_slope(q_own)]
        for i in range(3):
            for z in range(8):
                got = w_ref[i, z, e] - parts[i][z]
                if z in (0, 7):
                    got = got * open_ref[z // 7, e]
                out_ref[i, z, e] = got


def shape(*dims):
    return jax.ShapeDtypeStruct(dims, f32)


def call(kernel, out_shape, scratch, *args, space=pltpu.VMEM, vmem=48, cost=None):
    return pl.pallas_call(
        kernel,
        out_shape=out_shape,
        in_specs=[pl.BlockSpec(memory_space=space)] * len(args),
        out_specs=jax.tree.map(lambda s: pl.BlockSpec(memory_space=pltpu.VMEM), out_shape),
        scratch_shapes=scratch,
        cost_estimate=cost,
        compiler_params=pltpu.CompilerParams(vmem_limit_bytes=int(vmem * 2**20)),
    )(*args)


def shift(value, axis, by):
    size = lax.axis_size(axis)
    return lax.ppermute(value, axis, [(i, (i + by) % size) for i in range(size)])


def total_rows(packed):
    nx, ny = lax.axis_size("gx"), lax.axis_size("gy")
    planes = [[(2 * z + c) * ny + y for y in range(ny) for c in range(2)] for z in range(nx // 2)]
    part = lax.all_to_all(packed, ("gx", "gy"), 0, 0, axis_index_groups=planes, tiled=True)
    part = jnp.broadcast_to(jnp.sum(part, axis=0, keepdims=True), (nx // 2, 128))
    along = [[2 * z + c for z in range(nx // 2)] for c in range(2)]
    return lax.all_to_all(part, "gx", 0, 0, axis_index_groups=along, tiled=True)


def local(adjoint, checkpoints, wall_faces):
    adj = adjoint.reshape(3, 8, 2, 8, 128)
    flow = checkpoints.reshape(3, 8, 16, 128)
    vm = pltpu.VMEM
    table = jax.ShapeDtypeStruct((256, 256), bf16)
    strip = shape(8, 2, 8, 128)
    rhs, up, down = call(
        rhs_kernel,
        (shape(3, 8, 2, 8, 128), strip, strip),
        [
            vm((3, 8, 2, 8, 128), f32),
            vm((3, 8, 16, 128), bf16),
            vm((2, 2, 16), jnp.int32),
            vm((3, 8, 2, 8, 128), f32),
            vm((2, 2, 8, 128), f32),
            vm((256, 256), bf16),
            vm((256, 256), bf16),
            pltpu.SemaphoreType.DMA((3,)),
        ],
        adj, flow, wall_faces,
        space=pl.ANY,
        vmem=62,
    )
    left = shift(up, "gy", 1)
    right = shift(down, "gy", -1)
    packet = shape(10, 8, 256)
    cost = pl.CostEstimate(flops=10**6, bytes_accessed=4 * 10**5, transcendentals=0)
    turned, dy, ky = call(
        hold_kernel, (shape(3, 8, 2, 8, 128), table, table), [], rhs, cost=cost
    )
    wide, up, down = call(
        join_kernel, (shape(3, 8, 2, 8, 256), packet, packet), [], turned, left, right
    )
    before = shift(up, "gx", 1)
    after = shift(down, "gx", -1)
    source, moved, opened = call(
        source_kernel,
        (shape(8, 2, 8, 256), shape(3, 8, 2, 8, 128), shape(2, 2, 8, 128)),
        [vm((8, 2, 8, 256), f32)],
        before, wide, after, dy,
    )
    left = shift(source, "gx", 1)
    right = shift(source, "gx", -1)
    right, left = lax.optimization_barrier((right, left))
    left2 = shift(left, "gx", 1)
    right2 = shift(right, "gx", -1)
    cost = pl.CostEstimate(flops=5 * 10**6, bytes_accessed=4 * 10**6, transcendentals=0)
    low, images, acc = call(
        inner_kernel,
        (shape(3, 8, 10, 8, 256), shape(3, 8, 10, 8, 256), shape(9, 8, 256)),
        [vm((2, 10, 8, 256), f32)],
        left, source, right, ky,
        cost=cost,
    )
    high, packed = call(
        outer_kernel,
        (shape(2, 8, 4, 8, 256), shape(2 * lax.axis_size("gy"), 128)),
        [
            vm((4, 8, 10, 8, 256), f32),
            vm((4, 8, 10, 8, 256), f32),
            vm((2, 10, 8, 256), f32),
        ],
        left2, left, source, right, right2, low, images, acc, ky,
    )
    velocity, pressure = call(
        final_kernel,
        (shape(3, 8, 2, 8, 128), shape(8, 2, 8, 128)),
        [],
        total_rows(packed), low, high, moved, opened, dy,
    )
    return velocity.reshape(3, 8, 16, 128), pressure.reshape(8, 16, 128)


def solution(mesh):
    return jax.shard_map(
        local,
        mesh=mesh,
        in_specs=(P(None, None, "gx", "gy"), P(None, None, None, "gx", "gy"), P(None, "gx", "gy")),
        out_specs=(P(None, None, "gx", "gy"), P(None, "gx", "gy")),
        check_vma=False,
    )
```

```python
import jax
import jax.numpy as jnp
import numpy as np
from jax import lax
from jax.experimental import pallas as pl
from jax.experimental.pallas import tpu as pltpu
from jax.sharding import PartitionSpec as P

f32 = jnp.float32
bf16 = jnp.bfloat16

node_points = np.array(
    [
        -1.0,
        -0.8717401485096066,
        -0.5917001814331423,
        -0.2092992179024789,
        0.2092992179024789,
        0.5917001814331423,
        0.8717401485096066,
        1.0,
    ]
)
node_weights = np.array(
    [
        0.03571428571428571,
        0.2107042271435061,
        0.3411226924835044,
        0.4124587946587038,
        0.4124587946587038,
        0.3411226924835044,
        0.2107042271435061,
        0.03571428571428571,
    ]
)
time_step = 0.05
viscosity = 0.02
span = 8.0
ROUNDS = 4


def derivative_table(points):
    identity = np.eye(points.shape[0])
    spacing = points[:, None] - points[None, :] + identity
    barycentric = 1.0 / np.prod(spacing, axis=1)
    matrix = barycentric[None, :] / barycentric[:, None] / spacing
    matrix = matrix * (1.0 - identity)
    return matrix - identity * np.sum(matrix, axis=1)[:, None]


deriv = derivative_table(node_points)
stiff = deriv.T @ np.diag(node_weights) @ deriv
copies = np.array([2.0, 1, 1, 1, 1, 1, 1, 2.0])
inverse_mass = 1.0 / (copies * node_weights)


scaled_stiff = stiff / node_weights[:, None]


def iota(lanes, dim):
    return lax.broadcasted_iota(jnp.int32, (8, lanes), dim)


def pick(place, values):
    out = jnp.full(place.shape, float(values[0]), f32)
    for k in range(1, 8):
        out = jnp.where(place == k, float(values[k]), out)
    return out


def node_x(lanes, values):
    return pick(iota(lanes, 0), values)


def node_y(lanes, values):
    return pick(iota(lanes, 1) & 7, values)


def rim_mask(lanes):
    a = iota(lanes, 0)
    b = iota(lanes, 1) & 7
    return (a == 0) | (a == 7) | (b == 0) | (b == 7)


def row_coefs(lanes, matrix):
    return [node_x(lanes, [matrix[a, (a - r) % 8] for a in range(8)]) for r in range(8)]


def row_turns(value):
    return [value] + [pltpu.roll(value, r, axis=1) for r in range(1, 8)]


def weigh(turns, coefs):
    out = turns[0] * coefs[0]
    for r in range(1, 8):
        out = out + turns[r] * coefs[r]
    return out


def depth(planes, matrix, sign):
    plus = [planes[k] + planes[7 - k] for k in range(4)]
    minus = [planes[k] - planes[7 - k] for k in range(4)]
    out = [None] * 8
    for a in range(4):
        even = plus[0] * float(0.5 * (matrix[a, 0] + matrix[a, 7]))
        odd = minus[0] * float(0.5 * (matrix[a, 0] - matrix[a, 7]))
        for k in range(1, 4):
            even = even + plus[k] * float(0.5 * (matrix[a, k] + matrix[a, 7 - k]))
            odd = odd + minus[k] * float(0.5 * (matrix[a, k] - matrix[a, 7 - k]))
        out[a] = even + odd
        out[7 - a] = even - odd if sign > 0 else odd - even
    return out


def z_slope(value):
    return jnp.stack(depth([value[z] for z in range(8)], deriv, -1))


def lane_table(matrix):
    lane = iota(128, 1)
    pattern = jnp.zeros((8, 128), f32)
    for b in range(8):
        pattern = jnp.where((lane & 7) == b, node_x(128, matrix[b]), pattern)
    full = jnp.concatenate([jnp.where(lane // 8 == k, pattern, 0.0) for k in range(16)], axis=0)
    high = full.astype(bf16)
    low = (full - high.astype(f32)).astype(bf16)
    pair = jnp.concatenate([high, low], axis=1)
    return jnp.concatenate([pair, pair], axis=0)


def lanes_times(value, table):
    n, _, lanes = value.shape
    blocks = [value[:, :, k * 128 : (k + 1) * 128].reshape(n * 8, 128) for k in range(lanes // 128)]
    rows = blocks[0] if len(blocks) == 1 else jnp.concatenate(blocks, axis=0)
    high = rows.astype(bf16)
    low = (rows - high.astype(f32)).astype(bf16)
    both = jnp.concatenate([high, low], axis=1)
    got = jnp.dot(both, table, preferred_element_type=f32)
    got = got[:, :128] + got[:, 128:]
    parts = [got[k * n * 8 : (k + 1) * n * 8].reshape(n, 8, 128) for k in range(lanes // 128)]
    return parts[0] if len(parts) == 1 else jnp.concatenate(parts, axis=2)


def sum_lanes(value, first, last):
    lanes = value.shape[2]
    return (
        value
        + last * pltpu.roll(value, lanes - 1, axis=2)
        + first * pltpu.roll(value, 1, axis=2)
    )


def sum_rows(before, here, after, first, last):
    return here + last * pltpu.roll(after, 7, axis=1) + first * pltpu.roll(before, 1, axis=1)


def own_lanes(value):
    n = value.shape[0]
    lane = lax.broadcasted_iota(jnp.int32, (n, 8, 128), 2)
    mixed = jnp.where(lane >= 64, value[:, :, :128], value[:, :, 128:])
    return pltpu.roll(mixed, 64, axis=2)


def expand_walls(faces_ref):
    spread = (
        lax.broadcasted_iota(jnp.int32, (16, 128), 1) // 8
        == lax.broadcasted_iota(jnp.int32, (16, 128), 0)
    ).astype(f32)
    out = []
    for face in range(2):
        rows = faces_ref[face].astype(f32)
        wide = jnp.dot(rows, spread, preferred_element_type=f32)
        out.append(wide)
    return out


def rhs_kernel(
    adj_hbm, flow_hbm, faces_hbm,
    r_ref, up_ref, down_ref,
    adj_ref, flow_ref, faces_ref, u_ref, wall_ref, dy_ref, ky_ref, sems,
):
    moves = [
        pltpu.make_async_copy(src, dst, sems.at[k])
        for k, (src, dst) in enumerate(
            ((adj_hbm, adj_ref), (flow_hbm, flow_ref), (faces_hbm, faces_ref))
        )
    ]
    for move in moves:
        move.start()
    lanes = 128
    dy_ref[...] = lane_table(deriv)
    ky_ref[...] = lane_table(scaled_stiff)
    dcoef = row_coefs(lanes, deriv)
    kcoef = row_coefs(lanes, scaled_stiff)
    wxy = node_x(lanes, node_weights) * node_y(lanes, node_weights)
    rim = rim_mask(lanes)
    lane = iota(lanes, 1)
    for move in moves:
        move.wait()
    for face, wide in enumerate(expand_walls(faces_ref)):
        for e in range(2):
            wall_ref[face, e] = jnp.broadcast_to(wide[e : e + 1], (8, lanes))
    for c in range(3):
        for z in range(8):
            rows = flow_ref[c, z].astype(f32)
            u_ref[c, z, 0] = rows[:8]
            u_ref[c, z, 1] = rows[8:]

    def body(e, carry):
        v = [adj_ref[c, :, e] for c in range(3)]
        u = [u_ref[c, :, e] for c in range(3)]
        vall = jnp.concatenate(v, axis=0)
        uall = jnp.concatenate(u, axis=0)
        vdy = lanes_times(vall, dy_ref[...])
        vky = lanes_times(vall, ky_ref[...])
        udy = lanes_times(uall, dy_ref[...])
        stretch = [jnp.zeros((8, 8, lanes), f32)] * 3
        for j in range(3):
            stretch[0] = stretch[0] + v[j] * weigh(row_turns(u[j]), dcoef)
            stretch[1] = stretch[1] + v[j] * udy[8 * j : 8 * j + 8]
            stretch[2] = stretch[2] + v[j] * z_slope(u[j])
        ups, downs = [None] * 8, [None] * 8
        for i in range(3):
            turns = row_turns(v[i])
            planes = [v[i][z] for z in range(8)]
            zd = depth(planes, deriv, -1)
            zk = depth(planes, scaled_stiff, 1)
            xd = weigh(turns, dcoef)
            xk = weigh(turns, kcoef)
            made = []
            for z in range(8):
                wz = float(node_weights[z])
                adv = (
                    u[0][z] * xd[z]
                    + u[1][z] * vdy[8 * i + z]
                    + u[2][z] * zd[z]
                    - stretch[i][z]
                )
                bend = xk[z] + vky[8 * i + z] + zk[z]
                out = (wxy * wz) * (v[i][z] + time_step * adv - (time_step * viscosity) * bend)
                if i == 0 and z in (0, 7):
                    out = jnp.where(rim, wall_ref[z // 7, e], out)
                r_ref[i, z, e] = out
                made.append(out)
            for z in range(8):
                up, down = made[z], made[z]
                if 0 < z < 7:
                    up = up + jnp.where(lane == 88, pltpu.roll(up, 1, axis=1), 0.0)
                    down = down + jnp.where(lane == 39, pltpu.roll(down, 127, axis=1), 0.0)
                up = pltpu.roll(up, (40 * i - 88) % 128, axis=1)
                down = pltpu.roll(down, 40 * i, axis=1) if i else down
                here = (lane >= 40 * i) & (lane < 40 * i + 40)
                ups[z] = up if i == 0 else jnp.where(here, up, ups[z])
                downs[z] = down if i == 0 else jnp.where(here, down, downs[z])
        for z in range(8):
            up_ref[z, e] = ups[z]
            down_ref[z, e] = downs[z]
        return carry

    lax.fori_loop(0, 2, body, 0, unroll=2)


def hold_kernel(r_ref, turned_ref, dy_ref, ky_ref):
    dy_ref[...] = lane_table(deriv)
    ky_ref[...] = lane_table(scaled_stiff)
    for c in range(3):
        for z in range(8):
            for e in range(2):
                turned_ref[c, z, e] = pltpu.roll(r_ref[c, z, e], 64, axis=1)


def join_kernel(r_ref, left_ref, right_ref, e_ref, up_ref, down_ref):
    lane = iota(128, 1)
    half = lane < 64
    place = iota(256, 0)
    first = place == 0
    last = place == 7
    for c in range(3):
        faces_up = jnp.zeros((8, 256), f32)
        faces_down = jnp.zeros((8, 256), f32)
        for z in range(8):
            tiles = []
            for e in range(2):
                turned = r_ref[c, z, e]
                left = pltpu.roll(left_ref[z, e], (24 - 40 * c) % 128, axis=1)
                right = pltpu.roll(right_ref[z, e], (64 - 40 * c) % 128, axis=1)
                tile = jnp.concatenate(
                    [
                        jnp.where(half, jnp.where(lane >= 24, left, 0.0), turned),
                        jnp.where(half, turned, jnp.where(lane < 104, right, 0.0)),
                    ],
                    axis=1,
                )
                e_ref[c, z, e] = tile
                tiles.append(tile)
            if c == 0:
                go_up, go_down = tiles[1], tiles[0]
                if 0 < z < 7:
                    go_up = go_up + jnp.where(first, pltpu.roll(tiles[0], 1, axis=0), 0.0)
                    go_down = go_down + jnp.where(last, pltpu.roll(tiles[1], 7, axis=0), 0.0)
                up_ref[z] = go_up
                down_ref[z] = go_down
            else:
                turned = pltpu.roll(tiles[1], (z + 1) % 8, axis=0) if z < 7 else tiles[1]
                faces_up = jnp.where(place == z, turned, faces_up)
                turned = pltpu.roll(tiles[0], z, axis=0) if z else tiles[0]
                faces_down = jnp.where(place == z, turned, faces_down)
        if c:
            up_ref[7 + c] = faces_up
            down_ref[7 + c] = faces_down


def flags(lanes):
    first_x = (iota(lanes, 0) == 0).astype(f32)
    last_x = (iota(lanes, 0) == 7).astype(f32)
    first_y = ((iota(lanes, 1) & 7) == 0).astype(f32)
    last_y = ((iota(lanes, 1) & 7) == 7).astype(f32)
    return first_x, last_x, first_y, last_y


def source_kernel(left_ref, mid_ref, right_ref, dy_ref, b_ref, pack_ref, w_ref, open_ref, t_ref):
    lanes = 256
    dcoef = row_coefs(lanes, deriv)
    wx = node_x(lanes, node_weights)
    wy = node_y(lanes, node_weights)
    mx = node_x(lanes, copies)
    my = node_y(lanes, copies)
    inv = node_x(lanes, inverse_mass) * node_y(lanes, inverse_mass)
    first_x, last_x, first_y, last_y = flags(lanes)
    inside = 1.0 - rim_mask(lanes).astype(f32)
    half = iota(128, 1) < 64

    def wall(tile):
        return jnp.broadcast_to(tile[0:1, :], (8, lanes))

    def finish(rows, faces):
        total = sum_lanes(rows, first_y, last_y)
        planes = []
        for z in range(8):
            got = total[z] * (inv * float(1.0 / node_weights[z]))
            if z in (0, 7):
                got = got * (inside * (1.0 - wall(faces[z])))
            planes.append(got)
        return jnp.stack(planes)

    def turn(tile, by):
        by = by % 8
        return pltpu.roll(tile, by, axis=0) if by else tile

    slope = {}
    left = left_ref[0:8]
    right = right_ref[0:8]
    near = finish(left + last_x * pltpu.roll(mid_ref[0, :, 0], 7, axis=1), left)
    slope[-1] = weigh(row_turns(near), dcoef)
    near = finish(right + first_x * pltpu.roll(mid_ref[0, :, 1], 1, axis=1), right)
    slope[2] = weigh(row_turns(near), dcoef)
    for e in range(2):
        faces = mid_ref[0, :, e]
        for face in range(2):
            open_face = inside * (1.0 - wall(faces[7 * face]))
            open_ref[face, e] = own_lanes(open_face[None])[0]
        w = []
        for c in range(3):
            if c == 0:
                before, after = left, right
            else:
                before = jnp.stack([turn(left_ref[7 + c], 7 - z) for z in range(8)])
                after = jnp.stack([turn(right_ref[7 + c], 8 - z) for z in range(8)])
            if e == 0:
                rows = sum_rows(before, mid_ref[c, :, 0], mid_ref[c, :, 1], first_x, last_x)
            else:
                rows = sum_rows(mid_ref[c, :, 0], mid_ref[c, :, 1], after, first_x, last_x)
            got = finish(rows, faces)
            w.append(got)
            w_ref[c, :, e] = own_lanes(got)
        slope[e] = weigh(row_turns(w[0]), dcoef)
        along = sum_lanes(lanes_times(w[1], dy_ref[...]) * wy, first_y, last_y) * (mx * wx)
        t_ref[:, e] = along + z_slope(w[2]) * (mx * wx * my * wy)
    for e in range(2):
        faces = mid_ref[0, :, e]
        rows = sum_rows(slope[e - 1], slope[e], slope[e + 1], first_x, last_x)
        total = rows * (wx * my * wy) + t_ref[:, e]
        edges = []
        for z in range(8):
            got = total[z] * float(-node_weights[z])
            if z in (0, 7):
                face = wall(faces[z])
                got = jnp.where(inside > 0.5, got * face, face)
            b_ref[z, e] = got
            pack_ref[z, e] = own_lanes(got[None])[0]
            edges.append(jnp.where(half, got[:, :128], got[:, 128:]))
        for z in range(4):
            pack_ref[8 + z, e] = jnp.where(
                half, pltpu.roll(edges[z], 96, axis=1), pltpu.roll(edges[z + 4], 32, axis=1)
            )


def unpack(ref, z, e):
    lane = iota(128, 1)
    middle = pltpu.roll(ref[z, e], 64, axis=1)
    edge = pltpu.roll(ref[8 + z % 4, e], 32 if z < 4 else 96, axis=1)
    low = jnp.where(lane >= 64, middle, jnp.where(lane >= 32, edge, 0.0))
    high = jnp.where(lane < 64, middle, jnp.where(lane < 96, edge, 0.0))
    return jnp.concatenate([low, high], axis=1)


def fold(value):
    total = value[0]
    for z in range(1, 8):
        total = total + value[z]
    return total


def load_block(read, at, v_ref, p_ref, rim):
    for e in range(2):
        for z in range(8):
            got = read(z, e)
            if z in (0, 7):
                face = jnp.broadcast_to(got[0:1, :], got.shape)
                p_ref[z // 7, at + e] = jnp.where(rim, 0.0, face)
                got = jnp.where(rim, 0.0, got)
            v_ref[0, z, at + e] = got


def krylov_tools(ky_ref, v_ref, k_ref, p_ref):
    lanes = 256
    kcoef = row_coefs(lanes, scaled_stiff)
    wxy = node_x(lanes, node_weights) * node_y(lanes, node_weights)
    first_x, last_x, first_y, last_y = flags(lanes)

    def apply(j, e):
        v = v_ref[j, :, e]
        yk = lanes_times(v, ky_ref[...])
        xk = weigh(row_turns(v), kcoef)
        zk = depth([v[z] for z in range(8)], scaled_stiff, 1)
        for z in range(8):
            k_ref[j, z, e] = (xk[z] + zk[z] + yk[z]) * (wxy * float(node_weights[z] / span))

    def step(j, e):
        rows = sum_rows(
            k_ref[j, :, e - 1], k_ref[j, :, e], k_ref[j, :, e + 1], first_x, last_x
        )
        total = sum_lanes(rows, first_y, last_y)
        for z in range(8):
            image = total[z]
            if z in (0, 7):
                image = image * p_ref[z // 7, e]
            v_ref[j + 1, z, e] = image - 0.5 * v_ref[j, z, e]

    return apply, step


def over(low, high, body):
    count = high - low
    lax.fori_loop(
        low, high, lambda e, c: (body(e), c)[1], 0, unroll=count if count <= 4 else count // 2
    )


def sides(low, body):
    over(0, 4, lambda t: body(low + t + (t // 2) * (6 - 2 * low)))


def inner_kernel(left_ref, mid_ref, right_ref, ky_ref, v_ref, k_ref, acc_ref, p_ref):
    rim = rim_mask(256)
    load_block(lambda z, e: unpack(left_ref, z, e), 2, v_ref, p_ref, rim)
    load_block(lambda z, e: mid_ref[z, e], 4, v_ref, p_ref, rim)
    load_block(lambda z, e: unpack(right_ref, z, e), 6, v_ref, p_ref, rim)
    apply, step = krylov_tools(ky_ref, v_ref, k_ref, p_ref)
    slot = 0
    for j in range(3):
        over(2 + j, 8 - j, lambda e, j=j: apply(j, e))
        for i in range(j + 1):
            acc_ref[slot + i] = fold(v_ref[i, :, 4] * k_ref[j, :, 4]) + fold(
                v_ref[i, :, 5] * k_ref[j, :, 5]
            )
        acc_ref[6 + j] = fold(v_ref[j, :, 4] * v_ref[0, :, 4]) + fold(
            v_ref[j, :, 5] * v_ref[0, :, 5]
        )
        slot += j + 1
        if j < 2:
            over(3 + j, 7 - j, lambda e, j=j: step(j, e))


def outer_kernel(
    left_ref, right_ref, v_in, k_in, acc_ref, p_in, ky_ref, v_out, m_out, v_ref, k_ref, p_ref
):
    lanes = 256
    rim = rim_mask(lanes)
    load_block(lambda z, e: unpack(left_ref, z, e), 0, v_ref, p_ref, rim)
    load_block(lambda z, e: unpack(right_ref, z, e), 8, v_ref, p_ref, rim)
    for e in range(2, 8):
        p_ref[:, e] = p_in[:, e]
    for j, els in ((0, (2, 3, 4, 5, 6, 7)), (1, (3, 4, 5, 6)), (2, (4, 5))):
        for e in els:
            v_ref[j, :, e] = v_in[j, :, e]
            if j or e not in (4, 5):
                k_ref[j, :, e] = k_in[j, :, e]
    apply, step = krylov_tools(ky_ref, v_ref, k_ref, p_ref)
    for j in range(3):
        sides(j, lambda e, j=j: apply(j, e))
        if j < 2:
            sides(j + 1, lambda e, j=j: step(j, e))
        else:
            over(3, 7, lambda e: step(2, e))
    over(4, 6, lambda e: apply(3, e))
    for e in range(4):
        v_out[0, :, e] = v_ref[2, :, 3 + e]
        v_out[1, :, e] = v_ref[3, :, 3 + e]
    energy = [acc_ref[k] for k in range(6)]
    for i in range(ROUNDS):
        energy.append(
            fold(v_ref[i, :, 4] * k_ref[3, :, 4]) + fold(v_ref[i, :, 5] * k_ref[3, :, 5])
        )
    load = [acc_ref[6 + k] for k in range(3)]
    load.append(
        fold(v_ref[3, :, 4] * v_ref[0, :, 4]) + fold(v_ref[3, :, 5] * v_ref[0, :, 5])
    )
    lane = iota(lanes, 1)
    own = (lane >= 64) & (lane < 192)
    share = node_x(lanes, 1.0 / copies) * node_y(lanes, 1.0 / copies)
    lane = iota(128, 1)
    packed = jnp.zeros((8, 128), f32)
    for k, part in enumerate(energy + load):
        part = jnp.where(own, part, 0.0)
        if k >= 10:
            part = part * share
        part = part[:, :128] + part[:, 128:]
        total = jnp.sum(jnp.sum(part, axis=0, keepdims=True), axis=1, keepdims=True)
        packed = jnp.where(lane == k, total, packed)
    for k in range(m_out.shape[0] // 8):
        m_out[8 * k : 8 * k + 8] = packed


def final_kernel(m_ref, low_ref, high_ref, w_ref, open_ref, dy_ref, out_ref, q_ref):
    lanes = 256
    parts = [m_ref[8 * k : 8 * k + 8] for k in range(m_ref.shape[0] // 8)]
    while len(parts) > 1:
        odd = parts[len(parts) // 2 * 2 :]
        parts = [parts[k] + parts[k + 1] for k in range(0, len(parts) - 1, 2)] + odd
    sums = jnp.broadcast_to(jnp.sum(parts[0], axis=0, keepdims=True), (8, 128))
    lane = iota(128, 1)

    def moment(k):
        return jnp.sum(jnp.where(lane == k, sums, 0.0), axis=1, keepdims=True)

    e = {}
    slot = 0
    for j in range(ROUNDS):
        for i in range(j + 1):
            e[j, i] = moment(slot)
            slot += 1
    g = [moment(10 + j) for j in range(ROUNDS)]
    low, diag, scaled = {}, [], {}
    for j in range(ROUNDS):
        d = e[j, j]
        for k in range(j):
            d = d - low[j, k] * scaled[j, k]
        diag.append(d)
        for i in range(j + 1, ROUNDS):
            t = e[i, j]
            for k in range(j):
                t = t - scaled[i, k] * low[j, k]
            scaled[i, j] = t
            low[i, j] = t / d
    y = []
    for j in range(ROUNDS):
        t = g[j]
        for k in range(j):
            t = t - low[j, k] * y[k]
        y.append(t)
    c = [None] * ROUNDS
    for j in reversed(range(ROUNDS)):
        t = y[j] / diag[j]
        for k in range(j + 1, ROUNDS):
            t = t - low[k, j] * c[k]
        c[j] = t
    coef = [jnp.broadcast_to(t * (1.0 / span), (8, lanes)) for t in c]

    dcoef = row_coefs(lanes, deriv)
    first_x, last_x, first_y, last_y = flags(lanes)
    mean_x = node_x(lanes, 1.0 / copies)
    mean_y = node_y(lanes, 1.0 / copies)
    q, slope = [], []
    for e in range(4):
        got = low_ref[0, :, 3 + e] * coef[0] + low_ref[1, :, 3 + e] * coef[1]
        got = got + high_ref[0, :, e] * coef[2] + high_ref[1, :, e] * coef[3]
        q.append(got)
        slope.append(weigh(row_turns(got), dcoef))
    for e in range(2):
        here = q[e + 1]
        q_own = own_lanes(here)
        q_ref[:, e] = q_own
        along_x = sum_rows(slope[e], slope[e + 1], slope[e + 2], first_x, last_x) * mean_x
        along_y = sum_lanes(lanes_times(here, dy_ref[...]), first_y, last_y) * mean_y
        parts = [own_lanes(along_x), own_lanes(along_y), z_slope(q_own)]
        for i in range(3):
            for z in range(8):
                got = w_ref[i, z, e] - parts[i][z]
                if z in (0, 7):
                    got = got * open_ref[z // 7, e]
                out_ref[i, z, e] = got


def shape(*dims):
    return jax.ShapeDtypeStruct(dims, f32)


def call(kernel, out_shape, scratch, *args, space=pltpu.VMEM, vmem=48, cost=None):
    return pl.pallas_call(
        kernel,
        out_shape=out_shape,
        in_specs=[pl.BlockSpec(memory_space=space)] * len(args),
        out_specs=jax.tree.map(lambda s: pl.BlockSpec(memory_space=pltpu.VMEM), out_shape),
        scratch_shapes=scratch,
        cost_estimate=cost,
        compiler_params=pltpu.CompilerParams(vmem_limit_bytes=int(vmem * 2**20)),
    )(*args)


def shift(value, axis, by):
    size = lax.axis_size(axis)
    return lax.ppermute(value, axis, [(i, (i + by) % size) for i in range(size)])


def total_rows(packed):
    nx, ny = lax.axis_size("gx"), lax.axis_size("gy")
    planes = [[(2 * z + c) * ny + y for y in range(ny) for c in range(2)] for z in range(nx // 2)]
    part = lax.all_to_all(packed, ("gx", "gy"), 0, 0, axis_index_groups=planes, tiled=True)
    part = jnp.broadcast_to(jnp.sum(part, axis=0, keepdims=True), (nx // 2, 128))
    along = [[2 * z + c for z in range(nx // 2)] for c in range(2)]
    return lax.all_to_all(part, "gx", 0, 0, axis_index_groups=along, tiled=True)


def local(adjoint, checkpoints, wall_faces):
    adj = adjoint.reshape(3, 8, 2, 8, 128)
    flow = checkpoints.reshape(3, 8, 16, 128)
    vm = pltpu.VMEM
    table = jax.ShapeDtypeStruct((256, 256), bf16)
    strip = shape(8, 2, 8, 128)
    rhs, up, down = call(
        rhs_kernel,
        (shape(3, 8, 2, 8, 128), strip, strip),
        [
            vm((3, 8, 2, 8, 128), f32),
            vm((3, 8, 16, 128), bf16),
            vm((2, 2, 16), jnp.int32),
            vm((3, 8, 2, 8, 128), f32),
            vm((2, 2, 8, 128), f32),
            vm((256, 256), bf16),
            vm((256, 256), bf16),
            pltpu.SemaphoreType.DMA((3,)),
        ],
        adj, flow, wall_faces,
        space=pl.ANY,
        vmem=62,
    )
    left = shift(up, "gy", 1)
    right = shift(down, "gy", -1)
    packet = shape(10, 8, 256)
    cost = pl.CostEstimate(flops=10**6, bytes_accessed=4 * 10**5, transcendentals=0)
    turned, dy, ky = call(
        hold_kernel, (shape(3, 8, 2, 8, 128), table, table), [], rhs, cost=cost
    )
    wide, up, down = call(
        join_kernel, (shape(3, 8, 2, 8, 256), packet, packet), [], turned, left, right
    )
    before = shift(up, "gx", 1)
    after = shift(down, "gx", -1)
    source, pack, moved, opened = call(
        source_kernel,
        (shape(8, 2, 8, 256), shape(12, 2, 8, 128), shape(3, 8, 2, 8, 128), shape(2, 2, 8, 128)),
        [vm((8, 2, 8, 256), f32)],
        before, wide, after, dy,
    )
    left = shift(pack, "gx", 1)
    right = shift(pack, "gx", -1)
    right, left = lax.optimization_barrier((right, left))
    left2 = shift(left, "gx", 1)
    right2 = shift(right, "gx", -1)
    cost = pl.CostEstimate(flops=5 * 10**6, bytes_accessed=4 * 10**6, transcendentals=0)
    low, images, acc, faces = call(
        inner_kernel,
        (
            shape(3, 8, 10, 8, 256),
            shape(3, 8, 10, 8, 256),
            shape(9, 8, 256),
            shape(2, 10, 8, 256),
        ),
        [],
        left, source, right, ky,
        cost=cost,
    )
    high, packed = call(
        outer_kernel,
        (shape(2, 8, 4, 8, 256), shape(2 * lax.axis_size("gy"), 128)),
        [
            vm((4, 8, 10, 8, 256), f32),
            vm((4, 8, 10, 8, 256), f32),
            vm((2, 10, 8, 256), f32),
        ],
        left2, right2, low, images, acc, faces, ky,
    )
    velocity, pressure = call(
        final_kernel,
        (shape(3, 8, 2, 8, 128), shape(8, 2, 8, 128)),
        [],
        total_rows(packed), low, high, moved, opened, dy,
    )
    return velocity.reshape(3, 8, 16, 128), pressure.reshape(8, 16, 128)


def solution(mesh):
    return jax.shard_map(
        local,
        mesh=mesh,
        in_specs=(P(None, None, "gx", "gy"), P(None, None, None, "gx", "gy"), P(None, "gx", "gy")),
        out_specs=(P(None, None, "gx", "gy"), P(None, "gx", "gy")),
        check_vma=False,
    )
```

```python
import jax
import jax.numpy as jnp
import numpy as np
from jax import lax
from jax.experimental import pallas as pl
from jax.experimental.pallas import tpu as pltpu
from jax.sharding import PartitionSpec as P

f32 = jnp.float32
bf16 = jnp.bfloat16

node_points = np.array(
    [
        -1.0,
        -0.8717401485096066,
        -0.5917001814331423,
        -0.2092992179024789,
        0.2092992179024789,
        0.5917001814331423,
        0.8717401485096066,
        1.0,
    ]
)
node_weights = np.array(
    [
        0.03571428571428571,
        0.2107042271435061,
        0.3411226924835044,
        0.4124587946587038,
        0.4124587946587038,
        0.3411226924835044,
        0.2107042271435061,
        0.03571428571428571,
    ]
)
time_step = 0.05
viscosity = 0.02
span = 8.0
ROUNDS = 4


def derivative_table(points):
    identity = np.eye(points.shape[0])
    spacing = points[:, None] - points[None, :] + identity
    barycentric = 1.0 / np.prod(spacing, axis=1)
    matrix = barycentric[None, :] / barycentric[:, None] / spacing
    matrix = matrix * (1.0 - identity)
    return matrix - identity * np.sum(matrix, axis=1)[:, None]


deriv = derivative_table(node_points)
stiff = deriv.T @ np.diag(node_weights) @ deriv
copies = np.array([2.0, 1, 1, 1, 1, 1, 1, 2.0])
inverse_mass = 1.0 / (copies * node_weights)


scaled_stiff = stiff / node_weights[:, None]


def iota(lanes, dim):
    return lax.broadcasted_iota(jnp.int32, (8, lanes), dim)


def pick(place, values):
    out = jnp.full(place.shape, float(values[0]), f32)
    for k in range(1, 8):
        out = jnp.where(place == k, float(values[k]), out)
    return out


def node_x(lanes, values):
    return pick(iota(lanes, 0), values)


def node_y(lanes, values):
    return pick(iota(lanes, 1) & 7, values)


def rim_mask(lanes):
    a = iota(lanes, 0)
    b = iota(lanes, 1) & 7
    return (a == 0) | (a == 7) | (b == 0) | (b == 7)


def row_coefs(lanes, matrix):
    return [node_x(lanes, [matrix[a, (a - r) % 8] for a in range(8)]) for r in range(8)]


def row_turns(value):
    return [value] + [pltpu.roll(value, r, axis=1) for r in range(1, 8)]


def weigh(turns, coefs):
    out = turns[0] * coefs[0]
    for r in range(1, 8):
        out = out + turns[r] * coefs[r]
    return out


def depth(planes, matrix, sign):
    plus = [planes[k] + planes[7 - k] for k in range(4)]
    minus = [planes[k] - planes[7 - k] for k in range(4)]
    out = [None] * 8
    for a in range(4):
        even = plus[0] * float(0.5 * (matrix[a, 0] + matrix[a, 7]))
        odd = minus[0] * float(0.5 * (matrix[a, 0] - matrix[a, 7]))
        for k in range(1, 4):
            even = even + plus[k] * float(0.5 * (matrix[a, k] + matrix[a, 7 - k]))
            odd = odd + minus[k] * float(0.5 * (matrix[a, k] - matrix[a, 7 - k]))
        out[a] = even + odd
        out[7 - a] = even - odd if sign > 0 else odd - even
    return out


def z_slope(value):
    return jnp.stack(depth([value[z] for z in range(8)], deriv, -1))


def lane_table(matrix):
    lane = iota(128, 1)
    pattern = jnp.zeros((8, 128), f32)
    for b in range(8):
        pattern = jnp.where((lane & 7) == b, node_x(128, matrix[b]), pattern)
    full = jnp.concatenate([jnp.where(lane // 8 == k, pattern, 0.0) for k in range(16)], axis=0)
    high = full.astype(bf16)
    low = (full - high.astype(f32)).astype(bf16)
    pair = jnp.concatenate([high, low], axis=1)
    return jnp.concatenate([pair, pair], axis=0)


def lanes_times(value, table):
    n, _, lanes = value.shape
    blocks = [value[:, :, k * 128 : (k + 1) * 128].reshape(n * 8, 128) for k in range(lanes // 128)]
    rows = blocks[0] if len(blocks) == 1 else jnp.concatenate(blocks, axis=0)
    high = rows.astype(bf16)
    low = (rows - high.astype(f32)).astype(bf16)
    both = jnp.concatenate([high, low], axis=1)
    got = jnp.dot(both, table, preferred_element_type=f32)
    got = got[:, :128] + got[:, 128:]
    parts = [got[k * n * 8 : (k + 1) * n * 8].reshape(n, 8, 128) for k in range(lanes // 128)]
    return parts[0] if len(parts) == 1 else jnp.concatenate(parts, axis=2)


def sum_lanes(value, first, last):
    lanes = value.shape[2]
    return (
        value
        + last * pltpu.roll(value, lanes - 1, axis=2)
        + first * pltpu.roll(value, 1, axis=2)
    )


def sum_rows(before, here, after, first, last):
    return here + last * pltpu.roll(after, 7, axis=1) + first * pltpu.roll(before, 1, axis=1)


def own_lanes(value):
    n = value.shape[0]
    lane = lax.broadcasted_iota(jnp.int32, (n, 8, 128), 2)
    mixed = jnp.where(lane >= 64, value[:, :, :128], value[:, :, 128:])
    return pltpu.roll(mixed, 64, axis=2)


def expand_walls(faces_ref):
    spread = (
        lax.broadcasted_iota(jnp.int32, (16, 128), 1) // 8
        == lax.broadcasted_iota(jnp.int32, (16, 128), 0)
    ).astype(f32)
    out = []
    for face in range(2):
        rows = faces_ref[face].astype(f32)
        wide = jnp.dot(rows, spread, preferred_element_type=f32)
        out.append(wide)
    return out


def rhs_kernel(
    adj_hbm, flow_hbm, faces_hbm,
    r_ref, up_ref, down_ref,
    adj_ref, flow_ref, faces_ref, u_ref, wall_ref, dy_ref, ky_ref, sems,
):
    moves = [
        pltpu.make_async_copy(src, dst, sems.at[k])
        for k, (src, dst) in enumerate(
            ((adj_hbm, adj_ref), (flow_hbm, flow_ref), (faces_hbm, faces_ref))
        )
    ]
    for move in moves:
        move.start()
    lanes = 128
    dy_ref[...] = lane_table(deriv)
    ky_ref[...] = lane_table(scaled_stiff)
    dcoef = row_coefs(lanes, deriv)
    kcoef = row_coefs(lanes, scaled_stiff)
    wxy = node_x(lanes, node_weights) * node_y(lanes, node_weights)
    rim = rim_mask(lanes)
    lane = iota(lanes, 1)
    for move in moves:
        move.wait()
    for face, wide in enumerate(expand_walls(faces_ref)):
        for e in range(2):
            wall_ref[face, e] = jnp.broadcast_to(wide[e : e + 1], (8, lanes))
    for c in range(3):
        for z in range(8):
            rows = flow_ref[c, z].astype(f32)
            u_ref[c, z, 0] = rows[:8]
            u_ref[c, z, 1] = rows[8:]

    def body(e, carry):
        v = [adj_ref[c, :, e] for c in range(3)]
        u = [u_ref[c, :, e] for c in range(3)]
        vall = jnp.concatenate(v, axis=0)
        uall = jnp.concatenate(u, axis=0)
        vdy = lanes_times(vall, dy_ref[...])
        vky = lanes_times(vall, ky_ref[...])
        udy = lanes_times(uall, dy_ref[...])
        stretch = [jnp.zeros((8, 8, lanes), f32)] * 3
        for j in range(3):
            stretch[0] = stretch[0] + v[j] * weigh(row_turns(u[j]), dcoef)
            stretch[1] = stretch[1] + v[j] * udy[8 * j : 8 * j + 8]
            stretch[2] = stretch[2] + v[j] * z_slope(u[j])
        ups, downs = [None] * 8, [None] * 8
        for i in range(3):
            turns = row_turns(v[i])
            planes = [v[i][z] for z in range(8)]
            zd = depth(planes, deriv, -1)
            zk = depth(planes, scaled_stiff, 1)
            xd = weigh(turns, dcoef)
            xk = weigh(turns, kcoef)
            made = []
            for z in range(8):
                wz = float(node_weights[z])
                adv = (
                    u[0][z] * xd[z]
                    + u[1][z] * vdy[8 * i + z]
                    + u[2][z] * zd[z]
                    - stretch[i][z]
                )
                bend = xk[z] + vky[8 * i + z] + zk[z]
                out = (wxy * wz) * (v[i][z] + time_step * adv - (time_step * viscosity) * bend)
                if i == 0 and z in (0, 7):
                    out = jnp.where(rim, wall_ref[z // 7, e], out)
                r_ref[i, z, e] = out
                made.append(out)
            for z in range(8):
                up, down = made[z], made[z]
                if 0 < z < 7:
                    up = up + jnp.where(lane == 88, pltpu.roll(up, 1, axis=1), 0.0)
                    down = down + jnp.where(lane == 39, pltpu.roll(down, 127, axis=1), 0.0)
                up = pltpu.roll(up, (40 * i - 88) % 128, axis=1)
                down = pltpu.roll(down, 40 * i, axis=1) if i else down
                here = (lane >= 40 * i) & (lane < 40 * i + 40)
                ups[z] = up if i == 0 else jnp.where(here, up, ups[z])
                downs[z] = down if i == 0 else jnp.where(here, down, downs[z])
        for z in range(8):
            up_ref[z, e] = ups[z]
            down_ref[z, e] = downs[z]
        return carry

    lax.fori_loop(0, 2, body, 0, unroll=2)


def hold_kernel(r_ref, turned_ref, dy_ref, ky_ref):
    dy_ref[...] = lane_table(deriv)
    ky_ref[...] = lane_table(scaled_stiff)
    for c in range(3):
        for z in range(8):
            for e in range(2):
                turned_ref[c, z, e] = pltpu.roll(r_ref[c, z, e], 64, axis=1)


def join_kernel(r_ref, left_ref, right_ref, e_ref, up_ref, down_ref):
    lane = iota(128, 1)
    half = lane < 64
    place = iota(256, 0)
    first = place == 0
    last = place == 7
    for c in range(3):
        faces_up = jnp.zeros((8, 256), f32)
        faces_down = jnp.zeros((8, 256), f32)
        for z in range(8):
            tiles = []
            for e in range(2):
                turned = r_ref[c, z, e]
                left = pltpu.roll(left_ref[z, e], (24 - 40 * c) % 128, axis=1)
                right = pltpu.roll(right_ref[z, e], (64 - 40 * c) % 128, axis=1)
                tile = jnp.concatenate(
                    [
                        jnp.where(half, jnp.where(lane >= 24, left, 0.0), turned),
                        jnp.where(half, turned, jnp.where(lane < 104, right, 0.0)),
                    ],
                    axis=1,
                )
                e_ref[c, z, e] = tile
                tiles.append(tile)
            if c == 0:
                go_up, go_down = tiles[1], tiles[0]
                if 0 < z < 7:
                    go_up = go_up + jnp.where(first, pltpu.roll(tiles[0], 1, axis=0), 0.0)
                    go_down = go_down + jnp.where(last, pltpu.roll(tiles[1], 7, axis=0), 0.0)
                up_ref[z] = go_up
                down_ref[z] = go_down
            else:
                turned = pltpu.roll(tiles[1], (z + 1) % 8, axis=0) if z < 7 else tiles[1]
                faces_up = jnp.where(place == z, turned, faces_up)
                turned = pltpu.roll(tiles[0], z, axis=0) if z else tiles[0]
                faces_down = jnp.where(place == z, turned, faces_down)
        if c:
            up_ref[7 + c] = faces_up
            down_ref[7 + c] = faces_down


def flags(lanes):
    first_x = (iota(lanes, 0) == 0).astype(f32)
    last_x = (iota(lanes, 0) == 7).astype(f32)
    first_y = ((iota(lanes, 1) & 7) == 0).astype(f32)
    last_y = ((iota(lanes, 1) & 7) == 7).astype(f32)
    return first_x, last_x, first_y, last_y


def source_kernel(left_ref, mid_ref, right_ref, dy_ref, b_ref, pack_ref, w_ref, open_ref, t_ref):
    lanes = 256
    dcoef = row_coefs(lanes, deriv)
    wx = node_x(lanes, node_weights)
    wy = node_y(lanes, node_weights)
    mx = node_x(lanes, copies)
    my = node_y(lanes, copies)
    inv = node_x(lanes, inverse_mass) * node_y(lanes, inverse_mass)
    first_x, last_x, first_y, last_y = flags(lanes)
    inside = 1.0 - rim_mask(lanes).astype(f32)
    half = iota(128, 1) < 64

    def wall(tile):
        return jnp.broadcast_to(tile[0:1, :], (8, lanes))

    def finish(rows, faces):
        total = sum_lanes(rows, first_y, last_y)
        planes = []
        for z in range(8):
            got = total[z] * (inv * float(1.0 / node_weights[z]))
            if z in (0, 7):
                got = got * (inside * (1.0 - wall(faces[z])))
            planes.append(got)
        return jnp.stack(planes)

    def turn(tile, by):
        by = by % 8
        return pltpu.roll(tile, by, axis=0) if by else tile

    slope = {}
    left = left_ref[0:8]
    right = right_ref[0:8]
    near = finish(left + last_x * pltpu.roll(mid_ref[0, :, 0], 7, axis=1), left)
    slope[-1] = weigh(row_turns(near), dcoef)
    near = finish(right + first_x * pltpu.roll(mid_ref[0, :, 1], 1, axis=1), right)
    slope[2] = weigh(row_turns(near), dcoef)
    for e in range(2):
        faces = mid_ref[0, :, e]
        for face in range(2):
            open_face = inside * (1.0 - wall(faces[7 * face]))
            open_ref[face, e] = own_lanes(open_face[None])[0]
        w = []
        for c in range(3):
            if c == 0:
                before, after = left, right
            else:
                before = jnp.stack([turn(left_ref[7 + c], 7 - z) for z in range(8)])
                after = jnp.stack([turn(right_ref[7 + c], 8 - z) for z in range(8)])
            if e == 0:
                rows = sum_rows(before, mid_ref[c, :, 0], mid_ref[c, :, 1], first_x, last_x)
            else:
                rows = sum_rows(mid_ref[c, :, 0], mid_ref[c, :, 1], after, first_x, last_x)
            got = finish(rows, faces)
            w.append(got)
            w_ref[c, :, e] = own_lanes(got)
        slope[e] = weigh(row_turns(w[0]), dcoef)
        along = sum_lanes(lanes_times(w[1], dy_ref[...]) * wy, first_y, last_y) * (mx * wx)
        t_ref[:, e] = along + z_slope(w[2]) * (mx * wx * my * wy)
    for e in range(2):
        faces = mid_ref[0, :, e]
        rows = sum_rows(slope[e - 1], slope[e], slope[e + 1], first_x, last_x)
        total = rows * (wx * my * wy) + t_ref[:, e]
        edges = []
        for z in range(8):
            got = total[z] * float(-node_weights[z])
            if z in (0, 7):
                face = wall(faces[z])
                got = jnp.where(inside > 0.5, got * face, face)
            b_ref[z, e] = got
            pack_ref[z, e] = own_lanes(got[None])[0]
            edges.append(jnp.where(half, got[:, :128], got[:, 128:]))
        for z in range(4):
            pack_ref[8 + z, e] = jnp.where(
                half, pltpu.roll(edges[z], 96, axis=1), pltpu.roll(edges[z + 4], 32, axis=1)
            )


def unpack(ref, z, e):
    lane = iota(128, 1)
    middle = pltpu.roll(ref[z, e], 64, axis=1)
    edge = pltpu.roll(ref[8 + z % 4, e], 32 if z < 4 else 96, axis=1)
    low = jnp.where(lane >= 64, middle, jnp.where(lane >= 32, edge, 0.0))
    high = jnp.where(lane < 64, middle, jnp.where(lane < 96, edge, 0.0))
    return jnp.concatenate([low, high], axis=1)


def fold(value):
    total = value[0]
    for z in range(1, 8):
        total = total + value[z]
    return total


def load_block(read, at, v_ref, p_ref, rim):
    for e in range(2):
        for z in range(8):
            got = read(z, e)
            if z in (0, 7):
                face = jnp.broadcast_to(got[0:1, :], got.shape)
                p_ref[z // 7, at + e] = jnp.where(rim, 0.0, face)
                got = jnp.where(rim, 0.0, got)
            v_ref[0, z, at + e] = got


def krylov_tools(ky_ref, v_ref, k_ref, p_ref):
    lanes = 256
    kcoef = row_coefs(lanes, scaled_stiff)
    wxy = node_x(lanes, node_weights) * node_y(lanes, node_weights)
    first_x, last_x, first_y, last_y = flags(lanes)

    def apply(j, e):
        v = v_ref[j, :, e]
        yk = lanes_times(v, ky_ref[...])
        xk = weigh(row_turns(v), kcoef)
        zk = depth([v[z] for z in range(8)], scaled_stiff, 1)
        for z in range(8):
            k_ref[j, z, e] = (xk[z] + zk[z] + yk[z]) * (wxy * float(node_weights[z] / span))

    def step(j, e):
        rows = sum_rows(
            k_ref[j, :, e - 1], k_ref[j, :, e], k_ref[j, :, e + 1], first_x, last_x
        )
        total = sum_lanes(rows, first_y, last_y)
        for z in range(8):
            image = total[z]
            if z in (0, 7):
                image = image * p_ref[z // 7, e]
            v_ref[j + 1, z, e] = image - 0.5 * v_ref[j, z, e]

    return apply, step


def over(low, high, body):
    count = high - low
    lax.fori_loop(
        low, high, lambda e, c: (body(e), c)[1], 0, unroll=count if count <= 4 else count // 2
    )


def sides(low, body):
    over(0, 4, lambda t: body(low + t + (t // 2) * (6 - 2 * low)))


def inner_kernel(left_ref, mid_ref, right_ref, ky_ref, v_ref, k_ref, acc_ref, p_ref):
    rim = rim_mask(256)
    load_block(lambda z, e: unpack(left_ref, z, e), 2, v_ref, p_ref, rim)
    load_block(lambda z, e: mid_ref[z, e], 4, v_ref, p_ref, rim)
    load_block(lambda z, e: unpack(right_ref, z, e), 6, v_ref, p_ref, rim)
    apply, step = krylov_tools(ky_ref, v_ref, k_ref, p_ref)
    slot = 0
    for j in range(3):
        over(2 + j, 8 - j, lambda e, j=j: apply(j, e))
        for i in range(j + 1):
            acc_ref[slot + i] = fold(v_ref[i, :, 4] * k_ref[j, :, 4]) + fold(
                v_ref[i, :, 5] * k_ref[j, :, 5]
            )
        acc_ref[6 + j] = fold(v_ref[j, :, 4] * v_ref[0, :, 4]) + fold(
            v_ref[j, :, 5] * v_ref[0, :, 5]
        )
        slot += j + 1
        if j < 2:
            over(3 + j, 7 - j, lambda e, j=j: step(j, e))


def outer_kernel(
    left_ref, right_ref, v_in, k_in, acc_ref, p_in, ky_ref, v_out, m_out, v_ref, k_ref, p_ref
):
    lanes = 256
    rim = rim_mask(lanes)
    load_block(lambda z, e: unpack(left_ref, z, e), 0, v_ref, p_ref, rim)
    load_block(lambda z, e: unpack(right_ref, z, e), 8, v_ref, p_ref, rim)
    for e in range(2, 8):
        p_ref[:, e] = p_in[:, e]
    for j, els in ((0, (2, 3, 4, 5, 6, 7)), (1, (3, 4, 5, 6)), (2, (4, 5))):
        for e in els:
            v_ref[j, :, e] = v_in[j, :, e]
            if j or e not in (4, 5):
                k_ref[j, :, e] = k_in[j, :, e]
    apply, step = krylov_tools(ky_ref, v_ref, k_ref, p_ref)
    for j in range(3):
        sides(j, lambda e, j=j: apply(j, e))
        if j < 2:
            sides(j + 1, lambda e, j=j: step(j, e))
        else:
            over(3, 7, lambda e: step(2, e))
    over(4, 6, lambda e: apply(3, e))
    for e in range(4):
        v_out[0, :, e] = v_ref[2, :, 3 + e]
        v_out[1, :, e] = v_ref[3, :, 3 + e]
    energy = [acc_ref[k] for k in range(6)]
    for i in range(ROUNDS):
        energy.append(
            fold(v_ref[i, :, 4] * k_ref[3, :, 4]) + fold(v_ref[i, :, 5] * k_ref[3, :, 5])
        )
    load = [acc_ref[6 + k] for k in range(3)]
    load.append(
        fold(v_ref[3, :, 4] * v_ref[0, :, 4]) + fold(v_ref[3, :, 5] * v_ref[0, :, 5])
    )
    lane = iota(lanes, 1)
    own = (lane >= 64) & (lane < 192)
    share = node_x(lanes, 1.0 / copies) * node_y(lanes, 1.0 / copies)
    lane = iota(128, 1)
    packed = jnp.zeros((8, 128), f32)
    for k, part in enumerate(energy + load):
        part = jnp.where(own, part, 0.0)
        if k >= 10:
            part = part * share
        part = part[:, :128] + part[:, 128:]
        total = jnp.sum(jnp.sum(part, axis=0, keepdims=True), axis=1, keepdims=True)
        packed = jnp.where(lane == k, total, packed)
    for k in range(m_out.shape[0] // 8):
        m_out[8 * k : 8 * k + 8] = packed


def final_kernel(m_ref, low_ref, high_ref, w_ref, open_ref, dy_ref, out_ref, q_ref):
    lanes = 256
    parts = [m_ref[8 * k : 8 * k + 8] for k in range(m_ref.shape[0] // 8)]
    while len(parts) > 1:
        odd = parts[len(parts) // 2 * 2 :]
        parts = [parts[k] + parts[k + 1] for k in range(0, len(parts) - 1, 2)] + odd
    sums = jnp.broadcast_to(jnp.sum(parts[0], axis=0, keepdims=True), (8, 128))
    lane = iota(128, 1)

    def moment(k):
        return jnp.sum(jnp.where(lane == k, sums, 0.0), axis=1, keepdims=True)

    e = {}
    slot = 0
    for j in range(ROUNDS):
        for i in range(j + 1):
            e[j, i] = moment(slot)
            slot += 1
    g = [moment(10 + j) for j in range(ROUNDS)]
    low, diag, scaled = {}, [], {}
    for j in range(ROUNDS):
        d = e[j, j]
        for k in range(j):
            d = d - low[j, k] * scaled[j, k]
        diag.append(d)
        for i in range(j + 1, ROUNDS):
            t = e[i, j]
            for k in range(j):
                t = t - scaled[i, k] * low[j, k]
            scaled[i, j] = t
            low[i, j] = t / d
    y = []
    for j in range(ROUNDS):
        t = g[j]
        for k in range(j):
            t = t - low[j, k] * y[k]
        y.append(t)
    c = [None] * ROUNDS
    for j in reversed(range(ROUNDS)):
        t = y[j] / diag[j]
        for k in range(j + 1, ROUNDS):
            t = t - low[k, j] * c[k]
        c[j] = t
    coef = [jnp.broadcast_to(t * (1.0 / span), (8, lanes)) for t in c]

    dcoef = row_coefs(lanes, deriv)
    first_x, last_x, first_y, last_y = flags(lanes)
    mean_x = node_x(lanes, 1.0 / copies)
    mean_y = node_y(lanes, 1.0 / copies)
    q, slope = [], []
    for e in range(4):
        got = low_ref[0, :, 3 + e] * coef[0] + low_ref[1, :, 3 + e] * coef[1]
        got = got + high_ref[0, :, e] * coef[2] + high_ref[1, :, e] * coef[3]
        q.append(got)
        slope.append(weigh(row_turns(got), dcoef))
    for e in range(2):
        here = q[e + 1]
        q_own = own_lanes(here)
        q_ref[:, e] = q_own
        along_x = sum_rows(slope[e], slope[e + 1], slope[e + 2], first_x, last_x) * mean_x
        along_y = sum_lanes(lanes_times(here, dy_ref[...]), first_y, last_y) * mean_y
        parts = [own_lanes(along_x), own_lanes(along_y), z_slope(q_own)]
        for i in range(3):
            for z in range(8):
                got = w_ref[i, z, e] - parts[i][z]
                if z in (0, 7):
                    got = got * open_ref[z // 7, e]
                out_ref[i, z, e] = got


def shape(*dims):
    return jax.ShapeDtypeStruct(dims, f32)


def call(kernel, out_shape, scratch, *args, space=pltpu.VMEM, vmem=48, cost=None):
    return pl.pallas_call(
        kernel,
        out_shape=out_shape,
        in_specs=[pl.BlockSpec(memory_space=space)] * len(args),
        out_specs=jax.tree.map(lambda s: pl.BlockSpec(memory_space=pltpu.VMEM), out_shape),
        scratch_shapes=scratch,
        cost_estimate=cost,
        compiler_params=pltpu.CompilerParams(vmem_limit_bytes=int(vmem * 2**20)),
    )(*args)


def shift(value, axis, by):
    size = lax.axis_size(axis)
    return lax.ppermute(value, axis, [(i, (i + by) % size) for i in range(size)])


def sum_groups(nx, ny):
    side = 4 if ny % 4 == 0 else 1
    near = [
        [(2 * z + c) * ny + x * side + y for y in range(side) for c in range(2)]
        for z in range(nx // 2)
        for x in range(ny // side)
    ]
    far = [
        [(2 * z + c) * ny + x * side + y for z in range(nx // 2) for x in range(ny // side)]
        for y in range(side)
        for c in range(2)
    ]
    return near, far


def total_rows(packed):
    near, far = sum_groups(lax.axis_size("gx"), lax.axis_size("gy"))
    both = ("gx", "gy")
    part = lax.all_to_all(packed, both, 0, 0, axis_index_groups=near, tiled=True)
    part = jnp.broadcast_to(jnp.sum(part, axis=0, keepdims=True), (len(far[0]), 128))
    return lax.all_to_all(part, both, 0, 0, axis_index_groups=far, tiled=True)


def local(adjoint, checkpoints, wall_faces):
    adj = adjoint.reshape(3, 8, 2, 8, 128)
    flow = checkpoints.reshape(3, 8, 16, 128)
    vm = pltpu.VMEM
    table = jax.ShapeDtypeStruct((256, 256), bf16)
    strip = shape(8, 2, 8, 128)
    rhs, up, down = call(
        rhs_kernel,
        (shape(3, 8, 2, 8, 128), strip, strip),
        [
            vm((3, 8, 2, 8, 128), f32),
            vm((3, 8, 16, 128), bf16),
            vm((2, 2, 16), jnp.int32),
            vm((3, 8, 2, 8, 128), f32),
            vm((2, 2, 8, 128), f32),
            vm((256, 256), bf16),
            vm((256, 256), bf16),
            pltpu.SemaphoreType.DMA((3,)),
        ],
        adj, flow, wall_faces,
        space=pl.ANY,
        vmem=62,
    )
    left = shift(up, "gy", 1)
    right = shift(down, "gy", -1)
    packet = shape(10, 8, 256)
    cost = pl.CostEstimate(flops=10**6, bytes_accessed=4 * 10**5, transcendentals=0)
    turned, dy, ky = call(
        hold_kernel, (shape(3, 8, 2, 8, 128), table, table), [], rhs, cost=cost
    )
    wide, up, down = call(
        join_kernel, (shape(3, 8, 2, 8, 256), packet, packet), [], turned, left, right
    )
    before = shift(up, "gx", 1)
    after = shift(down, "gx", -1)
    source, pack, moved, opened = call(
        source_kernel,
        (shape(8, 2, 8, 256), shape(12, 2, 8, 128), shape(3, 8, 2, 8, 128), shape(2, 2, 8, 128)),
        [vm((8, 2, 8, 256), f32)],
        before, wide, after, dy,
    )
    left = shift(pack, "gx", 1)
    right = shift(pack, "gx", -1)
    right, left = lax.optimization_barrier((right, left))
    left2 = shift(left, "gx", 1)
    right2 = shift(right, "gx", -1)
    cost = pl.CostEstimate(flops=5 * 10**6, bytes_accessed=4 * 10**6, transcendentals=0)
    low, images, acc, faces = call(
        inner_kernel,
        (
            shape(3, 8, 10, 8, 256),
            shape(3, 8, 10, 8, 256),
            shape(9, 8, 256),
            shape(2, 10, 8, 256),
        ),
        [],
        left, source, right, ky,
        cost=cost,
    )
    high, packed = call(
        outer_kernel,
        (shape(2, 8, 4, 8, 256), shape(len(sum_groups(lax.axis_size("gx"), lax.axis_size("gy"))[0][0]), 128)),
        [
            vm((4, 8, 10, 8, 256), f32),
            vm((4, 8, 10, 8, 256), f32),
            vm((2, 10, 8, 256), f32),
        ],
        left2, right2, low, images, acc, faces, ky,
    )
    velocity, pressure = call(
        final_kernel,
        (shape(3, 8, 2, 8, 128), shape(8, 2, 8, 128)),
        [],
        total_rows(packed), low, high, moved, opened, dy,
    )
    return velocity.reshape(3, 8, 16, 128), pressure.reshape(8, 16, 128)


def solution(mesh):
    return jax.shard_map(
        local,
        mesh=mesh,
        in_specs=(P(None, None, "gx", "gy"), P(None, None, None, "gx", "gy"), P(None, "gx", "gy")),
        out_specs=(P(None, None, "gx", "gy"), P(None, "gx", "gy")),
        check_vma=False,
    )
```

```python
import jax
import jax.numpy as jnp
import numpy as np
from jax import lax
from jax.experimental import pallas as pl
from jax.experimental.pallas import tpu as pltpu
from jax.sharding import PartitionSpec as P

f32 = jnp.float32
bf16 = jnp.bfloat16

node_points = np.array(
    [
        -1.0,
        -0.8717401485096066,
        -0.5917001814331423,
        -0.2092992179024789,
        0.2092992179024789,
        0.5917001814331423,
        0.8717401485096066,
        1.0,
    ]
)
node_weights = np.array(
    [
        0.03571428571428571,
        0.2107042271435061,
        0.3411226924835044,
        0.4124587946587038,
        0.4124587946587038,
        0.3411226924835044,
        0.2107042271435061,
        0.03571428571428571,
    ]
)
time_step = 0.05
viscosity = 0.02
span = 8.0
ROUNDS = 4


def derivative_table(points):
    identity = np.eye(points.shape[0])
    spacing = points[:, None] - points[None, :] + identity
    barycentric = 1.0 / np.prod(spacing, axis=1)
    matrix = barycentric[None, :] / barycentric[:, None] / spacing
    matrix = matrix * (1.0 - identity)
    return matrix - identity * np.sum(matrix, axis=1)[:, None]


deriv = derivative_table(node_points)
stiff = deriv.T @ np.diag(node_weights) @ deriv
copies = np.array([2.0, 1, 1, 1, 1, 1, 1, 2.0])
inverse_mass = 1.0 / (copies * node_weights)


scaled_stiff = stiff / node_weights[:, None]


def iota(lanes, dim):
    return lax.broadcasted_iota(jnp.int32, (8, lanes), dim)


def pick(place, values):
    out = jnp.full(place.shape, float(values[0]), f32)
    for k in range(1, 8):
        out = jnp.where(place == k, float(values[k]), out)
    return out


def node_x(lanes, values):
    return pick(iota(lanes, 0), values)


def node_y(lanes, values):
    return pick(iota(lanes, 1) & 7, values)


def rim_mask(lanes):
    a = iota(lanes, 0)
    b = iota(lanes, 1) & 7
    return (a == 0) | (a == 7) | (b == 0) | (b == 7)


def row_coefs(lanes, matrix):
    return [node_x(lanes, [matrix[a, (a - r) % 8] for a in range(8)]) for r in range(8)]


def row_turns(value):
    return [value] + [pltpu.roll(value, r, axis=1) for r in range(1, 8)]


def weigh(turns, coefs):
    out = turns[0] * coefs[0]
    for r in range(1, 8):
        out = out + turns[r] * coefs[r]
    return out


def depth(planes, matrix, sign):
    plus = [planes[k] + planes[7 - k] for k in range(4)]
    minus = [planes[k] - planes[7 - k] for k in range(4)]
    out = [None] * 8
    for a in range(4):
        even = plus[0] * float(0.5 * (matrix[a, 0] + matrix[a, 7]))
        odd = minus[0] * float(0.5 * (matrix[a, 0] - matrix[a, 7]))
        for k in range(1, 4):
            even = even + plus[k] * float(0.5 * (matrix[a, k] + matrix[a, 7 - k]))
            odd = odd + minus[k] * float(0.5 * (matrix[a, k] - matrix[a, 7 - k]))
        out[a] = even + odd
        out[7 - a] = even - odd if sign > 0 else odd - even
    return out


def z_slope(value):
    return jnp.stack(depth([value[z] for z in range(8)], deriv, -1))


def lane_table(matrix):
    lane = iota(128, 1)
    pattern = jnp.zeros((8, 128), f32)
    for b in range(8):
        pattern = jnp.where((lane & 7) == b, node_x(128, matrix[b]), pattern)
    full = jnp.concatenate([jnp.where(lane // 8 == k, pattern, 0.0) for k in range(16)], axis=0)
    high = full.astype(bf16)
    low = (full - high.astype(f32)).astype(bf16)
    pair = jnp.concatenate([high, low], axis=1)
    return jnp.concatenate([pair, pair], axis=0)


def lanes_times(value, table):
    n, _, lanes = value.shape
    blocks = [value[:, :, k * 128 : (k + 1) * 128].reshape(n * 8, 128) for k in range(lanes // 128)]
    rows = blocks[0] if len(blocks) == 1 else jnp.concatenate(blocks, axis=0)
    high = rows.astype(bf16)
    low = (rows - high.astype(f32)).astype(bf16)
    both = jnp.concatenate([high, low], axis=1)
    got = jnp.dot(both, table, preferred_element_type=f32)
    got = got[:, :128] + got[:, 128:]
    parts = [got[k * n * 8 : (k + 1) * n * 8].reshape(n, 8, 128) for k in range(lanes // 128)]
    return parts[0] if len(parts) == 1 else jnp.concatenate(parts, axis=2)


def sum_lanes(value, first, last):
    lanes = value.shape[2]
    return (
        value
        + last * pltpu.roll(value, lanes - 1, axis=2)
        + first * pltpu.roll(value, 1, axis=2)
    )


def sum_rows(before, here, after, first, last):
    return here + last * pltpu.roll(after, 7, axis=1) + first * pltpu.roll(before, 1, axis=1)


def own_lanes(value):
    n = value.shape[0]
    lane = lax.broadcasted_iota(jnp.int32, (n, 8, 128), 2)
    mixed = jnp.where(lane >= 64, value[:, :, :128], value[:, :, 128:])
    return pltpu.roll(mixed, 64, axis=2)


def expand_walls(faces_ref):
    spread = (
        lax.broadcasted_iota(jnp.int32, (16, 128), 1) // 8
        == lax.broadcasted_iota(jnp.int32, (16, 128), 0)
    ).astype(f32)
    out = []
    for face in range(2):
        rows = faces_ref[face].astype(f32)
        wide = jnp.dot(rows, spread, preferred_element_type=f32)
        out.append(wide)
    return out


def rhs_kernel(
    adj_hbm, flow_hbm, faces_hbm,
    r_ref, up_ref, down_ref,
    adj_ref, flow_ref, faces_ref, u_ref, wall_ref, dy_ref, ky_ref, sems,
):
    moves = [
        pltpu.make_async_copy(src, dst, sems.at[k])
        for k, (src, dst) in enumerate(
            ((adj_hbm, adj_ref), (flow_hbm, flow_ref), (faces_hbm, faces_ref))
        )
    ]
    for move in moves:
        move.start()
    lanes = 128
    dy_ref[...] = lane_table(deriv)
    ky_ref[...] = lane_table(scaled_stiff)
    dcoef = row_coefs(lanes, deriv)
    kcoef = row_coefs(lanes, scaled_stiff)
    wxy = node_x(lanes, node_weights) * node_y(lanes, node_weights)
    rim = rim_mask(lanes)
    lane = iota(lanes, 1)
    for move in moves:
        move.wait()
    for face, wide in enumerate(expand_walls(faces_ref)):
        for e in range(2):
            wall_ref[face, e] = jnp.broadcast_to(wide[e : e + 1], (8, lanes))
    for c in range(3):
        for z in range(8):
            rows = flow_ref[c, z].astype(f32)
            u_ref[c, z, 0] = rows[:8]
            u_ref[c, z, 1] = rows[8:]

    def body(e, carry):
        v = [adj_ref[c, :, e] for c in range(3)]
        u = [u_ref[c, :, e] for c in range(3)]
        vall = jnp.concatenate(v, axis=0)
        uall = jnp.concatenate(u, axis=0)
        vdy = lanes_times(vall, dy_ref[...])
        vky = lanes_times(vall, ky_ref[...])
        udy = lanes_times(uall, dy_ref[...])
        stretch = [jnp.zeros((8, 8, lanes), f32)] * 3
        for j in range(3):
            stretch[0] = stretch[0] + v[j] * weigh(row_turns(u[j]), dcoef)
            stretch[1] = stretch[1] + v[j] * udy[8 * j : 8 * j + 8]
            stretch[2] = stretch[2] + v[j] * z_slope(u[j])
        ups, downs = [None] * 8, [None] * 8
        for i in range(3):
            turns = row_turns(v[i])
            planes = [v[i][z] for z in range(8)]
            zd = depth(planes, deriv, -1)
            zk = depth(planes, scaled_stiff, 1)
            xd = weigh(turns, dcoef)
            xk = weigh(turns, kcoef)
            made = []
            for z in range(8):
                wz = float(node_weights[z])
                adv = (
                    u[0][z] * xd[z]
                    + u[1][z] * vdy[8 * i + z]
                    + u[2][z] * zd[z]
                    - stretch[i][z]
                )
                bend = xk[z] + vky[8 * i + z] + zk[z]
                out = (wxy * wz) * (v[i][z] + time_step * adv - (time_step * viscosity) * bend)
                if i == 0 and z in (0, 7):
                    out = jnp.where(rim, wall_ref[z // 7, e], out)
                r_ref[i, z, e] = out
                made.append(out)
            for z in range(8):
                up, down = made[z], made[z]
                if 0 < z < 7:
                    up = up + jnp.where(lane == 88, pltpu.roll(up, 1, axis=1), 0.0)
                    down = down + jnp.where(lane == 39, pltpu.roll(down, 127, axis=1), 0.0)
                up = pltpu.roll(up, (40 * i - 88) % 128, axis=1)
                down = pltpu.roll(down, 40 * i, axis=1) if i else down
                here = (lane >= 40 * i) & (lane < 40 * i + 40)
                ups[z] = up if i == 0 else jnp.where(here, up, ups[z])
                downs[z] = down if i == 0 else jnp.where(here, down, downs[z])
        for z in range(8):
            up_ref[z, e] = ups[z]
            down_ref[z, e] = downs[z]
        return carry

    lax.fori_loop(0, 2, body, 0, unroll=2)


def hold_kernel(r_ref, turned_ref, dy_ref, ky_ref):
    dy_ref[...] = lane_table(deriv)
    ky_ref[...] = lane_table(scaled_stiff)
    for c in range(3):
        for z in range(8):
            for e in range(2):
                turned_ref[c, z, e] = pltpu.roll(r_ref[c, z, e], 64, axis=1)


def join_kernel(r_ref, left_ref, right_ref, e_ref, up_ref, down_ref):
    lane = iota(128, 1)
    half = lane < 64
    place = iota(256, 0)
    first = place == 0
    last = place == 7
    for c in range(3):
        faces_up = jnp.zeros((8, 256), f32)
        faces_down = jnp.zeros((8, 256), f32)
        for z in range(8):
            tiles = []
            for e in range(2):
                turned = r_ref[c, z, e]
                left = pltpu.roll(left_ref[z, e], (24 - 40 * c) % 128, axis=1)
                right = pltpu.roll(right_ref[z, e], (64 - 40 * c) % 128, axis=1)
                tile = jnp.concatenate(
                    [
                        jnp.where(half, jnp.where(lane >= 24, left, 0.0), turned),
                        jnp.where(half, turned, jnp.where(lane < 104, right, 0.0)),
                    ],
                    axis=1,
                )
                e_ref[c, z, e] = tile
                tiles.append(tile)
            if c == 0:
                go_up, go_down = tiles[1], tiles[0]
                if 0 < z < 7:
                    go_up = go_up + jnp.where(first, pltpu.roll(tiles[0], 1, axis=0), 0.0)
                    go_down = go_down + jnp.where(last, pltpu.roll(tiles[1], 7, axis=0), 0.0)
                up_ref[z] = go_up
                down_ref[z] = go_down
            else:
                turned = pltpu.roll(tiles[1], (z + 1) % 8, axis=0) if z < 7 else tiles[1]
                faces_up = jnp.where(place == z, turned, faces_up)
                turned = pltpu.roll(tiles[0], z, axis=0) if z else tiles[0]
                faces_down = jnp.where(place == z, turned, faces_down)
        if c:
            up_ref[7 + c] = faces_up
            down_ref[7 + c] = faces_down


def flags(lanes):
    first_x = (iota(lanes, 0) == 0).astype(f32)
    last_x = (iota(lanes, 0) == 7).astype(f32)
    first_y = ((iota(lanes, 1) & 7) == 0).astype(f32)
    last_y = ((iota(lanes, 1) & 7) == 7).astype(f32)
    return first_x, last_x, first_y, last_y


def source_kernel(left_ref, mid_ref, right_ref, dy_ref, b_ref, pack_ref, w_ref, open_ref, t_ref):
    lanes = 256
    dcoef = row_coefs(lanes, deriv)
    wx = node_x(lanes, node_weights)
    wy = node_y(lanes, node_weights)
    mx = node_x(lanes, copies)
    my = node_y(lanes, copies)
    inv = node_x(lanes, inverse_mass) * node_y(lanes, inverse_mass)
    first_x, last_x, first_y, last_y = flags(lanes)
    inside = 1.0 - rim_mask(lanes).astype(f32)
    half = iota(128, 1) < 64

    def wall(tile):
        return jnp.broadcast_to(tile[0:1, :], (8, lanes))

    def finish(rows, faces):
        total = sum_lanes(rows, first_y, last_y)
        planes = []
        for z in range(8):
            got = total[z] * (inv * float(1.0 / node_weights[z]))
            if z in (0, 7):
                got = got * (inside * (1.0 - wall(faces[z])))
            planes.append(got)
        return jnp.stack(planes)

    def turn(tile, by):
        by = by % 8
        return pltpu.roll(tile, by, axis=0) if by else tile

    slope = {}
    left = left_ref[0:8]
    right = right_ref[0:8]
    near = finish(left + last_x * pltpu.roll(mid_ref[0, :, 0], 7, axis=1), left)
    slope[-1] = weigh(row_turns(near), dcoef)
    near = finish(right + first_x * pltpu.roll(mid_ref[0, :, 1], 1, axis=1), right)
    slope[2] = weigh(row_turns(near), dcoef)
    for e in range(2):
        faces = mid_ref[0, :, e]
        for face in range(2):
            open_face = inside * (1.0 - wall(faces[7 * face]))
            open_ref[face, e] = own_lanes(open_face[None])[0]
        w = []
        for c in range(3):
            if c == 0:
                before, after = left, right
            else:
                before = jnp.stack([turn(left_ref[7 + c], 7 - z) for z in range(8)])
                after = jnp.stack([turn(right_ref[7 + c], 8 - z) for z in range(8)])
            if e == 0:
                rows = sum_rows(before, mid_ref[c, :, 0], mid_ref[c, :, 1], first_x, last_x)
            else:
                rows = sum_rows(mid_ref[c, :, 0], mid_ref[c, :, 1], after, first_x, last_x)
            got = finish(rows, faces)
            w.append(got)
            w_ref[c, :, e] = own_lanes(got)
        slope[e] = weigh(row_turns(w[0]), dcoef)
        along = sum_lanes(lanes_times(w[1], dy_ref[...]) * wy, first_y, last_y) * (mx * wx)
        t_ref[:, e] = along + z_slope(w[2]) * (mx * wx * my * wy)
    for e in range(2):
        faces = mid_ref[0, :, e]
        rows = sum_rows(slope[e - 1], slope[e], slope[e + 1], first_x, last_x)
        total = rows * (wx * my * wy) + t_ref[:, e]
        edges = []
        for z in range(8):
            got = total[z] * float(-node_weights[z])
            if z in (0, 7):
                face = wall(faces[z])
                got = jnp.where(inside > 0.5, got * face, face)
            b_ref[z, e] = got
            pack_ref[z, e] = own_lanes(got[None])[0]
            edges.append(jnp.where(half, got[:, :128], got[:, 128:]))
        for z in range(4):
            pack_ref[8 + z, e] = jnp.where(
                half, pltpu.roll(edges[z], 96, axis=1), pltpu.roll(edges[z + 4], 32, axis=1)
            )


def unpack(ref, z, e):
    lane = iota(128, 1)
    middle = pltpu.roll(ref[z, e], 64, axis=1)
    edge = pltpu.roll(ref[8 + z % 4, e], 32 if z < 4 else 96, axis=1)
    low = jnp.where(lane >= 64, middle, jnp.where(lane >= 32, edge, 0.0))
    high = jnp.where(lane < 64, middle, jnp.where(lane < 96, edge, 0.0))
    return jnp.concatenate([low, high], axis=1)


def fold(value):
    total = value[0]
    for z in range(1, 8):
        total = total + value[z]
    return total


def load_block(read, at, v_ref, p_ref, rim):
    for e in range(2):
        for z in range(8):
            got = read(z, e)
            if z in (0, 7):
                face = jnp.broadcast_to(got[0:1, :], got.shape)
                p_ref[z // 7, at + e] = jnp.where(rim, 0.0, face)
                got = jnp.where(rim, 0.0, got)
            v_ref[0, z, at + e] = got


def krylov_tools(ky_ref, v_ref, k_ref, p_ref):
    lanes = 256
    kcoef = row_coefs(lanes, scaled_stiff)
    wxy = node_x(lanes, node_weights) * node_y(lanes, node_weights)
    first_x, last_x, first_y, last_y = flags(lanes)

    def apply(j, e):
        v = v_ref[j, :, e]
        yk = lanes_times(v, ky_ref[...])
        xk = weigh(row_turns(v), kcoef)
        zk = depth([v[z] for z in range(8)], scaled_stiff, 1)
        for z in range(8):
            k_ref[j, z, e] = (xk[z] + zk[z] + yk[z]) * (wxy * float(node_weights[z] / span))

    def step(j, e):
        rows = sum_rows(
            k_ref[j, :, e - 1], k_ref[j, :, e], k_ref[j, :, e + 1], first_x, last_x
        )
        total = sum_lanes(rows, first_y, last_y)
        for z in range(8):
            image = total[z]
            if z in (0, 7):
                image = image * p_ref[z // 7, e]
            v_ref[j + 1, z, e] = image - 0.5 * v_ref[j, z, e]

    return apply, step


def over(low, high, body):
    count = high - low
    lax.fori_loop(
        low, high, lambda e, c: (body(e), c)[1], 0, unroll=count if count <= 4 else count // 2
    )


def sides(low, body):
    over(0, 4, lambda t: body(low + t + (t // 2) * (6 - 2 * low)))


def pack_sums(parts, packed):
    lane = iota(256, 1)
    own = (lane >= 64) & (lane < 192)
    share = node_x(256, 1.0 / copies) * node_y(256, 1.0 / copies)
    lane = iota(128, 1)
    for k, part in parts.items():
        part = jnp.where(own, part, 0.0)
        if k >= 10:
            part = part * share
        part = part[:, :128] + part[:, 128:]
        total = jnp.sum(jnp.sum(part, axis=0, keepdims=True), axis=1, keepdims=True)
        packed = jnp.where(lane == k, total, packed)
    return packed


def own_product(former, latter):
    return fold(former(4) * latter(4)) + fold(former(5) * latter(5))


def inner_kernel(left_ref, mid_ref, right_ref, ky_ref, v_ref, k_ref, p_ref, sum_ref):
    rim = rim_mask(256)
    load_block(lambda z, e: unpack(left_ref, z, e), 2, v_ref, p_ref, rim)
    load_block(lambda z, e: mid_ref[z, e], 4, v_ref, p_ref, rim)
    load_block(lambda z, e: unpack(right_ref, z, e), 6, v_ref, p_ref, rim)
    apply, step = krylov_tools(ky_ref, v_ref, k_ref, p_ref)
    parts = {}
    for j in range(3):
        over(2 + j, 8 - j, lambda e, j=j: apply(j, e))
        for i in range(j + 1):
            parts[j * (j + 1) // 2 + i] = own_product(
                lambda e, i=i: v_ref[i, :, e], lambda e, j=j: k_ref[j, :, e]
            )
        parts[10 + j] = own_product(lambda e, j=j: v_ref[j, :, e], lambda e: v_ref[0, :, e])
        if j < 2:
            over(3 + j, 7 - j, lambda e, j=j: step(j, e))
    sum_ref[...] = pack_sums(parts, jnp.zeros((8, 128), f32))


def outer_kernel(
    left_ref, right_ref, sum_ref, ky_ref, v_in, k_in, p_in, v_ref, k_ref, p_ref, m_out
):
    rim = rim_mask(256)
    load_block(lambda z, e: unpack(left_ref, z, e), 0, v_ref, p_ref, rim)
    load_block(lambda z, e: unpack(right_ref, z, e), 8, v_ref, p_ref, rim)
    apply, step = krylov_tools(ky_ref, v_ref, k_ref, p_ref)
    for j in range(3):
        sides(j, lambda e, j=j: apply(j, e))
        if j < 2:
            sides(j + 1, lambda e, j=j: step(j, e))
        else:
            over(3, 7, lambda e: step(2, e))
    over(4, 6, lambda e: apply(3, e))
    parts = {}
    for i in range(ROUNDS):
        parts[6 + i] = own_product(lambda e, i=i: v_ref[i, :, e], lambda e: k_ref[3, :, e])
    parts[13] = own_product(lambda e: v_ref[3, :, e], lambda e: v_ref[0, :, e])
    packed = pack_sums(parts, sum_ref[...])
    for k in range(m_out.shape[0] // 8):
        m_out[8 * k : 8 * k + 8] = packed


def final_kernel(m_ref, v_ref, w_ref, open_ref, dy_ref, out_ref, q_ref):
    lanes = 256
    parts = [m_ref[8 * k : 8 * k + 8] for k in range(m_ref.shape[0] // 8)]
    while len(parts) > 1:
        odd = parts[len(parts) // 2 * 2 :]
        parts = [parts[k] + parts[k + 1] for k in range(0, len(parts) - 1, 2)] + odd
    sums = jnp.broadcast_to(jnp.sum(parts[0], axis=0, keepdims=True), (8, 128))
    lane = iota(128, 1)

    def moment(k):
        return jnp.sum(jnp.where(lane == k, sums, 0.0), axis=1, keepdims=True)

    e = {}
    slot = 0
    for j in range(ROUNDS):
        for i in range(j + 1):
            e[j, i] = moment(slot)
            slot += 1
    g = [moment(10 + j) for j in range(ROUNDS)]
    low, diag, scaled = {}, [], {}
    for j in range(ROUNDS):
        d = e[j, j]
        for k in range(j):
            d = d - low[j, k] * scaled[j, k]
        diag.append(d)
        for i in range(j + 1, ROUNDS):
            t = e[i, j]
            for k in range(j):
                t = t - scaled[i, k] * low[j, k]
            scaled[i, j] = t
            low[i, j] = t / d
    y = []
    for j in range(ROUNDS):
        t = g[j]
        for k in range(j):
            t = t - low[j, k] * y[k]
        y.append(t)
    c = [None] * ROUNDS
    for j in reversed(range(ROUNDS)):
        t = y[j] / diag[j]
        for k in range(j + 1, ROUNDS):
            t = t - low[k, j] * c[k]
        c[j] = t
    coef = [jnp.broadcast_to(t * (1.0 / span), (8, lanes)) for t in c]

    dcoef = row_coefs(lanes, deriv)
    first_x, last_x, first_y, last_y = flags(lanes)
    mean_x = node_x(lanes, 1.0 / copies)
    mean_y = node_y(lanes, 1.0 / copies)
    q, slope = [], []
    for e in range(4):
        got = v_ref[0, :, 3 + e] * coef[0]
        for j in range(1, ROUNDS):
            got = got + v_ref[j, :, 3 + e] * coef[j]
        q.append(got)
        slope.append(weigh(row_turns(got), dcoef))
    for e in range(2):
        here = q[e + 1]
        q_own = own_lanes(here)
        q_ref[:, e] = q_own
        along_x = sum_rows(slope[e], slope[e + 1], slope[e + 2], first_x, last_x) * mean_x
        along_y = sum_lanes(lanes_times(here, dy_ref[...]), first_y, last_y) * mean_y
        parts = [own_lanes(along_x), own_lanes(along_y), z_slope(q_own)]
        for i in range(3):
            for z in range(8):
                got = w_ref[i, z, e] - parts[i][z]
                if z in (0, 7):
                    got = got * open_ref[z // 7, e]
                out_ref[i, z, e] = got


def shape(*dims):
    return jax.ShapeDtypeStruct(dims, f32)


def call(kernel, out_shape, scratch, *args, space=pltpu.VMEM, vmem=48, cost=None, aliases={}):
    return pl.pallas_call(
        kernel,
        out_shape=out_shape,
        in_specs=[pl.BlockSpec(memory_space=space)] * len(args),
        out_specs=jax.tree.map(lambda s: pl.BlockSpec(memory_space=pltpu.VMEM), out_shape),
        scratch_shapes=scratch,
        cost_estimate=cost,
        input_output_aliases=aliases,
        compiler_params=pltpu.CompilerParams(vmem_limit_bytes=int(vmem * 2**20)),
    )(*args)


def shift(value, axis, by):
    size = lax.axis_size(axis)
    return lax.ppermute(value, axis, [(i, (i + by) % size) for i in range(size)])


def total_rows(packed):
    nx, ny = lax.axis_size("gx"), lax.axis_size("gy")
    planes = [[(2 * z + c) * ny + y for y in range(ny) for c in range(2)] for z in range(nx // 2)]
    part = lax.all_to_all(packed, ("gx", "gy"), 0, 0, axis_index_groups=planes, tiled=True)
    part = jnp.broadcast_to(jnp.sum(part, axis=0, keepdims=True), (nx // 2, 128))
    along = [[2 * z + c for z in range(nx // 2)] for c in range(2)]
    return lax.all_to_all(part, "gx", 0, 0, axis_index_groups=along, tiled=True)


def local(adjoint, checkpoints, wall_faces):
    adj = adjoint.reshape(3, 8, 2, 8, 128)
    flow = checkpoints.reshape(3, 8, 16, 128)
    vm = pltpu.VMEM
    table = jax.ShapeDtypeStruct((256, 256), bf16)
    strip = shape(8, 2, 8, 128)
    rhs, up, down = call(
        rhs_kernel,
        (shape(3, 8, 2, 8, 128), strip, strip),
        [
            vm((3, 8, 2, 8, 128), f32),
            vm((3, 8, 16, 128), bf16),
            vm((2, 2, 16), jnp.int32),
            vm((3, 8, 2, 8, 128), f32),
            vm((2, 2, 8, 128), f32),
            vm((256, 256), bf16),
            vm((256, 256), bf16),
            pltpu.SemaphoreType.DMA((3,)),
        ],
        adj, flow, wall_faces,
        space=pl.ANY,
        vmem=62,
    )
    left = shift(up, "gy", 1)
    right = shift(down, "gy", -1)
    packet = shape(10, 8, 256)
    cost = pl.CostEstimate(flops=10**6, bytes_accessed=4 * 10**5, transcendentals=0)
    turned, dy, ky = call(
        hold_kernel, (shape(3, 8, 2, 8, 128), table, table), [], rhs, cost=cost
    )
    wide, up, down = call(
        join_kernel, (shape(3, 8, 2, 8, 256), packet, packet), [], turned, left, right
    )
    before = shift(up, "gx", 1)
    after = shift(down, "gx", -1)
    source, pack, moved, opened = call(
        source_kernel,
        (shape(8, 2, 8, 256), shape(12, 2, 8, 128), shape(3, 8, 2, 8, 128), shape(2, 2, 8, 128)),
        [vm((8, 2, 8, 256), f32)],
        before, wide, after, dy,
    )
    left = shift(pack, "gx", 1)
    right = shift(pack, "gx", -1)
    right, left = lax.optimization_barrier((right, left))
    left2 = shift(left, "gx", 1)
    right2 = shift(right, "gx", -1)
    cost = pl.CostEstimate(flops=5 * 10**6, bytes_accessed=4 * 10**6, transcendentals=0)
    state = (shape(4, 8, 10, 8, 256), shape(4, 8, 10, 8, 256), shape(2, 10, 8, 256))
    basis, images, faces, known = call(
        inner_kernel, state + (shape(8, 128),), [], left, source, right, ky, cost=cost
    )
    basis, images, faces, packed = call(
        outer_kernel,
        state + (shape(2 * lax.axis_size("gy"), 128),),
        [],
        left2, right2, known, ky, basis, images, faces,
        aliases={4: 0, 5: 1, 6: 2},
    )
    velocity, pressure = call(
        final_kernel,
        (shape(3, 8, 2, 8, 128), shape(8, 2, 8, 128)),
        [],
        total_rows(packed), basis, moved, opened, dy,
    )
    return velocity.reshape(3, 8, 16, 128), pressure.reshape(8, 16, 128)


def solution(mesh):
    return jax.shard_map(
        local,
        mesh=mesh,
        in_specs=(P(None, None, "gx", "gy"), P(None, None, None, "gx", "gy"), P(None, "gx", "gy")),
        out_specs=(P(None, None, "gx", "gy"), P(None, "gx", "gy")),
        check_vma=False,
    )
```

```python
import jax
import jax.numpy as jnp
import numpy as np
from jax import lax
from jax.experimental import pallas as pl
from jax.experimental.pallas import tpu as pltpu
from jax.sharding import PartitionSpec as P

f32 = jnp.float32
bf16 = jnp.bfloat16

node_points = np.array(
    [
        -1.0,
        -0.8717401485096066,
        -0.5917001814331423,
        -0.2092992179024789,
        0.2092992179024789,
        0.5917001814331423,
        0.8717401485096066,
        1.0,
    ]
)
node_weights = np.array(
    [
        0.03571428571428571,
        0.2107042271435061,
        0.3411226924835044,
        0.4124587946587038,
        0.4124587946587038,
        0.3411226924835044,
        0.2107042271435061,
        0.03571428571428571,
    ]
)
time_step = 0.05
viscosity = 0.02
span = 8.0
ROUNDS = 4


def derivative_table(points):
    identity = np.eye(points.shape[0])
    spacing = points[:, None] - points[None, :] + identity
    barycentric = 1.0 / np.prod(spacing, axis=1)
    matrix = barycentric[None, :] / barycentric[:, None] / spacing
    matrix = matrix * (1.0 - identity)
    return matrix - identity * np.sum(matrix, axis=1)[:, None]


deriv = derivative_table(node_points)
stiff = deriv.T @ np.diag(node_weights) @ deriv
copies = np.array([2.0, 1, 1, 1, 1, 1, 1, 2.0])
inverse_mass = 1.0 / (copies * node_weights)


scaled_stiff = stiff / node_weights[:, None]


def iota(lanes, dim):
    return lax.broadcasted_iota(jnp.int32, (8, lanes), dim)


def pick(place, values):
    out = jnp.full(place.shape, float(values[0]), f32)
    for k in range(1, 8):
        out = jnp.where(place == k, float(values[k]), out)
    return out


def node_x(lanes, values):
    return pick(iota(lanes, 0), values)


def node_y(lanes, values):
    return pick(iota(lanes, 1) & 7, values)


def rim_mask(lanes):
    a = iota(lanes, 0)
    b = iota(lanes, 1) & 7
    return (a == 0) | (a == 7) | (b == 0) | (b == 7)


def row_coefs(lanes, matrix):
    return [node_x(lanes, [matrix[a, (a - r) % 8] for a in range(8)]) for r in range(8)]


def row_turns(value):
    return [value] + [pltpu.roll(value, r, axis=1) for r in range(1, 8)]


def weigh(turns, coefs):
    out = turns[0] * coefs[0]
    for r in range(1, 8):
        out = out + turns[r] * coefs[r]
    return out


def depth(planes, matrix, sign):
    plus = [planes[k] + planes[7 - k] for k in range(4)]
    minus = [planes[k] - planes[7 - k] for k in range(4)]
    out = [None] * 8
    for a in range(4):
        even = plus[0] * float(0.5 * (matrix[a, 0] + matrix[a, 7]))
        odd = minus[0] * float(0.5 * (matrix[a, 0] - matrix[a, 7]))
        for k in range(1, 4):
            even = even + plus[k] * float(0.5 * (matrix[a, k] + matrix[a, 7 - k]))
            odd = odd + minus[k] * float(0.5 * (matrix[a, k] - matrix[a, 7 - k]))
        out[a] = even + odd
        out[7 - a] = even - odd if sign > 0 else odd - even
    return out


def z_slope(value):
    return jnp.stack(depth([value[z] for z in range(8)], deriv, -1))


def lane_table(matrix):
    lane = iota(128, 1)
    pattern = jnp.zeros((8, 128), f32)
    for b in range(8):
        pattern = jnp.where((lane & 7) == b, node_x(128, matrix[b]), pattern)
    full = jnp.concatenate([jnp.where(lane // 8 == k, pattern, 0.0) for k in range(16)], axis=0)
    high = full.astype(bf16)
    low = (full - high.astype(f32)).astype(bf16)
    pair = jnp.concatenate([high, low], axis=1)
    return jnp.concatenate([pair, pair], axis=0)


def lanes_times(value, table):
    n, _, lanes = value.shape
    blocks = [value[:, :, k * 128 : (k + 1) * 128].reshape(n * 8, 128) for k in range(lanes // 128)]
    rows = blocks[0] if len(blocks) == 1 else jnp.concatenate(blocks, axis=0)
    high = rows.astype(bf16)
    low = (rows - high.astype(f32)).astype(bf16)
    both = jnp.concatenate([high, low], axis=1)
    got = jnp.dot(both, table, preferred_element_type=f32)
    got = got[:, :128] + got[:, 128:]
    parts = [got[k * n * 8 : (k + 1) * n * 8].reshape(n, 8, 128) for k in range(lanes // 128)]
    return parts[0] if len(parts) == 1 else jnp.concatenate(parts, axis=2)


def sum_lanes(value, first, last):
    lanes = value.shape[2]
    return (
        value
        + last * pltpu.roll(value, lanes - 1, axis=2)
        + first * pltpu.roll(value, 1, axis=2)
    )


def sum_rows(before, here, after, first, last):
    return here + last * pltpu.roll(after, 7, axis=1) + first * pltpu.roll(before, 1, axis=1)


def own_lanes(value):
    n = value.shape[0]
    lane = lax.broadcasted_iota(jnp.int32, (n, 8, 128), 2)
    mixed = jnp.where(lane >= 64, value[:, :, :128], value[:, :, 128:])
    return pltpu.roll(mixed, 64, axis=2)


def expand_walls(faces_ref):
    spread = (
        lax.broadcasted_iota(jnp.int32, (16, 128), 1) // 8
        == lax.broadcasted_iota(jnp.int32, (16, 128), 0)
    ).astype(f32)
    out = []
    for face in range(2):
        rows = faces_ref[face].astype(f32)
        wide = jnp.dot(rows, spread, preferred_element_type=f32)
        out.append(wide)
    return out


def rhs_kernel(
    adj_hbm, flow_hbm, faces_hbm,
    r_ref, up_ref, down_ref,
    adj_ref, flow_ref, faces_ref, u_ref, wall_ref, dy_ref, ky_ref, sems,
):
    moves = [
        pltpu.make_async_copy(src, dst, sems.at[k])
        for k, (src, dst) in enumerate(
            ((adj_hbm, adj_ref), (flow_hbm, flow_ref), (faces_hbm, faces_ref))
        )
    ]
    for move in moves:
        move.start()
    lanes = 128
    dy_ref[...] = lane_table(deriv)
    ky_ref[...] = lane_table(scaled_stiff)
    dcoef = row_coefs(lanes, deriv)
    kcoef = row_coefs(lanes, scaled_stiff)
    wxy = node_x(lanes, node_weights) * node_y(lanes, node_weights)
    rim = rim_mask(lanes)
    lane = iota(lanes, 1)
    for move in moves:
        move.wait()
    for face, wide in enumerate(expand_walls(faces_ref)):
        for e in range(2):
            wall_ref[face, e] = jnp.broadcast_to(wide[e : e + 1], (8, lanes))
    for c in range(3):
        for z in range(8):
            rows = flow_ref[c, z].astype(f32)
            u_ref[c, z, 0] = rows[:8]
            u_ref[c, z, 1] = rows[8:]

    def body(e, carry):
        v = [adj_ref[c, :, e] for c in range(3)]
        u = [u_ref[c, :, e] for c in range(3)]
        vall = jnp.concatenate(v, axis=0)
        uall = jnp.concatenate(u, axis=0)
        vdy = lanes_times(vall, dy_ref[...])
        vky = lanes_times(vall, ky_ref[...])
        udy = lanes_times(uall, dy_ref[...])
        stretch = [jnp.zeros((8, 8, lanes), f32)] * 3
        for j in range(3):
            stretch[0] = stretch[0] + v[j] * weigh(row_turns(u[j]), dcoef)
            stretch[1] = stretch[1] + v[j] * udy[8 * j : 8 * j + 8]
            stretch[2] = stretch[2] + v[j] * z_slope(u[j])
        ups, downs = [None] * 8, [None] * 8
        for i in range(3):
            turns = row_turns(v[i])
            planes = [v[i][z] for z in range(8)]
            zd = depth(planes, deriv, -1)
            zk = depth(planes, scaled_stiff, 1)
            xd = weigh(turns, dcoef)
            xk = weigh(turns, kcoef)
            made = []
            for z in range(8):
                wz = float(node_weights[z])
                adv = (
                    u[0][z] * xd[z]
                    + u[1][z] * vdy[8 * i + z]
                    + u[2][z] * zd[z]
                    - stretch[i][z]
                )
                bend = xk[z] + vky[8 * i + z] + zk[z]
                out = (wxy * wz) * (v[i][z] + time_step * adv - (time_step * viscosity) * bend)
                if i == 0 and z in (0, 7):
                    out = jnp.where(rim, wall_ref[z // 7, e], out)
                r_ref[i, z, e] = out
                made.append(out)
            for z in range(8):
                up, down = made[z], made[z]
                if 0 < z < 7:
                    up = up + jnp.where(lane == 88, pltpu.roll(up, 1, axis=1), 0.0)
                    down = down + jnp.where(lane == 39, pltpu.roll(down, 127, axis=1), 0.0)
                up = pltpu.roll(up, (40 * i - 88) % 128, axis=1)
                down = pltpu.roll(down, 40 * i, axis=1) if i else down
                here = (lane >= 40 * i) & (lane < 40 * i + 40)
                ups[z] = up if i == 0 else jnp.where(here, up, ups[z])
                downs[z] = down if i == 0 else jnp.where(here, down, downs[z])
        for z in range(8):
            up_ref[z, e] = ups[z]
            down_ref[z, e] = downs[z]
        return carry

    lax.fori_loop(0, 2, body, 0, unroll=2)


def hold_kernel(r_ref, turned_ref, dy_ref, ky_ref):
    dy_ref[...] = lane_table(deriv)
    ky_ref[...] = lane_table(scaled_stiff)
    for c in range(3):
        for z in range(8):
            for e in range(2):
                turned_ref[c, z, e] = pltpu.roll(r_ref[c, z, e], 64, axis=1)


def join_kernel(r_ref, left_ref, right_ref, e_ref, up_ref, down_ref):
    lane = iota(128, 1)
    half = lane < 64
    place = iota(256, 0)
    first = place == 0
    last = place == 7
    for c in range(3):
        faces_up = jnp.zeros((8, 256), f32)
        faces_down = jnp.zeros((8, 256), f32)
        for z in range(8):
            tiles = []
            for e in range(2):
                turned = r_ref[c, z, e]
                left = pltpu.roll(left_ref[z, e], (24 - 40 * c) % 128, axis=1)
                right = pltpu.roll(right_ref[z, e], (64 - 40 * c) % 128, axis=1)
                tile = jnp.concatenate(
                    [
                        jnp.where(half, jnp.where(lane >= 24, left, 0.0), turned),
                        jnp.where(half, turned, jnp.where(lane < 104, right, 0.0)),
                    ],
                    axis=1,
                )
                e_ref[c, z, e] = tile
                tiles.append(tile)
            if c == 0:
                go_up, go_down = tiles[1], tiles[0]
                if 0 < z < 7:
                    go_up = go_up + jnp.where(first, pltpu.roll(tiles[0], 1, axis=0), 0.0)
                    go_down = go_down + jnp.where(last, pltpu.roll(tiles[1], 7, axis=0), 0.0)
                up_ref[z] = go_up
                down_ref[z] = go_down
            else:
                turned = pltpu.roll(tiles[1], (z + 1) % 8, axis=0) if z < 7 else tiles[1]
                faces_up = jnp.where(place == z, turned, faces_up)
                turned = pltpu.roll(tiles[0], z, axis=0) if z else tiles[0]
                faces_down = jnp.where(place == z, turned, faces_down)
        if c:
            up_ref[7 + c] = faces_up
            down_ref[7 + c] = faces_down


def flags(lanes):
    first_x = (iota(lanes, 0) == 0).astype(f32)
    last_x = (iota(lanes, 0) == 7).astype(f32)
    first_y = ((iota(lanes, 1) & 7) == 0).astype(f32)
    last_y = ((iota(lanes, 1) & 7) == 7).astype(f32)
    return first_x, last_x, first_y, last_y


def source_kernel(left_ref, mid_ref, right_ref, dy_ref, b_ref, pack_ref, w_ref, open_ref, t_ref):
    lanes = 256
    dcoef = row_coefs(lanes, deriv)
    wx = node_x(lanes, node_weights)
    wy = node_y(lanes, node_weights)
    mx = node_x(lanes, copies)
    my = node_y(lanes, copies)
    inv = node_x(lanes, inverse_mass) * node_y(lanes, inverse_mass)
    first_x, last_x, first_y, last_y = flags(lanes)
    inside = 1.0 - rim_mask(lanes).astype(f32)
    half = iota(128, 1) < 64

    def wall(tile):
        return jnp.broadcast_to(tile[0:1, :], (8, lanes))

    def finish(rows, faces):
        total = sum_lanes(rows, first_y, last_y)
        planes = []
        for z in range(8):
            got = total[z] * (inv * float(1.0 / node_weights[z]))
            if z in (0, 7):
                got = got * (inside * (1.0 - wall(faces[z])))
            planes.append(got)
        return jnp.stack(planes)

    def turn(tile, by):
        by = by % 8
        return pltpu.roll(tile, by, axis=0) if by else tile

    slope = {}
    left = left_ref[0:8]
    right = right_ref[0:8]
    near = finish(left + last_x * pltpu.roll(mid_ref[0, :, 0], 7, axis=1), left)
    slope[-1] = weigh(row_turns(near), dcoef)
    near = finish(right + first_x * pltpu.roll(mid_ref[0, :, 1], 1, axis=1), right)
    slope[2] = weigh(row_turns(near), dcoef)
    for e in range(2):
        faces = mid_ref[0, :, e]
        for face in range(2):
            open_face = inside * (1.0 - wall(faces[7 * face]))
            open_ref[face, e] = own_lanes(open_face[None])[0]
        w = []
        for c in range(3):
            if c == 0:
                before, after = left, right
            else:
                before = jnp.stack([turn(left_ref[7 + c], 7 - z) for z in range(8)])
                after = jnp.stack([turn(right_ref[7 + c], 8 - z) for z in range(8)])
            if e == 0:
                rows = sum_rows(before, mid_ref[c, :, 0], mid_ref[c, :, 1], first_x, last_x)
            else:
                rows = sum_rows(mid_ref[c, :, 0], mid_ref[c, :, 1], after, first_x, last_x)
            got = finish(rows, faces)
            w.append(got)
            w_ref[c, :, e] = own_lanes(got)
        slope[e] = weigh(row_turns(w[0]), dcoef)
        along = sum_lanes(lanes_times(w[1], dy_ref[...]) * wy, first_y, last_y) * (mx * wx)
        t_ref[:, e] = along + z_slope(w[2]) * (mx * wx * my * wy)
    for e in range(2):
        faces = mid_ref[0, :, e]
        rows = sum_rows(slope[e - 1], slope[e], slope[e + 1], first_x, last_x)
        total = rows * (wx * my * wy) + t_ref[:, e]
        edges = []
        for z in range(8):
            got = total[z] * float(-node_weights[z])
            if z in (0, 7):
                face = wall(faces[z])
                got = jnp.where(inside > 0.5, got * face, face)
            b_ref[z, e] = got
            pack_ref[z, e] = own_lanes(got[None])[0]
            edges.append(jnp.where(half, got[:, :128], got[:, 128:]))
        for z in range(4):
            pack_ref[8 + z, e] = jnp.where(
                half, pltpu.roll(edges[z], 96, axis=1), pltpu.roll(edges[z + 4], 32, axis=1)
            )


def unpack(ref, z, e):
    lane = iota(128, 1)
    middle = pltpu.roll(ref[z, e], 64, axis=1)
    edge = pltpu.roll(ref[8 + z % 4, e], 32 if z < 4 else 96, axis=1)
    low = jnp.where(lane >= 64, middle, jnp.where(lane >= 32, edge, 0.0))
    high = jnp.where(lane < 64, middle, jnp.where(lane < 96, edge, 0.0))
    return jnp.concatenate([low, high], axis=1)


def fold(value):
    total = value[0]
    for z in range(1, 8):
        total = total + value[z]
    return total


def load_block(read, at, v_ref, p_ref, rim):
    for e in range(2):
        for z in range(8):
            got = read(z, e)
            if z in (0, 7):
                face = jnp.broadcast_to(got[0:1, :], got.shape)
                p_ref[z // 7, at + e] = jnp.where(rim, 0.0, face)
                got = jnp.where(rim, 0.0, got)
            v_ref[0, z, at + e] = got


def krylov_tools(ky_ref, v_ref, k_ref, p_ref):
    lanes = 256
    kcoef = row_coefs(lanes, scaled_stiff)
    wxy = node_x(lanes, node_weights) * node_y(lanes, node_weights)
    first_x, last_x, first_y, last_y = flags(lanes)

    def apply(j, e):
        v = v_ref[j, :, e]
        yk = lanes_times(v, ky_ref[...])
        xk = weigh(row_turns(v), kcoef)
        zk = depth([v[z] for z in range(8)], scaled_stiff, 1)
        for z in range(8):
            k_ref[j, z, e] = (xk[z] + zk[z] + yk[z]) * (wxy * float(node_weights[z] / span))

    def step(j, e):
        rows = sum_rows(
            k_ref[j, :, e - 1], k_ref[j, :, e], k_ref[j, :, e + 1], first_x, last_x
        )
        total = sum_lanes(rows, first_y, last_y)
        for z in range(8):
            image = total[z]
            if z in (0, 7):
                image = image * p_ref[z // 7, e]
            v_ref[j + 1, z, e] = image - 0.5 * v_ref[j, z, e]

    return apply, step


def over(low, high, body):
    count = high - low
    if count <= 4:
        for e in range(low, high):
            body(e)
    else:
        lax.fori_loop(low, high, lambda e, c: (body(e), c)[1], 0, unroll=count // 2)


def sides(low, body):
    for e in (low, low + 1, 8 - low, 9 - low):
        body(e)


def pack_sums(parts, packed):
    lane = iota(256, 1)
    own = (lane >= 64) & (lane < 192)
    share = node_x(256, 1.0 / copies) * node_y(256, 1.0 / copies)
    lane = iota(128, 1)
    for k, part in parts.items():
        part = jnp.where(own, part, 0.0)
        if k >= 10:
            part = part * share
        part = part[:, :128] + part[:, 128:]
        total = jnp.sum(jnp.sum(part, axis=0, keepdims=True), axis=1, keepdims=True)
        packed = jnp.where(lane == k, total, packed)
    return packed


def own_product(former, latter):
    return fold(former(4) * latter(4)) + fold(former(5) * latter(5))


def inner_kernel(left_ref, mid_ref, right_ref, ky_ref, v_ref, k_ref, p_ref, sum_ref):
    rim = rim_mask(256)
    load_block(lambda z, e: unpack(left_ref, z, e), 2, v_ref, p_ref, rim)
    load_block(lambda z, e: mid_ref[z, e], 4, v_ref, p_ref, rim)
    load_block(lambda z, e: unpack(right_ref, z, e), 6, v_ref, p_ref, rim)
    apply, step = krylov_tools(ky_ref, v_ref, k_ref, p_ref)
    parts = {}
    for j in range(3):
        over(2 + j, 8 - j, lambda e, j=j: apply(j, e))
        for i in range(j + 1):
            parts[j * (j + 1) // 2 + i] = own_product(
                lambda e, i=i: v_ref[i, :, e], lambda e, j=j: k_ref[j, :, e]
            )
        parts[10 + j] = own_product(lambda e, j=j: v_ref[j, :, e], lambda e: v_ref[0, :, e])
        if j < 2:
            over(3 + j, 7 - j, lambda e, j=j: step(j, e))
    sum_ref[...] = pack_sums(parts, jnp.zeros((8, 128), f32))


def outer_kernel(
    left_ref, right_ref, sum_ref, ky_ref, v_in, k_in, p_in, v_ref, k_ref, p_ref, m_out
):
    rim = rim_mask(256)
    load_block(lambda z, e: unpack(left_ref, z, e), 0, v_ref, p_ref, rim)
    load_block(lambda z, e: unpack(right_ref, z, e), 8, v_ref, p_ref, rim)
    apply, step = krylov_tools(ky_ref, v_ref, k_ref, p_ref)
    for j in range(3):
        sides(j, lambda e, j=j: apply(j, e))
        if j < 2:
            sides(j + 1, lambda e, j=j: step(j, e))
        else:
            over(3, 7, lambda e: step(2, e))
    over(4, 6, lambda e: apply(3, e))
    parts = {}
    for i in range(ROUNDS):
        parts[6 + i] = own_product(lambda e, i=i: v_ref[i, :, e], lambda e: k_ref[3, :, e])
    parts[13] = own_product(lambda e: v_ref[3, :, e], lambda e: v_ref[0, :, e])
    packed = pack_sums(parts, sum_ref[...])
    for k in range(m_out.shape[0] // 8):
        m_out[8 * k : 8 * k + 8] = packed


def final_kernel(m_ref, v_ref, w_ref, open_ref, dy_ref, out_ref, q_ref):
    lanes = 256
    parts = [m_ref[8 * k : 8 * k + 8] for k in range(m_ref.shape[0] // 8)]
    while len(parts) > 1:
        odd = parts[len(parts) // 2 * 2 :]
        parts = [parts[k] + parts[k + 1] for k in range(0, len(parts) - 1, 2)] + odd
    sums = jnp.broadcast_to(jnp.sum(parts[0], axis=0, keepdims=True), (8, 128))
    lane = iota(128, 1)

    def moment(k):
        return jnp.sum(jnp.where(lane == k, sums, 0.0), axis=1, keepdims=True)

    e = {}
    slot = 0
    for j in range(ROUNDS):
        for i in range(j + 1):
            e[j, i] = moment(slot)
            slot += 1
    g = [moment(10 + j) for j in range(ROUNDS)]
    low, diag, scaled = {}, [], {}
    for j in range(ROUNDS):
        d = e[j, j]
        for k in range(j):
            d = d - low[j, k] * scaled[j, k]
        diag.append(d)
        for i in range(j + 1, ROUNDS):
            t = e[i, j]
            for k in range(j):
                t = t - scaled[i, k] * low[j, k]
            scaled[i, j] = t
            low[i, j] = t / d
    y = []
    for j in range(ROUNDS):
        t = g[j]
        for k in range(j):
            t = t - low[j, k] * y[k]
        y.append(t)
    c = [None] * ROUNDS
    for j in reversed(range(ROUNDS)):
        t = y[j] / diag[j]
        for k in range(j + 1, ROUNDS):
            t = t - low[k, j] * c[k]
        c[j] = t
    coef = [jnp.broadcast_to(t * (1.0 / span), (8, lanes)) for t in c]

    dcoef = row_coefs(lanes, deriv)
    first_x, last_x, first_y, last_y = flags(lanes)
    mean_x = node_x(lanes, 1.0 / copies)
    mean_y = node_y(lanes, 1.0 / copies)
    q, slope = [], []
    for e in range(4):
        got = v_ref[0, :, 3 + e] * coef[0]
        for j in range(1, ROUNDS):
            got = got + v_ref[j, :, 3 + e] * coef[j]
        q.append(got)
        slope.append(weigh(row_turns(got), dcoef))
    for e in range(2):
        here = q[e + 1]
        q_own = own_lanes(here)
        q_ref[:, e] = q_own
        along_x = sum_rows(slope[e], slope[e + 1], slope[e + 2], first_x, last_x) * mean_x
        along_y = sum_lanes(lanes_times(here, dy_ref[...]), first_y, last_y) * mean_y
        parts = [own_lanes(along_x), own_lanes(along_y), z_slope(q_own)]
        for i in range(3):
            for z in range(8):
                got = w_ref[i, z, e] - parts[i][z]
                if z in (0, 7):
                    got = got * open_ref[z // 7, e]
                out_ref[i, z, e] = got


def shape(*dims):
    return jax.ShapeDtypeStruct(dims, f32)


def call(kernel, out_shape, scratch, *args, space=pltpu.VMEM, vmem=48, cost=None, aliases={}):
    return pl.pallas_call(
        kernel,
        out_shape=out_shape,
        in_specs=[pl.BlockSpec(memory_space=space)] * len(args),
        out_specs=jax.tree.map(lambda s: pl.BlockSpec(memory_space=pltpu.VMEM), out_shape),
        scratch_shapes=scratch,
        cost_estimate=cost,
        input_output_aliases=aliases,
        compiler_params=pltpu.CompilerParams(vmem_limit_bytes=int(vmem * 2**20)),
    )(*args)


def shift(value, axis, by):
    size = lax.axis_size(axis)
    return lax.ppermute(value, axis, [(i, (i + by) % size) for i in range(size)])


def total_rows(packed):
    nx, ny = lax.axis_size("gx"), lax.axis_size("gy")
    planes = [[(2 * z + c) * ny + y for y in range(ny) for c in range(2)] for z in range(nx // 2)]
    part = lax.all_to_all(packed, ("gx", "gy"), 0, 0, axis_index_groups=planes, tiled=True)
    part = jnp.broadcast_to(jnp.sum(part, axis=0, keepdims=True), (nx // 2, 128))
    along = [[2 * z + c for z in range(nx // 2)] for c in range(2)]
    return lax.all_to_all(part, "gx", 0, 0, axis_index_groups=along, tiled=True)


def local(adjoint, checkpoints, wall_faces):
    adj = adjoint.reshape(3, 8, 2, 8, 128)
    flow = checkpoints.reshape(3, 8, 16, 128)
    vm = pltpu.VMEM
    table = jax.ShapeDtypeStruct((256, 256), bf16)
    strip = shape(8, 2, 8, 128)
    rhs, up, down = call(
        rhs_kernel,
        (shape(3, 8, 2, 8, 128), strip, strip),
        [
            vm((3, 8, 2, 8, 128), f32),
            vm((3, 8, 16, 128), bf16),
            vm((2, 2, 16), jnp.int32),
            vm((3, 8, 2, 8, 128), f32),
            vm((2, 2, 8, 128), f32),
            vm((256, 256), bf16),
            vm((256, 256), bf16),
            pltpu.SemaphoreType.DMA((3,)),
        ],
        adj, flow, wall_faces,
        space=pl.ANY,
        vmem=62,
    )
    left = shift(up, "gy", 1)
    right = shift(down, "gy", -1)
    packet = shape(10, 8, 256)
    cost = pl.CostEstimate(flops=10**6, bytes_accessed=4 * 10**5, transcendentals=0)
    turned, dy, ky = call(
        hold_kernel, (shape(3, 8, 2, 8, 128), table, table), [], rhs, cost=cost
    )
    wide, up, down = call(
        join_kernel, (shape(3, 8, 2, 8, 256), packet, packet), [], turned, left, right
    )
    before = shift(up, "gx", 1)
    after = shift(down, "gx", -1)
    source, pack, moved, opened = call(
        source_kernel,
        (shape(8, 2, 8, 256), shape(12, 2, 8, 128), shape(3, 8, 2, 8, 128), shape(2, 2, 8, 128)),
        [vm((8, 2, 8, 256), f32)],
        before, wide, after, dy,
    )
    left = shift(pack, "gx", 1)
    right = shift(pack, "gx", -1)
    right, left = lax.optimization_barrier((right, left))
    left2 = shift(left, "gx", 1)
    right2 = shift(right, "gx", -1)
    cost = pl.CostEstimate(flops=5 * 10**6, bytes_accessed=4 * 10**6, transcendentals=0)
    state = (shape(4, 8, 10, 8, 256), shape(4, 8, 10, 8, 256), shape(2, 10, 8, 256))
    basis, images, faces, known = call(
        inner_kernel, state + (shape(8, 128),), [], left, source, right, ky, cost=cost
    )
    basis, images, faces, packed = call(
        outer_kernel,
        state + (shape(2 * lax.axis_size("gy"), 128),),
        [],
        left2, right2, known, ky, basis, images, faces,
        aliases={4: 0, 5: 1, 6: 2},
    )
    velocity, pressure = call(
        final_kernel,
        (shape(3, 8, 2, 8, 128), shape(8, 2, 8, 128)),
        [],
        total_rows(packed), basis, moved, opened, dy,
    )
    return velocity.reshape(3, 8, 16, 128), pressure.reshape(8, 16, 128)


def solution(mesh):
    return jax.shard_map(
        local,
        mesh=mesh,
        in_specs=(P(None, None, "gx", "gy"), P(None, None, None, "gx", "gy"), P(None, "gx", "gy")),
        out_specs=(P(None, None, "gx", "gy"), P(None, "gx", "gy")),
        check_vma=False,
    )
```

```python
import jax
import jax.numpy as jnp
import numpy as np
from jax import lax
from jax.experimental import pallas as pl
from jax.experimental.pallas import tpu as pltpu
from jax.sharding import PartitionSpec as P

f32 = jnp.float32
bf16 = jnp.bfloat16

node_points = np.array(
    [
        -1.0,
        -0.8717401485096066,
        -0.5917001814331423,
        -0.2092992179024789,
        0.2092992179024789,
        0.5917001814331423,
        0.8717401485096066,
        1.0,
    ]
)
node_weights = np.array(
    [
        0.03571428571428571,
        0.2107042271435061,
        0.3411226924835044,
        0.4124587946587038,
        0.4124587946587038,
        0.3411226924835044,
        0.2107042271435061,
        0.03571428571428571,
    ]
)
time_step = 0.05
viscosity = 0.02
span = 8.0
ROUNDS = 4


def derivative_table(points):
    identity = np.eye(points.shape[0])
    spacing = points[:, None] - points[None, :] + identity
    barycentric = 1.0 / np.prod(spacing, axis=1)
    matrix = barycentric[None, :] / barycentric[:, None] / spacing
    matrix = matrix * (1.0 - identity)
    return matrix - identity * np.sum(matrix, axis=1)[:, None]


deriv = derivative_table(node_points)
stiff = deriv.T @ np.diag(node_weights) @ deriv
copies = np.array([2.0, 1, 1, 1, 1, 1, 1, 2.0])
inverse_mass = 1.0 / (copies * node_weights)


scaled_stiff = stiff / node_weights[:, None]


def iota(lanes, dim):
    return lax.broadcasted_iota(jnp.int32, (8, lanes), dim)


def pick(place, values):
    out = jnp.full(place.shape, float(values[0]), f32)
    for k in range(1, 8):
        out = jnp.where(place == k, float(values[k]), out)
    return out


def node_x(lanes, values):
    return pick(iota(lanes, 0), values)


def node_y(lanes, values):
    return pick(iota(lanes, 1) & 7, values)


def rim_mask(lanes):
    a = iota(lanes, 0)
    b = iota(lanes, 1) & 7
    return (a == 0) | (a == 7) | (b == 0) | (b == 7)


def row_coefs(lanes, matrix):
    return [node_x(lanes, [matrix[a, (a - r) % 8] for a in range(8)]) for r in range(8)]


def row_turns(value):
    return [value] + [pltpu.roll(value, r, axis=1) for r in range(1, 8)]


def weigh(turns, coefs):
    out = turns[0] * coefs[0]
    for r in range(1, 8):
        out = out + turns[r] * coefs[r]
    return out


def depth(planes, matrix, sign):
    plus = [planes[k] + planes[7 - k] for k in range(4)]
    minus = [planes[k] - planes[7 - k] for k in range(4)]
    out = [None] * 8
    for a in range(4):
        even = plus[0] * float(0.5 * (matrix[a, 0] + matrix[a, 7]))
        odd = minus[0] * float(0.5 * (matrix[a, 0] - matrix[a, 7]))
        for k in range(1, 4):
            even = even + plus[k] * float(0.5 * (matrix[a, k] + matrix[a, 7 - k]))
            odd = odd + minus[k] * float(0.5 * (matrix[a, k] - matrix[a, 7 - k]))
        out[a] = even + odd
        out[7 - a] = even - odd if sign > 0 else odd - even
    return out


def z_slope(value):
    return jnp.stack(depth([value[z] for z in range(8)], deriv, -1))


def lane_table(matrix):
    lane = iota(128, 1)
    pattern = jnp.zeros((8, 128), f32)
    for b in range(8):
        pattern = jnp.where((lane & 7) == b, node_x(128, matrix[b]), pattern)
    full = jnp.concatenate([jnp.where(lane // 8 == k, pattern, 0.0) for k in range(16)], axis=0)
    high = full.astype(bf16)
    low = (full - high.astype(f32)).astype(bf16)
    pair = jnp.concatenate([high, low], axis=1)
    return jnp.concatenate([pair, pair], axis=0)


def lanes_times(value, table):
    n, _, lanes = value.shape
    blocks = [value[:, :, k * 128 : (k + 1) * 128].reshape(n * 8, 128) for k in range(lanes // 128)]
    rows = blocks[0] if len(blocks) == 1 else jnp.concatenate(blocks, axis=0)
    high = rows.astype(bf16)
    low = (rows - high.astype(f32)).astype(bf16)
    both = jnp.concatenate([high, low], axis=1)
    got = jnp.dot(both, table, preferred_element_type=f32)
    got = got[:, :128] + got[:, 128:]
    parts = [got[k * n * 8 : (k + 1) * n * 8].reshape(n, 8, 128) for k in range(lanes // 128)]
    return parts[0] if len(parts) == 1 else jnp.concatenate(parts, axis=2)


def sum_lanes(value, first, last):
    lanes = value.shape[2]
    return (
        value
        + last * pltpu.roll(value, lanes - 1, axis=2)
        + first * pltpu.roll(value, 1, axis=2)
    )


def sum_rows(before, here, after, first, last):
    return here + last * pltpu.roll(after, 7, axis=1) + first * pltpu.roll(before, 1, axis=1)


def own_lanes(value):
    n = value.shape[0]
    lane = lax.broadcasted_iota(jnp.int32, (n, 8, 128), 2)
    mixed = jnp.where(lane >= 64, value[:, :, :128], value[:, :, 128:])
    return pltpu.roll(mixed, 64, axis=2)


def expand_walls(faces_ref):
    spread = (
        lax.broadcasted_iota(jnp.int32, (16, 128), 1) // 8
        == lax.broadcasted_iota(jnp.int32, (16, 128), 0)
    ).astype(f32)
    out = []
    for face in range(2):
        rows = faces_ref[face].astype(f32)
        wide = jnp.dot(rows, spread, preferred_element_type=f32)
        out.append(wide)
    return out


def rhs_kernel(
    adj_hbm, flow_hbm, faces_hbm,
    r_ref, up_ref, down_ref,
    adj_ref, flow_ref, faces_ref, u_ref, wall_ref, dy_ref, ky_ref, sems,
):
    moves = [
        pltpu.make_async_copy(src, dst, sems.at[k])
        for k, (src, dst) in enumerate(
            ((adj_hbm, adj_ref), (flow_hbm, flow_ref), (faces_hbm, faces_ref))
        )
    ]
    for move in moves:
        move.start()
    lanes = 128
    dy_ref[...] = lane_table(deriv)
    ky_ref[...] = lane_table(scaled_stiff)
    dcoef = row_coefs(lanes, deriv)
    kcoef = row_coefs(lanes, scaled_stiff)
    wxy = node_x(lanes, node_weights) * node_y(lanes, node_weights)
    rim = rim_mask(lanes)
    lane = iota(lanes, 1)
    for move in moves:
        move.wait()
    for face, wide in enumerate(expand_walls(faces_ref)):
        for e in range(2):
            wall_ref[face, e] = jnp.broadcast_to(wide[e : e + 1], (8, lanes))
    for c in range(3):
        for z in range(8):
            rows = flow_ref[c, z].astype(f32)
            u_ref[c, z, 0] = rows[:8]
            u_ref[c, z, 1] = rows[8:]

    def body(e, carry):
        v = [adj_ref[c, :, e] for c in range(3)]
        u = [u_ref[c, :, e] for c in range(3)]
        vall = jnp.concatenate(v, axis=0)
        uall = jnp.concatenate(u, axis=0)
        vdy = lanes_times(vall, dy_ref[...])
        vky = lanes_times(vall, ky_ref[...])
        udy = lanes_times(uall, dy_ref[...])
        stretch = [jnp.zeros((8, 8, lanes), f32)] * 3
        for j in range(3):
            stretch[0] = stretch[0] + v[j] * weigh(row_turns(u[j]), dcoef)
            stretch[1] = stretch[1] + v[j] * udy[8 * j : 8 * j + 8]
            stretch[2] = stretch[2] + v[j] * z_slope(u[j])
        ups, downs = [None] * 8, [None] * 8
        for i in range(3):
            turns = row_turns(v[i])
            planes = [v[i][z] for z in range(8)]
            zd = depth(planes, deriv, -1)
            zk = depth(planes, scaled_stiff, 1)
            xd = weigh(turns, dcoef)
            xk = weigh(turns, kcoef)
            made = []
            for z in range(8):
                wz = float(node_weights[z])
                adv = (
                    u[0][z] * xd[z]
                    + u[1][z] * vdy[8 * i + z]
                    + u[2][z] * zd[z]
                    - stretch[i][z]
                )
                bend = xk[z] + vky[8 * i + z] + zk[z]
                out = (wxy * wz) * (v[i][z] + time_step * adv - (time_step * viscosity) * bend)
                if i == 0 and z in (0, 7):
                    out = jnp.where(rim, wall_ref[z // 7, e], out)
                r_ref[i, z, e] = out
                made.append(out)
            for z in range(8):
                up, down = made[z], made[z]
                if 0 < z < 7:
                    up = up + jnp.where(lane == 88, pltpu.roll(up, 1, axis=1), 0.0)
                    down = down + jnp.where(lane == 39, pltpu.roll(down, 127, axis=1), 0.0)
                up = pltpu.roll(up, (40 * i - 88) % 128, axis=1)
                down = pltpu.roll(down, 40 * i, axis=1) if i else down
                here = (lane >= 40 * i) & (lane < 40 * i + 40)
                ups[z] = up if i == 0 else jnp.where(here, up, ups[z])
                downs[z] = down if i == 0 else jnp.where(here, down, downs[z])
        for z in range(8):
            up_ref[z, e] = ups[z]
            down_ref[z, e] = downs[z]
        return carry

    lax.fori_loop(0, 2, body, 0, unroll=2)


def hold_kernel(r_ref, turned_ref, dy_ref, ky_ref):
    dy_ref[...] = lane_table(deriv)
    ky_ref[...] = lane_table(scaled_stiff)
    for c in range(3):
        for z in range(8):
            for e in range(2):
                turned_ref[c, z, e] = pltpu.roll(r_ref[c, z, e], 64, axis=1)


def join_kernel(r_ref, left_ref, right_ref, e_ref, up_ref, down_ref):
    lane = iota(128, 1)
    half = lane < 64
    place = iota(256, 0)
    first = place == 0
    last = place == 7
    for c in range(3):
        faces_up = jnp.zeros((8, 256), f32)
        faces_down = jnp.zeros((8, 256), f32)
        for z in range(8):
            tiles = []
            for e in range(2):
                turned = r_ref[c, z, e]
                left = pltpu.roll(left_ref[z, e], (24 - 40 * c) % 128, axis=1)
                right = pltpu.roll(right_ref[z, e], (64 - 40 * c) % 128, axis=1)
                tile = jnp.concatenate(
                    [
                        jnp.where(half, jnp.where(lane >= 24, left, 0.0), turned),
                        jnp.where(half, turned, jnp.where(lane < 104, right, 0.0)),
                    ],
                    axis=1,
                )
                e_ref[c, z, e] = tile
                tiles.append(tile)
            if c == 0:
                go_up, go_down = tiles[1], tiles[0]
                if 0 < z < 7:
                    go_up = go_up + jnp.where(first, pltpu.roll(tiles[0], 1, axis=0), 0.0)
                    go_down = go_down + jnp.where(last, pltpu.roll(tiles[1], 7, axis=0), 0.0)
                up_ref[z] = go_up
                down_ref[z] = go_down
            else:
                turned = pltpu.roll(tiles[1], (z + 1) % 8, axis=0) if z < 7 else tiles[1]
                faces_up = jnp.where(place == z, turned, faces_up)
                turned = pltpu.roll(tiles[0], z, axis=0) if z else tiles[0]
                faces_down = jnp.where(place == z, turned, faces_down)
        if c:
            up_ref[7 + c] = faces_up
            down_ref[7 + c] = faces_down


def flags(lanes):
    first_x = (iota(lanes, 0) == 0).astype(f32)
    last_x = (iota(lanes, 0) == 7).astype(f32)
    first_y = ((iota(lanes, 1) & 7) == 0).astype(f32)
    last_y = ((iota(lanes, 1) & 7) == 7).astype(f32)
    return first_x, last_x, first_y, last_y


def source_kernel(left_ref, mid_ref, right_ref, dy_ref, b_ref, pack_ref, w_ref, open_ref, t_ref):
    lanes = 256
    dcoef = row_coefs(lanes, deriv)
    wx = node_x(lanes, node_weights)
    wy = node_y(lanes, node_weights)
    mx = node_x(lanes, copies)
    my = node_y(lanes, copies)
    inv = node_x(lanes, inverse_mass) * node_y(lanes, inverse_mass)
    first_x, last_x, first_y, last_y = flags(lanes)
    inside = 1.0 - rim_mask(lanes).astype(f32)
    half = iota(128, 1) < 64

    def wall(tile):
        return jnp.broadcast_to(tile[0:1, :], (8, lanes))

    def finish(rows, faces):
        total = sum_lanes(rows, first_y, last_y)
        planes = []
        for z in range(8):
            got = total[z] * (inv * float(1.0 / node_weights[z]))
            if z in (0, 7):
                got = got * (inside * (1.0 - wall(faces[z])))
            planes.append(got)
        return jnp.stack(planes)

    def turn(tile, by):
        by = by % 8
        return pltpu.roll(tile, by, axis=0) if by else tile

    slope = {}
    left = left_ref[0:8]
    right = right_ref[0:8]
    near = finish(left + last_x * pltpu.roll(mid_ref[0, :, 0], 7, axis=1), left)
    slope[-1] = weigh(row_turns(near), dcoef)
    near = finish(right + first_x * pltpu.roll(mid_ref[0, :, 1], 1, axis=1), right)
    slope[2] = weigh(row_turns(near), dcoef)
    for e in range(2):
        faces = mid_ref[0, :, e]
        for face in range(2):
            open_face = inside * (1.0 - wall(faces[7 * face]))
            open_ref[face, e] = own_lanes(open_face[None])[0]
        w = []
        for c in range(3):
            if c == 0:
                before, after = left, right
            else:
                before = jnp.stack([turn(left_ref[7 + c], 7 - z) for z in range(8)])
                after = jnp.stack([turn(right_ref[7 + c], 8 - z) for z in range(8)])
            if e == 0:
                rows = sum_rows(before, mid_ref[c, :, 0], mid_ref[c, :, 1], first_x, last_x)
            else:
                rows = sum_rows(mid_ref[c, :, 0], mid_ref[c, :, 1], after, first_x, last_x)
            got = finish(rows, faces)
            w.append(got)
            w_ref[c, :, e] = own_lanes(got)
        slope[e] = weigh(row_turns(w[0]), dcoef)
        along = sum_lanes(lanes_times(w[1], dy_ref[...]) * wy, first_y, last_y) * (mx * wx)
        t_ref[:, e] = along + z_slope(w[2]) * (mx * wx * my * wy)
    for e in range(2):
        faces = mid_ref[0, :, e]
        rows = sum_rows(slope[e - 1], slope[e], slope[e + 1], first_x, last_x)
        total = rows * (wx * my * wy) + t_ref[:, e]
        edges = []
        for z in range(8):
            got = total[z] * float(-node_weights[z])
            if z in (0, 7):
                face = wall(faces[z])
                got = jnp.where(inside > 0.5, got * face, face)
            b_ref[z, e] = got
            pack_ref[z, e] = own_lanes(got[None])[0]
            edges.append(jnp.where(half, got[:, :128], got[:, 128:]))
        for z in range(4):
            pack_ref[8 + z, e] = jnp.where(
                half, pltpu.roll(edges[z], 96, axis=1), pltpu.roll(edges[z + 4], 32, axis=1)
            )


def unpack(ref, z, e):
    lane = iota(128, 1)
    middle = pltpu.roll(ref[z, e], 64, axis=1)
    edge = pltpu.roll(ref[8 + z % 4, e], 32 if z < 4 else 96, axis=1)
    low = jnp.where(lane >= 64, middle, jnp.where(lane >= 32, edge, 0.0))
    high = jnp.where(lane < 64, middle, jnp.where(lane < 96, edge, 0.0))
    return jnp.concatenate([low, high], axis=1)


def fold(value):
    total = value[0]
    for z in range(1, 8):
        total = total + value[z]
    return total


def load_block(read, at, v_ref, p_ref, rim):
    for e in range(2):
        for z in range(8):
            got = read(z, e)
            if z in (0, 7):
                face = jnp.broadcast_to(got[0:1, :], got.shape)
                p_ref[z // 7, at + e] = jnp.where(rim, 0.0, face)
                got = jnp.where(rim, 0.0, got)
            v_ref[0, z, at + e] = got


def krylov_tools(ky_ref, v_ref, k_ref, p_ref):
    lanes = 256
    kcoef = row_coefs(lanes, scaled_stiff)
    wxy = node_x(lanes, node_weights) * node_y(lanes, node_weights)
    first_x, last_x, first_y, last_y = flags(lanes)

    def apply(j, e):
        v = v_ref[j, :, e]
        yk = lanes_times(v, ky_ref[...])
        xk = weigh(row_turns(v), kcoef)
        zk = depth([v[z] for z in range(8)], scaled_stiff, 1)
        for z in range(8):
            k_ref[j, z, e] = (xk[z] + zk[z] + yk[z]) * (wxy * float(node_weights[z] / span))

    def step(j, e):
        rows = sum_rows(
            k_ref[j, :, e - 1], k_ref[j, :, e], k_ref[j, :, e + 1], first_x, last_x
        )
        total = sum_lanes(rows, first_y, last_y)
        for z in range(8):
            image = total[z]
            if z in (0, 7):
                image = image * p_ref[z // 7, e]
            v_ref[j + 1, z, e] = image - 0.5 * v_ref[j, z, e]

    return apply, step


def over(low, high, body):
    count = high - low
    lax.fori_loop(
        low, high, lambda e, c: (body(e), c)[1], 0, unroll=count if count <= 4 else count // 2
    )


def sides(low, body):
    over(0, 4, lambda t: body(low + t + (t // 2) * (6 - 2 * low)))


def pack_sums(parts, packed):
    lane = iota(256, 1)
    own = (lane >= 64) & (lane < 192)
    share = node_x(256, 1.0 / copies) * node_y(256, 1.0 / copies)
    lane = iota(128, 1)
    for k, part in parts.items():
        part = jnp.where(own, part, 0.0)
        if k >= 10:
            part = part * share
        part = part[:, :128] + part[:, 128:]
        total = jnp.sum(jnp.sum(part, axis=0, keepdims=True), axis=1, keepdims=True)
        packed = jnp.where(lane == k, total, packed)
    return packed


def own_product(former, latter):
    return fold(former(4) * latter(4)) + fold(former(5) * latter(5))


def inner_kernel(left_ref, mid_ref, right_ref, ky_ref, v_ref, k_ref, p_ref, sum_ref):
    rim = rim_mask(256)
    load_block(lambda z, e: unpack(left_ref, z, e), 2, v_ref, p_ref, rim)
    load_block(lambda z, e: mid_ref[z, e], 4, v_ref, p_ref, rim)
    load_block(lambda z, e: unpack(right_ref, z, e), 6, v_ref, p_ref, rim)
    apply, step = krylov_tools(ky_ref, v_ref, k_ref, p_ref)
    parts = {}
    for j in range(3):
        over(2 + j, 8 - j, lambda e, j=j: apply(j, e))
        for i in range(j + 1):
            parts[j * (j + 1) // 2 + i] = own_product(
                lambda e, i=i: v_ref[i, :, e], lambda e, j=j: k_ref[j, :, e]
            )
        parts[10 + j] = own_product(lambda e, j=j: v_ref[j, :, e], lambda e: v_ref[0, :, e])
        if j < 2:
            over(3 + j, 7 - j, lambda e, j=j: step(j, e))
    sum_ref[...] = pack_sums(parts, jnp.zeros((8, 128), f32))


def outer_kernel(
    left_ref, right_ref, sum_ref, ky_ref, v_in, k_in, p_in, v_ref, k_ref, p_ref, m_out
):
    rim = rim_mask(256)
    load_block(lambda z, e: unpack(left_ref, z, e), 0, v_ref, p_ref, rim)
    load_block(lambda z, e: unpack(right_ref, z, e), 8, v_ref, p_ref, rim)
    apply, step = krylov_tools(ky_ref, v_ref, k_ref, p_ref)
    for j in range(3):
        sides(j, lambda e, j=j: apply(j, e))
        if j < 2:
            sides(j + 1, lambda e, j=j: step(j, e))
        else:
            over(3, 7, lambda e: step(2, e))
    over(4, 6, lambda e: apply(3, e))
    parts = {}
    for i in range(ROUNDS):
        parts[6 + i] = own_product(lambda e, i=i: v_ref[i, :, e], lambda e: k_ref[3, :, e])
    parts[13] = own_product(lambda e: v_ref[3, :, e], lambda e: v_ref[0, :, e])
    packed = pack_sums(parts, sum_ref[...])
    for k in range(m_out.shape[0] // 8):
        m_out[8 * k : 8 * k + 8] = packed


def final_kernel(m_ref, v_ref, w_ref, open_ref, dy_ref, out_ref, q_ref):
    lanes = 256
    parts = [m_ref[8 * k : 8 * k + 8] for k in range(m_ref.shape[0] // 8)]
    while len(parts) > 1:
        odd = parts[len(parts) // 2 * 2 :]
        parts = [parts[k] + parts[k + 1] for k in range(0, len(parts) - 1, 2)] + odd
    sums = jnp.broadcast_to(jnp.sum(parts[0], axis=0, keepdims=True), (8, 128))
    lane = iota(128, 1)

    def moment(k):
        return jnp.sum(jnp.where(lane == k, sums, 0.0), axis=1, keepdims=True)

    e = {}
    slot = 0
    for j in range(ROUNDS):
        for i in range(j + 1):
            e[j, i] = moment(slot)
            slot += 1
    g = [moment(10 + j) for j in range(ROUNDS)]
    low, diag, scaled = {}, [], {}
    for j in range(ROUNDS):
        d = e[j, j]
        for k in range(j):
            d = d - low[j, k] * scaled[j, k]
        diag.append(d)
        for i in range(j + 1, ROUNDS):
            t = e[i, j]
            for k in range(j):
                t = t - scaled[i, k] * low[j, k]
            scaled[i, j] = t
            low[i, j] = t / d
    y = []
    for j in range(ROUNDS):
        t = g[j]
        for k in range(j):
            t = t - low[j, k] * y[k]
        y.append(t)
    c = [None] * ROUNDS
    for j in reversed(range(ROUNDS)):
        t = y[j] / diag[j]
        for k in range(j + 1, ROUNDS):
            t = t - low[k, j] * c[k]
        c[j] = t
    coef = [jnp.broadcast_to(t * (1.0 / span), (8, lanes)) for t in c]

    dcoef = row_coefs(lanes, deriv)
    first_x, last_x, first_y, last_y = flags(lanes)
    mean_x = node_x(lanes, 1.0 / copies)
    mean_y = node_y(lanes, 1.0 / copies)
    q, slope = [], []
    for e in range(4):
        got = v_ref[0, :, 3 + e] * coef[0]
        for j in range(1, ROUNDS):
            got = got + v_ref[j, :, 3 + e] * coef[j]
        q.append(got)
        slope.append(weigh(row_turns(got), dcoef))
    for e in range(2):
        here = q[e + 1]
        q_own = own_lanes(here)
        q_ref[:, e] = q_own
        along_x = sum_rows(slope[e], slope[e + 1], slope[e + 2], first_x, last_x) * mean_x
        along_y = sum_lanes(lanes_times(here, dy_ref[...]), first_y, last_y) * mean_y
        parts = [own_lanes(along_x), own_lanes(along_y), z_slope(q_own)]
        for i in range(3):
            for z in range(8):
                got = w_ref[i, z, e] - parts[i][z]
                if z in (0, 7):
                    got = got * open_ref[z // 7, e]
                out_ref[i, z, e] = got


def shape(*dims):
    return jax.ShapeDtypeStruct(dims, f32)


def call(kernel, out_shape, scratch, *args, space=pltpu.VMEM, vmem=48, cost=None, aliases={}):
    return pl.pallas_call(
        kernel,
        out_shape=out_shape,
        in_specs=[pl.BlockSpec(memory_space=space)] * len(args),
        out_specs=jax.tree.map(lambda s: pl.BlockSpec(memory_space=pltpu.VMEM), out_shape),
        scratch_shapes=scratch,
        cost_estimate=cost,
        input_output_aliases=aliases,
        compiler_params=pltpu.CompilerParams(vmem_limit_bytes=int(vmem * 2**20)),
    )(*args)


def shift(value, axis, by):
    size = lax.axis_size(axis)
    return lax.ppermute(value, axis, [(i, (i + by) % size) for i in range(size)])


def total_rows(packed):
    nx, ny = lax.axis_size("gx"), lax.axis_size("gy")
    pairs = [[i, i + 1] for i in range(0, nx, 2)]
    part = lax.all_gather(packed, "gx", axis_index_groups=pairs)
    part = jnp.broadcast_to(part[0, :1] + part[1, :1], (ny, 128))
    part = lax.all_to_all(part, "gy", 0, 0, tiled=True)
    part = jnp.broadcast_to(jnp.sum(part, axis=0, keepdims=True), (nx // 2, 128))
    along = [[2 * z + c for z in range(nx // 2)] for c in range(2)]
    return lax.all_to_all(part, "gx", 0, 0, axis_index_groups=along, tiled=True)


def local(adjoint, checkpoints, wall_faces):
    adj = adjoint.reshape(3, 8, 2, 8, 128)
    flow = checkpoints.reshape(3, 8, 16, 128)
    vm = pltpu.VMEM
    table = jax.ShapeDtypeStruct((256, 256), bf16)
    strip = shape(8, 2, 8, 128)
    rhs, up, down = call(
        rhs_kernel,
        (shape(3, 8, 2, 8, 128), strip, strip),
        [
            vm((3, 8, 2, 8, 128), f32),
            vm((3, 8, 16, 128), bf16),
            vm((2, 2, 16), jnp.int32),
            vm((3, 8, 2, 8, 128), f32),
            vm((2, 2, 8, 128), f32),
            vm((256, 256), bf16),
            vm((256, 256), bf16),
            pltpu.SemaphoreType.DMA((3,)),
        ],
        adj, flow, wall_faces,
        space=pl.ANY,
        vmem=62,
    )
    left = shift(up, "gy", 1)
    right = shift(down, "gy", -1)
    packet = shape(10, 8, 256)
    cost = pl.CostEstimate(flops=10**6, bytes_accessed=4 * 10**5, transcendentals=0)
    turned, dy, ky = call(
        hold_kernel, (shape(3, 8, 2, 8, 128), table, table), [], rhs, cost=cost
    )
    wide, up, down = call(
        join_kernel, (shape(3, 8, 2, 8, 256), packet, packet), [], turned, left, right
    )
    before = shift(up, "gx", 1)
    after = shift(down, "gx", -1)
    source, pack, moved, opened = call(
        source_kernel,
        (shape(8, 2, 8, 256), shape(12, 2, 8, 128), shape(3, 8, 2, 8, 128), shape(2, 2, 8, 128)),
        [vm((8, 2, 8, 256), f32)],
        before, wide, after, dy,
    )
    left = shift(pack, "gx", 1)
    right = shift(pack, "gx", -1)
    right, left = lax.optimization_barrier((right, left))
    left2 = shift(left, "gx", 1)
    right2 = shift(right, "gx", -1)
    cost = pl.CostEstimate(flops=5 * 10**6, bytes_accessed=4 * 10**6, transcendentals=0)
    state = (shape(4, 8, 10, 8, 256), shape(4, 8, 10, 8, 256), shape(2, 10, 8, 256))
    basis, images, faces, known = call(
        inner_kernel, state + (shape(8, 128),), [], left, source, right, ky, cost=cost
    )
    basis, images, faces, packed = call(
        outer_kernel,
        state + (shape(8, 128),),
        [],
        left2, right2, known, ky, basis, images, faces,
        aliases={4: 0, 5: 1, 6: 2},
    )
    velocity, pressure = call(
        final_kernel,
        (shape(3, 8, 2, 8, 128), shape(8, 2, 8, 128)),
        [],
        total_rows(packed), basis, moved, opened, dy,
    )
    return velocity.reshape(3, 8, 16, 128), pressure.reshape(8, 16, 128)


def solution(mesh):
    return jax.shard_map(
        local,
        mesh=mesh,
        in_specs=(P(None, None, "gx", "gy"), P(None, None, None, "gx", "gy"), P(None, "gx", "gy")),
        out_specs=(P(None, None, "gx", "gy"), P(None, "gx", "gy")),
        check_vma=False,
    )
```
